32 devices in a mesh: tab: 8 (over z, y), rep: 4 (over x, core).
Axes of the slice: x: 2, y: 2, z: 4, core: 2. Of those that a mesh axis runs over, the one named last changes fastest.
Arguments:
- ids: int32 [16384, 26], P(('tab', 'rep')), may hold values from 0 to 32767
- table_rows: int32 [26], replicated, may hold values from 4096 to 32768, as said below
- table_place: int32 [26], replicated, may hold values from 0 to 39, as said below
- dense_in: bfloat16 [16384, 13], P(('tab', 'rep')), may hold values from -6 to 6
- labels: int32 [16384], P(('tab', 'rep')), may hold values 0 or 1
- tables: bfloat16 [40, 39, 32768], P('tab'), may hold values from -6 to 6
- cross_w: bfloat16 [3, 1027, 1027], replicated, may hold values from -0.1875 to 0.1875
- cross_b: bfloat16 [3, 1027], replicated, may hold values from -3 to 3
- tower1_w: bfloat16 [1024, 1027], replicated, may hold values from -0.1875 to 0.1875
- tower1_b: bfloat16 [1024], replicated, may hold values from -3 to 3
- tower2_w: bfloat16 [1024, 1024], replicated, may hold values from -0.1875 to 0.1875
- tower2_b: bfloat16 [1024], replicated, may hold values from -3 to 3
- out_w: bfloat16 [2051], replicated, may hold values from -0.125 to 0.125
- out_b: bfloat16 [], replicated, may hold values from -2 to 2
Outputs:
- loss: float32 [], replicated
- logits: float32 [16384], P(('tab', 'rep'))
- dense_grad: float32 [16384, 13], P(('tab', 'rep'))
- cross_w_grad: float32 [3, 1027, 1027], replicated
- cross_b_grad: float32 [3, 1027], replicated
- tower1_w_grad: float32 [1024, 1027], replicated
- tower1_b_grad: float32 [1024], replicated
- tower2_w_grad: float32 [1024, 1024], replicated
- tower2_b_grad: float32 [1024], replicated
- out_w_grad: float32 [2051], replicated
- out_b_grad: float32 [], replicated
- table_grad: float32 [40, 39, 32768], P('tab', None, 'rep')
The draws below stay inside these ranges and needn't reach their ends.
Inputs may be any that keep to these rules, and one draw needn't show every extreme that they name: `table_rows`: every table has at least 4096 rows, and one table has exactly 32768. `table_place`: distinct slots; slot s lies on the device of index s // 5 along tab. Some device holds 5 tables.
All inputs are finite; a program needn't handle non-finite values. No bound on the sum of `labels` on one device may be relied on, other than what follows from the above.
Results may differ from the reference program's by a relative error of at most 0.0044.
Values may be sent and summed in bfloat16 or wider, within the bound.
No kernel may reach another device: no remote copies, remote signals or barrier semaphores. Data moves between devices by JAX's collectives and lax.ppermute only.
A program may use at most 1.0625 GiB of HBM per device.

```python
import math
import jax
import jax.numpy as jnp
import numpy as np
from jax import lax

FIELDS = 26
EMBED = 39
DENSE = 13
HIDDEN_SIZE = 1024
LAYERS = 3
ROWS = 32768
SLOTS = 5
SLOTS_ALL = 40
WIDTH = 1027
BATCH = 16384


def draw_table_rows(key, part):
    key = jax.random.fold_in(key, 11)
    key_counts, key_pick = jax.random.split(key)
    counts = jax.random.randint(key_counts, (FIELDS,), ROWS // 8, ROWS + 1)
    chosen = jax.random.randint(key_pick, (), 0, FIELDS)
    return jnp.where(jnp.arange(FIELDS) == chosen, ROWS, counts).astype(jnp.int32)


def draw_table_place(key, part):
    key = jax.random.fold_in(key, 23)
    key_ranks, key_full, key_order = jax.random.split(key, 3)
    slot_ranks = jax.random.permutation(key_ranks, SLOTS_ALL).astype(jnp.int32)
    full_device = jax.random.randint(key_full, (), 0, SLOTS_ALL // SLOTS)
    slot_ids = jnp.arange(SLOTS_ALL, dtype=jnp.int32)
    scores = jnp.where(slot_ids // SLOTS == full_device, slot_ids - SLOTS_ALL, slot_ranks)
    ordering = jnp.argsort(scores, stable=True)
    chosen = ordering[:FIELDS]
    return chosen[jax.random.permutation(key_order, FIELDS)].astype(jnp.int32)


def touch_ends(array, key, low, high):
    shape = array.shape
    spot = [jax.random.randint(jax.random.fold_in(key, axis), (), 0, shape[axis]) for axis in range(len(shape))]
    array = array.at[tuple(spot)].set(low)
    longest = shape.index(max(shape))
    spot[longest] = (spot[longest] + 1) % shape[longest]
    return array.at[tuple(spot)].set(high)


def levels(own_key, shape, cuts, low, top_value):
    gain = 1.0
    for dim, shards_of in cuts:
        steps = jax.random.uniform(jax.random.fold_in(jax.random.fold_in(own_key, 6), dim), (shards_of,), jnp.float32, low / len(cuts), top_value / len(cuts))
        gain = gain * jnp.repeat(jnp.exp(steps), shape[dim] // shards_of).reshape((-1,) + (1,) * (len(shape) - 1 - dim))
    return gain


def rank_table(count, skew):
    loads = [(1 << 20) // math.isqrt(standing ** skew) + 1 for standing in range(1, count + 1)]
    scale = 1 + sum(loads) // (1 << 30)
    return np.cumsum(np.array([max(1, weight // scale) for weight in loads]))


def ranked(stream_key, shape, amount, lean):
    listing = rank_table(amount, lean)
    ticket = jax.random.randint(jax.random.fold_in(stream_key, 1), shape, 0, int(listing[amount - 1]))
    standing = jnp.searchsorted(jnp.asarray(listing, jnp.int32), ticket, side="right")
    return jax.random.permutation(jax.random.fold_in(stream_key, 2), amount)[standing].astype(jnp.int32)


def noise(own_key, extent, width, most, shards=(), held_as=jnp.bfloat16):
    array = width * jax.random.normal(own_key, extent, jnp.float32)
    if shards:
        array = array * levels(own_key, extent, shards, -0.22, 0.18)
    return jnp.clip(array, -most, most).astype(held_as)


def setup_inputs(seed: int = 0) -> dict:
    splits = jax.random.split(jax.random.key(seed), 15)
    ids = touch_ends(ranked(splits[0], (BATCH, FIELDS), ROWS, 2), jax.random.fold_in(splits[0], 3), 0, ROWS - 1).astype(jnp.int32)
    table_rows = draw_table_rows(jax.random.fold_in(splits[14], 71), 0)
    table_place = draw_table_place(jax.random.fold_in(splits[14], 71), 0)
    dense_in = noise(splits[3], (BATCH, DENSE), 1.0, 6.0, ((0, 32),))
    labels = touch_ends((jax.random.randint(splits[4], (BATCH,), 0, 2) < 1).astype(jnp.int32), jax.random.fold_in(splits[4], 1), 0, 1)
    tables = noise(splits[5], (SLOTS_ALL, EMBED, ROWS), 1.0, 6.0, ((0, 8),))
    cross_w = noise(splits[6], (LAYERS, WIDTH, WIDTH), WIDTH ** -0.5, 0.1875)
    cross_b = noise(splits[7], (LAYERS, WIDTH), 0.5, 3.0)
    tower1_w = noise(splits[8], (HIDDEN_SIZE, WIDTH), WIDTH ** -0.5, 0.1875)
    tower1_b = noise(splits[9], (HIDDEN_SIZE,), 0.5, 3.0)
    tower2_w = noise(splits[10], (HIDDEN_SIZE, HIDDEN_SIZE), HIDDEN_SIZE ** -0.5, 0.1875)
    tower2_b = noise(splits[11], (HIDDEN_SIZE,), 0.5, 3.0)
    out_w = noise(splits[12], (WIDTH + HIDDEN_SIZE,), (WIDTH + HIDDEN_SIZE) ** -0.5, 0.125)
    out_b = noise(splits[13], (), 0.5, 2.0)
    return {"ids": ids, "table_rows": table_rows, "table_place": table_place, "dense_in": dense_in, "labels": labels, "tables": tables, "cross_w": cross_w, "cross_b": cross_b, "tower1_w": tower1_w, "tower1_b": tower1_b, "tower2_w": tower2_w, "tower2_b": tower2_b, "out_w": out_w, "out_b": out_b}


@jax.custom_vjp
def low(v):
    return lax.optimization_barrier(v.astype(jnp.bfloat16)).astype(jnp.float32)

@jax.custom_vjp
def low_back(v):
    return v

def low_keep(v):
    return (low(v), None)

def low_pass(kept, grad):
    return (grad,)

def back_keep(v):
    return (v, None)

def back_low(kept, grad):
    return (low(grad),)
low.defvjp(low_keep, low_pass)
low_back.defvjp(back_keep, back_low)
HIGH = lax.Precision.HIGHEST

def matmul(left_op, right_op):
    return jnp.dot(left_op, right_op, precision=HIGH, preferred_element_type=jnp.float32)

def network(params, tables_f, dense_block, id_block, label_block, table_place):
    cross_w, cross_b, tower1_w, tower1_b, tower2_w, tower2_b, out_w, out_b = params
    row_total = id_block.shape[0]
    looked = tables_f[table_place[None, :], :, id_block]
    embedded = low_back(looked.reshape(row_total, FIELDS * EMBED))
    anchor = jnp.concatenate([dense_block, embedded], axis=1)
    current = anchor
    for layer_at in range(LAYERS):
        update = low_back(matmul(low(current), cross_w[layer_at]) + cross_b[layer_at])
        current = anchor * update + current
    first_pre = low_back(matmul(low(anchor), tower1_w.T) + tower1_b)
    first_act = jax.nn.silu(first_pre)
    second_pre = low_back(matmul(low(first_act), tower2_w) + tower2_b)
    second_act = jax.nn.silu(second_pre)
    logits = matmul(current, out_w[:WIDTH]) + matmul(second_act, out_w[WIDTH:]) + out_b
    terms = jax.nn.softplus(logits) - label_block * logits
    return (jnp.sum(terms), logits)

def reference(ids, table_rows, table_place, dense_in, labels, tables, cross_w, cross_b, tower1_w, tower1_b, tower2_w, tower2_b, out_w, out_b):
    params = tuple((weight_item.astype(jnp.float32) for weight_item in (cross_w, cross_b, tower1_w, tower1_b, tower2_w, tower2_b, out_w, out_b)))
    tables_f = tables.astype(jnp.float32)
    effective = (ids % table_rows[None, :]).astype(jnp.int32)
    block_rows = math.gcd(BATCH, 4096)
    block_count = BATCH // block_rows
    id_blocks = effective.reshape(block_count, block_rows, FIELDS)
    dense_blocks = dense_in.astype(jnp.float32).reshape(block_count, block_rows, DENSE)
    label_blocks = labels.astype(jnp.float32).reshape(block_count, block_rows)

    def advance(carry, pieces):
        param_sum, table_sum, loss_sum = carry
        id_block, dense_block, label_block = pieces

        def closed(param_vals, table_vals, dense_vals):
            return network(param_vals, table_vals, dense_vals, id_block, label_block, table_place)
        total_loss, backward, logit_block = jax.vjp(closed, params, tables_f, dense_block, has_aux=True)
        param_grad, table_grad, dense_grad = backward(jnp.ones_like(total_loss))
        param_sum = jax.tree.map(jnp.add, param_sum, param_grad)
        return ((param_sum, table_sum + table_grad, loss_sum + total_loss), (logit_block, dense_grad))
    starting = (jax.tree.map(jnp.zeros_like, params), jnp.zeros_like(tables_f), jnp.zeros((), jnp.float32))
    (param_sum, table_sum, loss_sum), (logit_blocks, dense_grads) = lax.scan(advance, starting, (id_blocks, dense_blocks, label_blocks))
    cross_w_grad, cross_b_grad, tower1_w_grad, tower1_b_grad, tower2_w_grad, tower2_b_grad, out_w_grad, out_b_grad = param_sum
    return (loss_sum / BATCH, logit_blocks.reshape(BATCH), dense_grads.reshape(BATCH, DENSE), cross_w_grad, cross_b_grad, tower1_w_grad, tower1_b_grad, tower2_w_grad, tower2_b_grad, out_w_grad, out_b_grad, table_sum)
```

```python
import functools

import jax
import jax.numpy as jnp
from jax import lax
from jax.experimental import pallas as pl
from jax.experimental.pallas import tpu as pltpu
from jax.sharding import PartitionSpec as P

HIGH = lax.Precision.HIGHEST
BF = jnp.bfloat16
F32 = jnp.float32
LOOK_LOW = 512
LOOK_GROUP = 8
LOOK_COLS = 1024
ADD_LOW = 512
ADD_COLS = 2048


def round_up(size, unit):
    return -(-size // unit) * unit


def lookup_kernel(group_ref, ids_ref, table_ref, out_ref, stack):
    slot = pl.program_id(0)
    embed_dim = table_ref.shape[1]
    block_count, pad_dim, low_count = stack.shape
    cols = out_ref.shape[2]

    @pl.when(pl.program_id(1) == 0)
    def _():
        for block in range(block_count):
            stack[block, :embed_dim, :] = table_ref[0, :, block * low_count : (block + 1) * low_count]

    picked = ids_ref[0]
    high = lax.shift_right_arithmetic(picked, low_count.bit_length() - 1)
    low = picked & (low_count - 1)
    low_iota = lax.broadcasted_iota(jnp.int32, (low_count, cols), 0)
    onehot = jnp.where(low_iota == low, 1.0, 0.0).astype(BF)

    def step(group, total):
        left = stack[pl.ds(group * LOOK_GROUP, LOOK_GROUP)].reshape(LOOK_GROUP * pad_dim, low_count)
        partial = jnp.dot(left, onehot, preferred_element_type=F32)
        for at in range(LOOK_GROUP):
            rows = partial[at * pad_dim : at * pad_dim + total.shape[0]]
            total = total + jnp.where(high == group * LOOK_GROUP + at, rows, 0.0)
        return total

    rows_kept = round_up(embed_dim, 8)
    total = lax.fori_loop(0, group_ref[slot], step, jnp.zeros((rows_kept, cols), F32))
    out_ref[0] = total[:embed_dim].astype(BF)


def lookup(tables, wanted, own_rows):
    slot_count, embed_dim, table_len = tables.shape
    count = wanted.shape[1]
    pad_dim = round_up(embed_dim, 16)
    unit = LOOK_LOW * LOOK_GROUP
    groups = (own_rows + unit - 1) // unit
    return pl.pallas_call(
        lookup_kernel,
        grid_spec=pltpu.PrefetchScalarGridSpec(
            num_scalar_prefetch=1,
            grid=(slot_count, count // LOOK_COLS),
            in_specs=[
                pl.BlockSpec((1, 1, LOOK_COLS), lambda s, c, *_: (s, 0, c)),
                pl.BlockSpec((1, embed_dim, table_len), lambda s, c, *_: (s, 0, 0)),
            ],
            out_specs=pl.BlockSpec((1, embed_dim, LOOK_COLS), lambda s, c, *_: (s, 0, c)),
            scratch_shapes=[pltpu.VMEM((table_len // LOOK_LOW, pad_dim, LOOK_LOW), BF)],
        ),
        out_shape=jax.ShapeDtypeStruct((slot_count, embed_dim, count), BF),
        compiler_params=pltpu.CompilerParams(vmem_limit_bytes=48 * 1024 * 1024),
        cost_estimate=pl.CostEstimate(
            flops=2 * slot_count * count * table_len * pad_dim,
            bytes_accessed=2 * slot_count * embed_dim * (table_len + count),
            transcendentals=0,
        ),
        name="lookup",
    )(groups, wanted[:, None, :], tables)


def add_kernel(base_ref, ids_ref, grad_ref, out_ref, total):
    step = pl.program_id(1)
    embed_dim = grad_ref.shape[2]
    cols = grad_ref.shape[3]

    @pl.when(step == 0)
    def _():
        total[...] = jnp.zeros_like(total)

    local = ids_ref[0, 0] - base_ref[0]
    high = lax.shift_right_arithmetic(local, ADD_LOW.bit_length() - 1)
    low = local & (ADD_LOW - 1)
    high_count = total.shape[1] // embed_dim
    high_iota = lax.broadcasted_iota(jnp.int32, (high_count, cols), 0)
    low_iota = lax.broadcasted_iota(jnp.int32, (ADD_LOW, cols), 0)
    high_hot = jnp.where(high_iota == high, 1.0, 0.0)
    low_hot = jnp.where(low_iota == low, 1.0, 0.0).astype(BF)
    grads = grad_ref[0, 0].astype(F32)
    left = (grads[:, None, :] * high_hot[None, :, :]).astype(BF).reshape(embed_dim * high_count, cols)
    product = lax.dot_general(left, low_hot, (((1,), (1,)), ((), ())), preferred_element_type=F32)
    for lane in range(ADD_LOW // 128):
        total[lane] += product[:, lane * 128 : (lane + 1) * 128]

    @pl.when(step == pl.num_programs(1) - 1)
    def _():
        for at in range(high_count):
            for part in range(0, embed_dim, 8):
                size = min(8, embed_dim - part)
                for lane in range(ADD_LOW // 128):
                    first = at * ADD_LOW + lane * 128
                    out_ref[0, part : part + size, first : first + 128] = total[
                        lane, pl.ds(part * high_count + at, size, stride=high_count), :
                    ]


def add_rows(grads, wanted, base, share):
    part_count, slot_count, embed_dim, count = grads.shape
    steps = count // ADD_COLS
    return pl.pallas_call(
        add_kernel,
        grid_spec=pltpu.PrefetchScalarGridSpec(
            num_scalar_prefetch=1,
            grid=(slot_count, part_count * steps),
            in_specs=[
                pl.BlockSpec((1, 1, 1, ADD_COLS), lambda s, c, *_: (c // steps, s, 0, c % steps)),
                pl.BlockSpec(
                    (1, 1, embed_dim, ADD_COLS), lambda s, c, *_: (c // steps, s, 0, c % steps)
                ),
            ],
            out_specs=pl.BlockSpec((1, embed_dim, share), lambda s, c, *_: (s, 0, 0)),
            scratch_shapes=[pltpu.VMEM((ADD_LOW // 128, embed_dim * (share // ADD_LOW), 128), F32)],
        ),
        out_shape=jax.ShapeDtypeStruct((slot_count, embed_dim, share), F32),
        compiler_params=pltpu.CompilerParams(vmem_limit_bytes=48 * 1024 * 1024),
        cost_estimate=pl.CostEstimate(
            flops=2 * part_count * slot_count * count * share * embed_dim,
            bytes_accessed=2 * slot_count * embed_dim * (2 * share + part_count * count),
            transcendentals=0,
        ),
        name="add_rows",
    )(base, wanted[:, :, None, :], grads)


def swish_slope(preact):
    sigmoid_val = jax.nn.sigmoid(preact)
    return sigmoid_val * (1.0 + preact * (1.0 - sigmoid_val))


def contract_rows(left_op, right_op):
    return lax.dot_general(
        left_op, right_op, (((0,), (0,)), ((), ())), preferred_element_type=jnp.float32
    )


def contract_cols(left_op, right_op):
    return lax.dot_general(
        left_op, right_op, (((1,), (1,)), ((), ())), preferred_element_type=jnp.float32
    )


def on_device(
    ids,
    table_rows,
    table_place,
    dense_in,
    labels,
    tables,
    cross_w,
    cross_b,
    tower1_w,
    tower1_b,
    tower2_w,
    tower2_b,
    out_w,
    out_b,
):
    tab_count = lax.axis_size("tab")
    device_count = tab_count * lax.axis_size("rep")
    slot_count = tables.shape[0]
    embed_dim = tables.shape[1]
    table_len = tables.shape[2]
    row_count = dense_in.shape[0]
    dense_width = dense_in.shape[1]
    field_count = ids.shape[1]
    model_width = cross_w.shape[1]
    layer_count = cross_w.shape[0]
    all_slots = slot_count * tab_count
    effective = ids % table_rows[None, :]
    slot_iota = jnp.arange(all_slots, dtype=jnp.int32)
    matches = table_place[:, None] == slot_iota[None, :]
    field_iota = jnp.arange(field_count, dtype=jnp.int32)
    slot_field = jnp.sum(jnp.where(matches, field_iota[:, None], 0), axis=0)
    slot_used = jnp.any(matches, axis=0)
    gathered = lax.all_gather(effective, "tab", axis=0, tiled=True)
    first_slot = lax.axis_index("tab") * slot_count
    own_field = lax.dynamic_slice_in_dim(slot_field, first_slot, slot_count)
    own_used = lax.dynamic_slice_in_dim(slot_used, first_slot, slot_count)
    wanted = jnp.where(own_used[:, None], jnp.take(gathered.T, own_field, axis=0), 0)
    own_rows = jnp.where(own_used, jnp.take(table_rows, own_field), 1)
    wanted_all = lax.all_gather(wanted, "rep", axis=0, tiled=False)
    looked = lookup(tables, wanted, own_rows)
    arrived = lax.all_to_all(looked, "tab", split_axis=2, concat_axis=0, tiled=True)
    picked = jnp.take(arrived, table_place, axis=0)
    embedded = jnp.transpose(picked, (2, 0, 1)).reshape(row_count, field_count * embed_dim)
    anchor = jnp.concatenate([dense_in, embedded], axis=1)
    anchor_f = anchor.astype(jnp.float32)
    current = anchor_f
    kept_low = []
    kept_update = []
    for layer_at in range(layer_count):
        current_low = current.astype(jnp.bfloat16)
        update = jnp.dot(
            current_low, cross_w[layer_at], preferred_element_type=jnp.float32
        ) + cross_b[layer_at].astype(jnp.float32)
        kept_low.append(current_low)
        kept_update.append(update)
        current = anchor_f * update + current
    first_pre = contract_cols(anchor, tower1_w) + tower1_b.astype(jnp.float32)
    first_low = jax.nn.silu(first_pre).astype(jnp.bfloat16)
    second_pre = jnp.dot(first_low, tower2_w, preferred_element_type=jnp.float32) + tower2_b.astype(
        jnp.float32
    )
    second_act = jax.nn.silu(second_pre)
    out_weight = out_w.astype(jnp.float32)
    logits = (
        jnp.dot(current, out_weight[:model_width], precision=HIGH)
        + jnp.dot(second_act, out_weight[model_width:], precision=HIGH)
        + out_b.astype(jnp.float32)
    )
    target = labels.astype(jnp.float32)
    loss_part = jnp.sum(jax.nn.softplus(logits) - target * logits)
    residue = jax.nn.sigmoid(logits) - target
    out_w_part = jnp.concatenate(
        [jnp.dot(residue, current, precision=HIGH), jnp.dot(residue, second_act, precision=HIGH)]
    )
    out_b_part = jnp.sum(residue)
    grad_current = residue[:, None] * out_weight[None, :model_width]
    grad_second = (
        residue[:, None] * out_weight[None, model_width:] * swish_slope(second_pre)
    ).astype(jnp.bfloat16)
    tower2_w_part = contract_rows(first_low, grad_second)
    tower2_b_part = jnp.sum(grad_second.astype(jnp.float32), axis=0)
    grad_first_act = contract_cols(grad_second, tower2_w)
    grad_first = (grad_first_act * swish_slope(first_pre)).astype(jnp.bfloat16)
    tower1_b_part = jnp.sum(grad_first.astype(jnp.float32), axis=0)
    grad_anchor = jnp.dot(grad_first, tower1_w, preferred_element_type=jnp.float32)
    weight_parts = [None] * layer_count
    bias_parts = [None] * layer_count
    for layer_at in reversed(range(layer_count)):
        grad_update = (anchor_f * grad_current).astype(jnp.bfloat16)
        weight_part = contract_rows(kept_low[layer_at], grad_update)
        bias_part = jnp.sum(grad_update.astype(jnp.float32), axis=0)
        weight_parts[layer_at] = weight_part
        bias_parts[layer_at] = bias_part
        grad_anchor = grad_anchor + grad_current * kept_update[layer_at]
        grad_current = grad_current + contract_cols(grad_update, cross_w[layer_at])
    grad_anchor = grad_anchor + grad_current
    grad_embed = (
        grad_anchor[:, dense_width:].astype(jnp.bfloat16).reshape(row_count, field_count, embed_dim)
    )
    grad_fields = jnp.transpose(grad_embed, (1, 2, 0))
    grad_slots = (
        jnp.zeros((all_slots, embed_dim, row_count), jnp.bfloat16).at[table_place].set(grad_fields)
    )
    returned = lax.all_to_all(grad_slots, "tab", split_axis=0, concat_axis=2, tiled=True)

    returned_all = lax.all_gather(returned, "rep", axis=0, tiled=False)
    share = table_len // lax.axis_size("rep")
    base = (lax.axis_index("rep") * share).astype(jnp.int32).reshape(1)
    table_grad = add_rows(returned_all, wanted_all, base, share)
    tower_share = lax.psum_scatter(
        contract_rows(grad_first, anchor), ("tab", "rep"), scatter_dimension=0, tiled=True
    )
    tower1_w_grad = lax.all_gather(tower_share, ("tab", "rep"), axis=0, tiled=True)
    weight_stack = jnp.stack(weight_parts)
    bias_stack = jnp.stack(bias_parts)
    (
        cross_w_grad,
        cross_b_grad,
        tower2_w_grad,
        tower2_b_grad,
        tower1_b_grad,
        out_w_grad,
        out_b_grad,
        loss_total,
    ) = lax.psum(
        (
            weight_stack,
            bias_stack,
            tower2_w_part,
            tower2_b_part,
            tower1_b_part,
            out_w_part,
            out_b_part,
            loss_part,
        ),
        ("tab", "rep"),
    )
    loss = loss_total / (row_count * device_count)
    dense_grad = grad_anchor[:, :dense_width]
    return (
        loss,
        logits,
        dense_grad,
        cross_w_grad,
        cross_b_grad,
        tower1_w_grad,
        tower1_b_grad,
        tower2_w_grad,
        tower2_b_grad,
        out_w_grad,
        out_b_grad,
        table_grad,
    )


def solution(mesh):
    placed = (
        P(("tab", "rep"), None),
        P(),
        P(),
        P(("tab", "rep"), None),
        P(("tab", "rep")),
        P("tab", None, None),
        P(),
        P(),
        P(),
        P(),
        P(),
        P(),
        P(),
        P(),
    )
    return jax.shard_map(
        on_device,
        mesh=mesh,
        in_specs=placed,
        out_specs=(
            P(),
            P(("tab", "rep")),
            P(("tab", "rep"), None),
            P(),
            P(),
            P(),
            P(),
            P(),
            P(),
            P(),
            P(),
            P("tab", None, "rep"),
        ),
        check_vma=False,
    )
```

```python
import functools

import jax
import jax.numpy as jnp
from jax import lax
from jax.experimental import pallas as pl
from jax.experimental.pallas import tpu as pltpu
from jax.sharding import PartitionSpec as P

BF = jnp.bfloat16
F32 = jnp.float32
I32 = jnp.int32
LOOK_LOW = 512
LOOK_GROUP = 8
ADD_LOW = 512
MAIN = 1024
CHUNK = 384
PIECE = 32
MIB = 1024 * 1024
NT = (((1,), (1,)), ((), ()))
TN = (((0,), (0,)), ((), ()))


def round_up(size, unit):
    return -(-size // unit) * unit


def params(mib):
    return pltpu.CompilerParams(vmem_limit_bytes=mib * MIB)


def cost(flops, size):
    return pl.CostEstimate(flops=flops, bytes_accessed=size, transcendentals=0)


def swap(value, axis, mask):
    return lax.ppermute(value, axis, [(at, at ^ mask) for at in range(lax.axis_size(axis))])


def masks_of(axis):
    size = lax.axis_size(axis)
    return [1 << bit for bit in range(size.bit_length() - 1)]


def lookup_kernel(group_ref, ids_ref, table_ref, out_ref, stack):
    slot = pl.program_id(0)
    embed_dim = table_ref.shape[1]
    block_count, pad_dim, low_count = stack.shape
    cols = out_ref.shape[3]

    @pl.when(pl.program_id(1) == 0)
    def _():
        for block in range(block_count):
            stack[block, :embed_dim, :] = table_ref[0, :, block * low_count : (block + 1) * low_count]

    picked = ids_ref[0, 0]
    high = lax.shift_right_arithmetic(picked, low_count.bit_length() - 1)
    low = picked & (low_count - 1)
    low_iota = lax.broadcasted_iota(I32, (low_count, cols), 0)
    onehot = jnp.where(low_iota == low, 1.0, 0.0).astype(BF)
    rows_kept = round_up(embed_dim, 8)

    def step(group, total):
        left = stack[pl.ds(group * LOOK_GROUP, LOOK_GROUP)].reshape(LOOK_GROUP * pad_dim, low_count)
        partial = jnp.dot(left, onehot, preferred_element_type=F32)
        for at in range(LOOK_GROUP):
            rows = partial[at * pad_dim : at * pad_dim + rows_kept]
            total = total + jnp.where(high == group * LOOK_GROUP + at, rows, 0.0)
        return total

    total = lax.fori_loop(0, group_ref[slot], step, jnp.zeros((rows_kept, cols), F32))
    out_ref[0, 0] = total[:embed_dim].astype(BF)


def lookup(tables, wanted, own_rows):
    slot_count, embed_dim, table_len = tables.shape
    tab_count, _, count = wanted.shape
    pad_dim = round_up(embed_dim, 16)
    unit = LOOK_LOW * LOOK_GROUP
    groups = (own_rows + unit - 1) // unit
    return pl.pallas_call(
        lookup_kernel,
        grid_spec=pltpu.PrefetchScalarGridSpec(
            num_scalar_prefetch=1,
            grid=(slot_count, tab_count),
            in_specs=[
                pl.BlockSpec((1, 1, 1, count), lambda s, t, *_: (t, s, 0, 0)),
                pl.BlockSpec((1, embed_dim, table_len), lambda s, t, *_: (s, 0, 0)),
            ],
            out_specs=pl.BlockSpec((1, 1, embed_dim, count), lambda s, t, *_: (t, s, 0, 0)),
            scratch_shapes=[pltpu.VMEM((table_len // LOOK_LOW, pad_dim, LOOK_LOW), BF)],
        ),
        out_shape=jax.ShapeDtypeStruct((tab_count, slot_count, embed_dim, count), BF),
        compiler_params=params(48),
        cost_estimate=cost(
            2 * slot_count * tab_count * count * table_len * pad_dim,
            2 * slot_count * embed_dim * (table_len + tab_count * count),
        ),
        name="lookup",
    )(groups, wanted[:, :, None, :], tables)


def add_kernel(part_count, base_ref, *refs):
    ids_refs = refs[:part_count]
    grad_refs = refs[part_count : 2 * part_count]
    out_ref, total = refs[-2:]
    step = pl.program_id(0)
    embed_dim, cols = grad_refs[0].shape[2:]
    high_count = total.shape[1] // embed_dim

    @pl.when(step == 0)
    def _():
        total[...] = jnp.zeros_like(total)

    high_iota = lax.broadcasted_iota(I32, (high_count, cols), 0)
    low_iota = lax.broadcasted_iota(I32, (ADD_LOW, cols), 0)
    product = None
    for ids_ref, grad_ref in zip(ids_refs, grad_refs):
        local = ids_ref[0, 0] - base_ref[0]
        high = lax.shift_right_arithmetic(local, ADD_LOW.bit_length() - 1)
        low = local & (ADD_LOW - 1)
        high_hot = jnp.where(high_iota == high, 1.0, 0.0)
        low_hot = jnp.where(low_iota == low, 1.0, 0.0).astype(BF)
        grads = grad_ref[0, 0].astype(F32)
        left = (grads[:, None, :] * high_hot[None, :, :]).astype(BF)
        left = left.reshape(embed_dim * high_count, cols)
        term = lax.dot_general(left, low_hot, NT, preferred_element_type=F32)
        product = term if product is None else product + term
    for lane in range(ADD_LOW // 128):
        total[lane] += product[:, lane * 128 : (lane + 1) * 128]

    @pl.when(step == pl.num_programs(0) - 1)
    def _():
        for at in range(high_count):
            for part in range(0, embed_dim, 8):
                size = min(8, embed_dim - part)
                for lane in range(ADD_LOW // 128):
                    first = at * ADD_LOW + lane * 128
                    out_ref[0, part : part + size, first : first + 128] = total[
                        lane, pl.ds(part * high_count + at, size, stride=high_count), :
                    ]


def add_rows(grads, wanted, base, share, slot, so_far):
    tab_count, slot_count, embed_dim, count = grads[0].shape
    part_count = len(grads)
    whole = [] if so_far is None else [so_far]
    return pl.pallas_call(
        functools.partial(add_kernel, part_count),
        grid=(tab_count,),
        in_specs=[pl.BlockSpec(memory_space=pltpu.SMEM)]
        + [pl.BlockSpec((1, 1, 1, count), lambda t: (t, slot, 0, 0))] * part_count
        + [pl.BlockSpec((1, 1, embed_dim, count), lambda t: (t, slot, 0, 0))] * part_count
        + [pl.BlockSpec(memory_space=pl.ANY)] * len(whole),
        out_specs=pl.BlockSpec((1, embed_dim, share), lambda t: (slot, 0, 0)),
        scratch_shapes=[pltpu.VMEM((ADD_LOW // 128, embed_dim * (share // ADD_LOW), 128), F32)],
        out_shape=jax.ShapeDtypeStruct((slot_count, embed_dim, share), F32),
        input_output_aliases={} if so_far is None else {1 + 2 * part_count: 0},
        compiler_params=params(40),
        cost_estimate=cost(
            2 * part_count * tab_count * count * share * embed_dim,
            2 * embed_dim * (2 * share + part_count * tab_count * count),
        ),
        name="add_rows",
    )(base, *[part[:, :, None, :] for part in wanted], *grads, *whole)


def row_sums(value):
    part = value[:, :128]
    for first in range(128, value.shape[1], 128):
        part = part + value[:, first : first + 128]
    return jnp.sum(part.T, axis=0, keepdims=True)


def dense_kernel(
    dense_width,
    place_ref,
    bias_ref,
    arrived_ref,
    dense_ref,
    label_ref,
    weight_hbm,
    cols_ref,
    logits_ref,
    dense_grad_ref,
    slots_ref,
    left_ref,
    right_ref,
    sums_ref,
    weight,
    anchor,
    current,
    update,
    first_pre,
    second_pre,
    grad_anchor,
    grad_current,
    sems,
):
    layer_count = update.shape[0]
    tower1, tower2 = layer_count, layer_count + 1
    field_count = place_ref.shape[0]
    embed_dim = arrived_ref.shape[1]
    width = dense_width + field_count * embed_dim
    size, cols = anchor.shape
    spans = [pl.ds(first, CHUNK) for first in range(0, size, CHUNK)]
    copies = [
        pltpu.make_async_copy(weight_hbm.at[at], weight.at[at], sems.at[at])
        for at in range(layer_count + 2)
    ]
    for copy in copies:
        copy.start()

    def column(at, span):
        return cols_ref[span, at : at + 1]

    def times(at, span, operand):
        return jnp.dot(weight[at, span, :], operand[...], preferred_element_type=F32)

    def transposed_times(at, span, operand):
        return lax.dot_general(weight[at, :, span], operand[...], TN, preferred_element_type=F32)

    anchor[0:16] = dense_ref[...]
    tail = width // 8 * 8
    anchor[tail:] = jnp.zeros((size - tail, cols), F32)
    for field in range(field_count):
        first = dense_width + field * embed_dim
        anchor[first : first + embed_dim] = arrived_ref[place_ref[field]].astype(F32)
    for span in spans:
        left_ref[0, span] = anchor[span].astype(BF)
        right_ref[tower1, span] = anchor[span].astype(BF)
    for layer in range(layer_count):
        copies[layer].wait()
        for span in spans:
            value = transposed_times(layer, span, left_ref.at[layer]) + column(layer, span)
            update[layer, span] = value
            before = anchor if layer == 0 else current
            after = anchor[span] * value + before[span]
            current[span] = after
            if layer + 1 < layer_count:
                left_ref[layer + 1, span] = after.astype(BF)
    copies[tower1].wait()
    for span in spans:
        value = times(tower1, span, left_ref.at[0]) + column(tower1, span)
        first_pre[span] = value
        left_ref[tower2, span] = (value * jax.nn.sigmoid(value)).astype(BF)
    copies[tower2].wait()
    logits = jnp.full((1, cols), bias_ref[0], F32)
    for span in spans:
        value = transposed_times(tower2, span, left_ref.at[tower2]) + column(tower2, span)
        second_pre[span] = value
        act = value * jax.nn.sigmoid(value)
        terms = current[span] * column(layer_count + 2, span) + act * column(layer_count + 3, span)
        logits = logits + jnp.sum(terms, axis=0, keepdims=True)
    logits_ref[...] = logits
    target = label_ref[...]
    residue = jax.nn.sigmoid(logits) - target
    softplus = jnp.maximum(logits, 0.0) + jnp.log1p(jnp.exp(-jnp.abs(logits)))
    sums_ref[layer_count + 4 :, :] = jnp.zeros((sums_ref.shape[0] - layer_count - 4, size), F32)
    loss_row = jnp.sum(softplus - target * logits, axis=1, keepdims=True)
    bias_row = jnp.sum(residue, axis=1, keepdims=True)
    sums_ref[layer_count + 4 : layer_count + 5, 0:128] = jnp.broadcast_to(loss_row, (1, 128))
    sums_ref[layer_count + 4 : layer_count + 5, 128:256] = jnp.broadcast_to(bias_row, (1, 128))
    for span in spans:
        value = second_pre[span]
        sig = jax.nn.sigmoid(value)
        act = value * sig
        grad = residue * column(layer_count + 3, span) * (sig * (1.0 + value * (1.0 - sig)))
        low = grad.astype(BF)
        right_ref[tower2, span] = low
        sums_ref[tower2 : tower2 + 1, span] = row_sums(low.astype(F32))
        sums_ref[layer_count + 3 : layer_count + 4, span] = row_sums(residue * act)
        sums_ref[layer_count + 2 : layer_count + 3, span] = row_sums(residue * current[span])
        grad_current[span] = residue * column(layer_count + 2, span)
    for span in spans:
        value = first_pre[span]
        sig = jax.nn.sigmoid(value)
        grad = times(tower2, span, right_ref.at[tower2]) * (sig * (1.0 + value * (1.0 - sig)))
        low = grad.astype(BF)
        left_ref[tower1, span] = low
        sums_ref[tower1 : tower1 + 1, span] = row_sums(low.astype(F32))
    for span in spans:
        grad_anchor[span] = transposed_times(tower1, span, left_ref.at[tower1])
    for layer in reversed(range(layer_count)):
        for span in spans:
            grad = grad_current[span]
            low = (anchor[span] * grad).astype(BF)
            right_ref[layer, span] = low
            sums_ref[layer : layer + 1, span] = row_sums(low.astype(F32))
            grad_anchor[span] += grad * update[layer, span]
        for span in spans:
            grad_current[span] += times(layer, span, right_ref.at[layer])
    for span in spans:
        grad_anchor[span] += grad_current[span]
    dense_grad_ref[...] = grad_anchor[0:16]
    slots_ref[...] = jnp.zeros_like(slots_ref)
    for field in range(field_count):
        first = dense_width + field * embed_dim
        slots_ref[place_ref[field]] = grad_anchor[first : first + embed_dim].astype(BF)


def dense_step(arrived, place, dense_in, labels, weights, cols, out_b, layer_count):
    slot_count, embed_dim, count = arrived.shape
    dense_width = dense_in.shape[1]
    size = weights.shape[1]
    matrix_count = layer_count + 2
    dense_rows = jnp.pad(dense_in.T.astype(F32), ((0, 16 - dense_width), (0, 0)))
    vmem = pl.BlockSpec(memory_space=pltpu.VMEM)
    smem = pl.BlockSpec(memory_space=pltpu.SMEM)
    flat = pltpu.VMEM((size, count), F32)
    return pl.pallas_call(
        functools.partial(dense_kernel, dense_width),
        in_specs=[smem, smem, vmem, vmem, vmem, pl.BlockSpec(memory_space=pl.ANY), vmem],
        out_specs=[vmem] * 6,
        out_shape=[
            jax.ShapeDtypeStruct((1, count), F32),
            jax.ShapeDtypeStruct((16, count), F32),
            jax.ShapeDtypeStruct((slot_count, embed_dim, count), BF),
            jax.ShapeDtypeStruct((matrix_count, size, count), BF),
            jax.ShapeDtypeStruct((matrix_count, size, count), BF),
            jax.ShapeDtypeStruct((8, size), F32),
        ],
        scratch_shapes=[
            pltpu.VMEM(weights.shape, BF),
            flat,
            flat,
            pltpu.VMEM((layer_count, size, count), F32),
            flat,
            flat,
            flat,
            flat,
            pltpu.SemaphoreType.DMA((matrix_count,)),
        ],
        compiler_params=params(60),
        cost_estimate=cost(4 * matrix_count * size * size * count, 2 * weights.size + 30 * size * count),
        name="dense",
    )(
        place,
        out_b.astype(F32).reshape(1),
        arrived,
        dense_rows,
        labels.astype(F32).reshape(1, count),
        weights,
        cols,
    )


def weight_kernel(own_ref, left_ref, right_ref, keep_ref, send_ref, strip_ref, moved):
    pieces = MAIN // PIECE
    for at in range(pieces):
        first = pl.multiple_of((at ^ own_ref[0]) * PIECE, PIECE)
        moved[at * PIECE : (at + 1) * PIECE] = left_ref[0, pl.ds(first, PIECE), :]
    half = MAIN // 2
    right = right_ref[0, :MAIN, :]
    keep_ref[0] = lax.dot_general(moved[:half], right, NT, preferred_element_type=F32)
    send_ref[0] = lax.dot_general(moved[half:], right, NT, preferred_element_type=F32).astype(BF)
    below = lax.dot_general(left_ref[0, MAIN : MAIN + 16, :], right_ref[0], NT, preferred_element_type=F32)
    beside = lax.dot_general(right_ref[0, MAIN : MAIN + 16, :], left_ref[0], NT, preferred_element_type=F32)
    strip_ref[0, 0:3] = below[0:3]
    strip_ref[0, 3:6] = beside[0:3]
    strip_ref[0, 6:8] = jnp.zeros((2, strip_ref.shape[2]), F32)


def weight_parts(left, right, own):
    matrix_count, size, count = left.shape
    half = MAIN // 2
    return pl.pallas_call(
        weight_kernel,
        grid=(matrix_count,),
        in_specs=[
            pl.BlockSpec(memory_space=pltpu.SMEM),
            pl.BlockSpec((1, size, count), lambda m: (m, 0, 0)),
            pl.BlockSpec((1, size, count), lambda m: (m, 0, 0)),
        ],
        out_specs=[
            pl.BlockSpec((1, half, MAIN), lambda m: (m, 0, 0)),
            pl.BlockSpec((1, half, MAIN), lambda m: (m, 0, 0)),
            pl.BlockSpec((1, 8, size), lambda m: (m, 0, 0)),
        ],
        out_shape=[
            jax.ShapeDtypeStruct((matrix_count, half, MAIN), F32),
            jax.ShapeDtypeStruct((matrix_count, half, MAIN), BF),
            jax.ShapeDtypeStruct((matrix_count, 8, size), F32),
        ],
        scratch_shapes=[pltpu.VMEM((MAIN, count), BF)],
        compiler_params=params(40),
        cost_estimate=cost(2 * matrix_count * size * size * count, 10 * matrix_count * size * size),
        name="weight_parts",
    )(own, left, right)


def reduce_main(keep, send, swapped):
    total = keep + swap(send, "rep", 1).astype(F32)
    pair = [("rep", 2, 1), ("tab", 1, 2)]
    if swapped:
        pair = [pair[1], pair[0]]
    (axis, mask, dim) = pair[0]
    total = lax.index_in_dim(total, 0, dim, False) + swap(
        lax.index_in_dim(total, 1, dim, False).astype(BF), axis, mask
    ).astype(F32)
    (axis, mask, _) = pair[1]
    total = total[:, 0] + swap(total[:, 1].astype(BF), axis, mask).astype(F32)
    kept = total[:, 0, 0]
    for high, low in ((0, 1), (1, 0), (1, 1)):
        kept = kept + swap(total[:, high, low].astype(BF), "tab", 4 * high + 2 * low).astype(F32)
    piece = kept.astype(BF)
    for axis, known in (("rep", 2), ("tab", 3)):
        for mask in masks_of(axis)[known:]:
            piece = (piece.astype(F32) + swap(piece, axis, mask).astype(F32)).astype(BF)
    return piece


def gather_main(piece, swapped):
    low = jnp.stack([piece, swap(piece, "tab", 2)], axis=1)
    high = jnp.stack([swap(piece, "tab", 4), swap(piece, "tab", 6)], axis=1)
    value = jnp.stack([low, high], axis=1)
    pair = [("rep", 2, 1), ("tab", 1, 2)]
    if swapped:
        pair = [pair[1], pair[0]]
    (axis, mask, _) = pair[1]
    value = jnp.stack([value, swap(value, axis, mask)], axis=1)
    (axis, mask, dim) = pair[0]
    value = jnp.stack([value, swap(value, axis, mask)], axis=dim)
    value = value.reshape((value.shape[0], MAIN // PIECE // 2) + value.shape[-2:])
    return value, swap(value, "rep", 1)


def assemble_kernel(layer_count, chunk_count, own_ref, *refs):
    chunks = refs[: 2 * chunk_count]
    strip_ref, cross_ref, first_ref, second_ref = refs[2 * chunk_count :]
    matrix = pl.program_id(0)
    lanes_count = chunk_count // 2

    def fill(out_ref):
        for chunk in range(chunk_count):
            above, lane = divmod(chunk, lanes_count)
            for core in range(2):
                ref = chunks[2 * chunk + core]
                count, rows, lanes = ref.shape[1:]
                for at in range(count):
                    piece = (core * count + at) ^ own_ref[0]
                    first = pl.multiple_of(piece * PIECE + above * rows, rows)
                    out_ref[0, pl.ds(first, rows), lane * lanes : (lane + 1) * lanes] = ref[
                        0, at
                    ].astype(F32)
        height, width = out_ref.shape[1:]
        if width > MAIN:
            extra = width - MAIN
            for first in range(0, MAIN, 128):
                turned = strip_ref[0, :, first : first + 128].T
                out_ref[0, first : first + 128, MAIN:] = turned[:, 3 : 3 + extra]
        if height > MAIN:
            out_ref[0, MAIN:, :] = strip_ref[0, 0 : height - MAIN, :width]

    @pl.when(matrix < layer_count)
    def _():
        fill(cross_ref)

    @pl.when(matrix == layer_count)
    def _():
        fill(first_ref)

    @pl.when(matrix == layer_count + 1)
    def _():
        fill(second_ref)


def assemble(chunks, strips, own, layer_count, width, hidden):
    matrix_count = layer_count + 2
    size = strips.shape[2]
    specs = []
    for chunk in chunks:
        specs.append(pl.BlockSpec((1,) + chunk.shape[1:], lambda m: (m, 0, 0, 0)))
    return pl.pallas_call(
        functools.partial(assemble_kernel, layer_count, len(chunks) // 2),
        grid=(matrix_count,),
        in_specs=[pl.BlockSpec(memory_space=pltpu.SMEM)]
        + specs
        + [pl.BlockSpec((1, 8, size), lambda m: (m, 0, 0))],
        out_specs=[
            pl.BlockSpec((1, width, width), lambda m: (jnp.minimum(m, layer_count - 1), 0, 0)),
            pl.BlockSpec((1, hidden, width), lambda m: (0, 0, 0)),
            pl.BlockSpec((1, hidden, hidden), lambda m: (0, 0, 0)),
        ],
        out_shape=[
            jax.ShapeDtypeStruct((layer_count, width, width), F32),
            jax.ShapeDtypeStruct((1, hidden, width), F32),
            jax.ShapeDtypeStruct((1, hidden, hidden), F32),
        ],
        compiler_params=params(56),
        cost_estimate=cost(0, 6 * matrix_count * size * size),
        name="assemble",
    )(own, *chunks, strips)


def on_device(
    ids,
    table_rows,
    table_place,
    dense_in,
    labels,
    tables,
    cross_w,
    cross_b,
    tower1_w,
    tower1_b,
    tower2_w,
    tower2_b,
    out_w,
    out_b,
):
    tab_count = lax.axis_size("tab")
    rep_count = lax.axis_size("rep")
    slot_count, embed_dim, table_len = tables.shape
    row_count, dense_width = dense_in.shape
    field_count = ids.shape[1]
    layer_count, width = cross_w.shape[:2]
    hidden = tower1_w.shape[0]
    size = round_up(width, 128)
    all_slots = slot_count * tab_count
    tab_at = lax.axis_index("tab")
    rep_at = lax.axis_index("rep")

    matches = table_place[:, None] == jnp.arange(all_slots, dtype=I32)[None, :]
    effective = ids % table_rows[None, :]
    by_slot = jnp.sum(jnp.where(matches[:, :, None], effective.T[:, None, :], 0), axis=0)
    slot_rows = jnp.sum(jnp.where(matches, table_rows[:, None], 0), axis=0)
    own_rows = lax.dynamic_slice_in_dim(slot_rows, tab_at * slot_count, slot_count)
    wanted = lax.all_to_all(
        by_slot.reshape(tab_count, slot_count, row_count), "tab", split_axis=0, concat_axis=0, tiled=True
    )

    def padded(weight):
        return jnp.pad(weight, ((0, size - weight.shape[0]), (0, size - weight.shape[1])))

    weights = jnp.stack(
        [padded(cross_w[at]) for at in range(layer_count)] + [padded(tower1_w), padded(tower2_w)]
    )
    vectors = [cross_b[at] for at in range(layer_count)]
    vectors += [tower1_b, tower2_b, out_w[:width], out_w[width:], out_w[:0]]
    cols = jnp.stack([jnp.pad(v.astype(F32), (0, size - v.shape[0])) for v in vectors], axis=1)

    looked = lookup(tables, wanted, own_rows)
    arrived = lax.all_to_all(looked, "tab", split_axis=0, concat_axis=0, tiled=True)
    arrived = arrived.reshape(all_slots, embed_dim, row_count)
    logits, dense_grad, slots, left, right, sums = dense_step(
        arrived, table_place, dense_in, labels, weights, cols, out_b, layer_count
    )
    returned = lax.all_to_all(
        slots.reshape(tab_count, slot_count, embed_dim, row_count),
        "tab",
        split_axis=0,
        concat_axis=0,
        tiled=True,
    )

    def spread(own):
        parts = [own]
        for mask in reversed(masks_of("rep")):
            parts = parts + [swap(part, "rep", mask) for part in parts]
        return parts

    wanted_parts = spread(wanted)
    grad_parts = spread(returned)
    share = table_len // rep_count
    base = (rep_at * share).astype(I32).reshape(1)
    table_grad = None
    for slot in range(slot_count):
        table_grad = add_rows(grad_parts, wanted_parts, base, share, slot, table_grad)

    bits = [rep_at & 1, (rep_at >> 1) & 1, tab_at & 1, (tab_at >> 2) & 1, (tab_at >> 1) & 1]
    own = sum(bit << (4 - at) for at, bit in enumerate(bits)).astype(I32).reshape(1)
    keep, send, strips = weight_parts(left, right, own)
    matrix_count = layer_count + 2
    parts = (matrix_count, 2, 2, 2, 2, 2, PIECE // 2, 2, MAIN // 2)
    keep = keep.reshape(parts)
    send = send.reshape(parts)
    chunks = []
    for chunk in range(4):
        above, lane = divmod(chunk, 2)
        swapped = lane == 1
        piece = reduce_main(keep[..., above, :, lane, :], send[..., above, :, lane, :], swapped)
        chunks.extend(gather_main(piece, swapped))

    small = jnp.concatenate([strips.reshape(matrix_count * 8, size), sums], axis=0)
    for axis in ("rep", "tab"):
        for mask in masks_of(axis):
            small = small + swap(small, axis, mask)
    strips = small[:-8].reshape(matrix_count, 8, size)
    sums = small[-8:]
    cross_w_grad, tower1_w_grad, tower2_w_grad = assemble(
        chunks, strips, own, layer_count, width, hidden
    )
    scalars = sums[layer_count + 4]
    return (
        scalars[0] / (row_count * tab_count * rep_count),
        logits.reshape(row_count),
        dense_grad[:dense_width].T,
        cross_w_grad,
        sums[:layer_count, :width],
        tower1_w_grad[0],
        sums[layer_count, :hidden],
        tower2_w_grad[0],
        sums[layer_count + 1, :hidden],
        jnp.concatenate([sums[layer_count + 2, :width], sums[layer_count + 3, :hidden]]),
        scalars[128],
        table_grad,
    )


def solution(mesh):
    placed = (
        P(("tab", "rep"), None),
        P(),
        P(),
        P(("tab", "rep"), None),
        P(("tab", "rep")),
        P("tab", None, None),
        P(),
        P(),
        P(),
        P(),
        P(),
        P(),
        P(),
        P(),
    )
    return jax.shard_map(
        on_device,
        mesh=mesh,
        in_specs=placed,
        out_specs=(
            P(),
            P(("tab", "rep")),
            P(("tab", "rep"), None),
            P(),
            P(),
            P(),
            P(),
            P(),
            P(),
            P(),
            P(),
            P("tab", None, "rep"),
        ),
        check_vma=False,
    )
```

```python
import functools

import jax
import jax.numpy as jnp
from jax import lax
from jax.experimental import pallas as pl
from jax.experimental.pallas import tpu as pltpu
from jax.sharding import PartitionSpec as P

BF = jnp.bfloat16
F32 = jnp.float32
I32 = jnp.int32
LOOK_SLOTS = 3
LOOK_LANES = 40
LOOK_BLOCKS = 8
LOOK_ROWS = 32
ADD_LOW = 512
MAIN = 1024
CHUNK = 384
PIECE = 32
MIB = 1024 * 1024
NT = (((1,), (1,)), ((), ()))
TN = (((0,), (0,)), ((), ()))


def round_up(size, unit):
    return -(-size // unit) * unit


def params(mib):
    return pltpu.CompilerParams(vmem_limit_bytes=mib * MIB)


def cost(flops, size):
    return pl.CostEstimate(flops=flops, bytes_accessed=size, transcendentals=0)


def swap(value, axis, mask):
    return lax.ppermute(value, axis, [(at, at ^ mask) for at in range(lax.axis_size(axis))])


def masks_of(axis):
    size = lax.axis_size(axis)
    return [1 << bit for bit in range(size.bit_length() - 1)]


def lookup_kernel(first_slot, ids_ref, rows_ref, table_hbm, out_ref, raw, stack, major, picked, sems):
    tab_count, slot_count, pad_dim, count = out_ref.shape
    embed_dim = raw.shape[1]
    total = tab_count * count
    copies = [
        pltpu.make_async_copy(table_hbm.at[first_slot + at], raw.at[at], sems.at[at])
        for at in range(slot_count)
    ]
    for copy in copies:
        copy.start()
    lane = lax.broadcasted_iota(I32, (1, 128), 1)
    stack[...] = jnp.zeros_like(stack)
    most = jnp.maximum(rows_ref[first_slot], 1)
    for at in range(1, slot_count):
        most = jnp.maximum(most, rows_ref[first_slot + at])
    for copy in copies:
        copy.wait()
    unit = 128 * LOOK_BLOCKS

    @pl.loop(0, (most + unit - 1) // unit)
    def _(step):
        for block in range(LOOK_BLOCKS):
            first = pl.multiple_of((step * LOOK_BLOCKS + block) * 128, 128)
            for at in range(slot_count):
                stack[block, at * LOOK_LANES : at * LOOK_LANES + embed_dim, :] = raw[
                    at, :, pl.ds(first, 128)
                ].astype(F32)
            major[pl.ds(first, 128), :] = stack[block].T

    @pl.loop(0, total // LOOK_ROWS)
    def _(step):
        base = step * LOOK_ROWS
        starts = [(first_slot + at) * total + base for at in range(slot_count)]
        for row in range(LOOK_ROWS):
            value = None
            for at in reversed(range(slot_count)):
                one = major[pl.ds(ids_ref[starts[at] + row], 1), :]
                value = one if value is None else jnp.where(lane < (at + 1) * LOOK_LANES, one, value)
            picked[pl.ds(base + row, 1), :] = value

    @pl.loop(0, tab_count)
    def _(tab):
        for block in range(0, count, 128):
            turned = picked[pl.ds(pl.multiple_of(tab * count + block, 128), 128), :].T
            for at in range(slot_count):
                rows = turned[at * LOOK_LANES : at * LOOK_LANES + pad_dim]
                out_ref[tab, at, :, block : block + 128] = rows.astype(BF)


def lookup(tables, wanted, own_rows, tab_count, first_slot, slot_count):
    all_count, embed_dim, table_len = tables.shape
    count = wanted.shape[0] // (all_count * tab_count)
    smem = pl.BlockSpec(memory_space=pltpu.SMEM)
    return pl.pallas_call(
        functools.partial(lookup_kernel, first_slot),
        in_specs=[smem, smem, pl.BlockSpec(memory_space=pl.ANY)],
        out_specs=pl.BlockSpec(memory_space=pltpu.VMEM),
        out_shape=jax.ShapeDtypeStruct((tab_count, slot_count, round_up(embed_dim, 8), count), BF),
        scratch_shapes=[
            pltpu.VMEM((slot_count, embed_dim, table_len), BF),
            pltpu.VMEM((LOOK_BLOCKS, 128, 128), F32),
            pltpu.VMEM((table_len, 128), F32),
            pltpu.VMEM((tab_count * count, 128), F32),
            pltpu.SemaphoreType.DMA((slot_count,)),
        ],
        compiler_params=params(56),
        cost_estimate=cost(
            600 * tab_count * count * table_len * slot_count // 8,
            2 * slot_count * embed_dim * (table_len + tab_count * count),
        ),
        name="lookup",
    )(wanted, own_rows, tables)


def add_kernel(part_count, has_before, base_ref, *refs):
    ids_refs = refs[:part_count]
    grad_refs = refs[part_count : 2 * part_count]
    before_ref = refs[2 * part_count] if has_before else None
    out_ref, token_ref, total = refs[-3:]
    step = pl.program_id(0)
    embed_dim = out_ref.shape[1]
    cols = grad_refs[0].shape[3]
    high_count = total.shape[1] // embed_dim

    @pl.when(step == 0)
    def _():
        total[...] = jnp.zeros_like(total)
        token_ref[...] = jnp.zeros_like(token_ref)

    high_iota = lax.broadcasted_iota(I32, (high_count, cols), 0)
    low_iota = lax.broadcasted_iota(I32, (ADD_LOW, cols), 0)
    product = None
    for ids_ref, grad_ref in zip(ids_refs, grad_refs):
        local = ids_ref[0, 0] - base_ref[0]
        high = lax.shift_right_arithmetic(local, ADD_LOW.bit_length() - 1)
        low = local & (ADD_LOW - 1)
        high_hot = jnp.where(high_iota == high, 1.0, 0.0)
        low_hot = jnp.where(low_iota == low, 1.0, 0.0).astype(BF)
        grads = grad_ref[0, 0, :embed_dim].astype(F32)
        left = (grads[:, None, :] * high_hot[None, :, :]).astype(BF)
        left = left.reshape(embed_dim * high_count, cols)
        term = lax.dot_general(left, low_hot, NT, preferred_element_type=F32)
        product = term if product is None else product + term
    for lane in range(ADD_LOW // 128):
        total[lane] += product[:, lane * 128 : (lane + 1) * 128]

    @pl.when(step == pl.num_programs(0) - 1)
    def _():
        for at in range(high_count):
            for part in range(0, embed_dim, 8):
                size = min(8, embed_dim - part)
                for lane in range(ADD_LOW // 128):
                    first = at * ADD_LOW + lane * 128
                    value = total[lane, pl.ds(part * high_count + at, size, stride=high_count), :]
                    if before_ref is not None:
                        value = value + before_ref[0, part : part + size, first : first + 128]
                    out_ref[0, part : part + size, first : first + 128] = value


def add_rows(grads, wanted, base, share, embed_dim, slot, so_far, accumulate, after):
    tab_count, slot_count, pad_dim, count = grads[0].shape
    part_count = len(grads)
    anywhere = pl.BlockSpec(memory_space=pl.ANY)
    block = pl.BlockSpec((1, embed_dim, share), lambda t: (slot, 0, 0))
    whole = [] if so_far is None else [so_far]
    table_grad, token = pl.pallas_call(
        functools.partial(add_kernel, part_count, accumulate),
        grid=(tab_count,),
        in_specs=[pl.BlockSpec(memory_space=pltpu.SMEM)]
        + [pl.BlockSpec((1, 1, 1, count), lambda t: (t, slot, 0, 0))] * part_count
        + [pl.BlockSpec((1, 1, pad_dim, count), lambda t: (t, slot, 0, 0))] * part_count
        + [block if accumulate else anywhere] * len(whole)
        + [anywhere] * len(after),
        out_specs=[block, pl.BlockSpec((8, 128), lambda t: (0, 0))],
        scratch_shapes=[pltpu.VMEM((ADD_LOW // 128, embed_dim * (share // ADD_LOW), 128), F32)],
        out_shape=[
            jax.ShapeDtypeStruct((slot_count, embed_dim, share), F32),
            jax.ShapeDtypeStruct((8, 128), F32),
        ],
        input_output_aliases={1 + 2 * part_count: 0} if whole else {},
        compiler_params=params(40),
        cost_estimate=cost(
            2 * part_count * tab_count * count * share * embed_dim,
            2 * embed_dim * (2 * share + part_count * tab_count * count),
        ),
        name="add_rows",
    )(base, *[part[:, :, None, :] for part in wanted], *grads, *whole, *after)
    return table_grad, token[0, 0]


def row_sums(value):
    part = value[:, :128]
    for first in range(128, value.shape[1], 128):
        part = part + value[:, first : first + 128]
    return jnp.sum(part.T, axis=0, keepdims=True)


def dense_kernel(
    dense_width,
    width,
    starts,
    place_ref,
    bias_ref,
    *refs,
):
    group_count = len(starts)
    arrived_refs = refs[:group_count]
    dense_refs = refs[group_count:]
    dense_body(dense_width, width, starts, place_ref, bias_ref, arrived_refs, *dense_refs)


def dense_body(
    dense_width,
    width,
    starts,
    place_ref,
    bias_ref,
    arrived_refs,
    dense_ref,
    label_ref,
    weight_hbm,
    cols_ref,
    logits_ref,
    dense_grad_ref,
    slots_ref,
    left_ref,
    right_ref,
    sums_ref,
    weight,
    anchor,
    current,
    update,
    first_pre,
    second_pre,
    grad_anchor,
    grad_current,
    sems,
):
    layer_count = update.shape[0]
    tower1, tower2 = layer_count, layer_count + 1
    pad_dim = arrived_refs[0].shape[2]
    field_count = place_ref.shape[0]
    embed_dim = (width - dense_width) // field_count
    slot_count = sum(ref.shape[1] for ref in arrived_refs)
    size, cols = anchor.shape
    spans = [pl.ds(first, CHUNK) for first in range(0, size, CHUNK)]
    copies = [
        pltpu.make_async_copy(weight_hbm.at[at], weight.at[at], sems.at[at])
        for at in range(layer_count + 2)
    ]
    for copy in copies:
        copy.start()

    def column(at, span):
        return cols_ref[span, at : at + 1]

    def times(at, span, operand):
        return jnp.dot(weight[at, span, :], operand[...], preferred_element_type=F32)

    def transposed_times(at, span, operand):
        return lax.dot_general(weight[at, :, span], operand[...], TN, preferred_element_type=F32)

    anchor[0:16] = dense_ref[...]
    tail = width // 8 * 8
    anchor[tail:] = jnp.zeros((size - tail, cols), F32)
    for field in range(field_count):
        first = dense_width + field * embed_dim
        tab = place_ref[field] // slot_count
        slot = place_ref[field] - tab * slot_count
        value = arrived_refs[0][tab, jnp.minimum(slot, arrived_refs[0].shape[1] - 1)]
        for begin, ref in zip(starts[1:], arrived_refs[1:]):
            other = ref[tab, jnp.clip(slot - begin, 0, ref.shape[1] - 1)]
            value = jnp.where(slot >= begin, other, value)
        anchor[first : first + embed_dim] = value.astype(F32)[:embed_dim]
    for span in spans:
        left_ref[0, span] = anchor[span].astype(BF)
        left_ref[tower1, span] = anchor[span].astype(BF)
    for layer in range(layer_count):
        copies[layer].wait()
        for span in spans:
            value = transposed_times(layer, span, left_ref.at[layer]) + column(layer, span)
            update[layer, span] = value
            before = anchor if layer == 0 else current
            after = anchor[span] * value + before[span]
            current[span] = after
            if layer + 1 < layer_count:
                left_ref[layer + 1, span] = after.astype(BF)
    copies[tower1].wait()
    for span in spans:
        value = transposed_times(tower1, span, left_ref.at[0]) + column(tower1, span)
        first_pre[span] = value
        left_ref[tower2, span] = (value * jax.nn.sigmoid(value)).astype(BF)
    copies[tower2].wait()
    logits = jnp.full((1, cols), bias_ref[0], F32)
    for span in spans:
        value = transposed_times(tower2, span, left_ref.at[tower2]) + column(tower2, span)
        second_pre[span] = value
        act = value * jax.nn.sigmoid(value)
        terms = current[span] * column(layer_count + 2, span) + act * column(layer_count + 3, span)
        logits = logits + jnp.sum(terms, axis=0, keepdims=True)
    logits_ref[...] = logits
    target = label_ref[...]
    residue = jax.nn.sigmoid(logits) - target
    softplus = jnp.maximum(logits, 0.0) + jnp.log1p(jnp.exp(-jnp.abs(logits)))
    sums_ref[layer_count + 4 :, :] = jnp.zeros((sums_ref.shape[0] - layer_count - 4, size), F32)
    loss_row = jnp.sum(softplus - target * logits, axis=1, keepdims=True)
    bias_row = jnp.sum(residue, axis=1, keepdims=True)
    sums_ref[layer_count + 4 : layer_count + 5, 0:128] = jnp.broadcast_to(loss_row, (1, 128))
    sums_ref[layer_count + 4 : layer_count + 5, 128:256] = jnp.broadcast_to(bias_row, (1, 128))
    for span in spans:
        value = second_pre[span]
        sig = jax.nn.sigmoid(value)
        act = value * sig
        grad = residue * column(layer_count + 3, span) * (sig * (1.0 + value * (1.0 - sig)))
        low = grad.astype(BF)
        right_ref[tower2, span] = low
        sums_ref[tower2 : tower2 + 1, span] = row_sums(low.astype(F32))
        sums_ref[layer_count + 3 : layer_count + 4, span] = row_sums(residue * act)
        sums_ref[layer_count + 2 : layer_count + 3, span] = row_sums(residue * current[span])
        grad_current[span] = residue * column(layer_count + 2, span)
    for span in spans:
        value = first_pre[span]
        sig = jax.nn.sigmoid(value)
        grad = times(tower2, span, right_ref.at[tower2]) * (sig * (1.0 + value * (1.0 - sig)))
        low = grad.astype(BF)
        right_ref[tower1, span] = low
        sums_ref[tower1 : tower1 + 1, span] = row_sums(low.astype(F32))
    for span in spans:
        grad_anchor[span] = times(tower1, span, right_ref.at[tower1])
    for layer in reversed(range(layer_count)):
        for span in spans:
            grad = grad_current[span]
            low = (anchor[span] * grad).astype(BF)
            right_ref[layer, span] = low
            sums_ref[layer : layer + 1, span] = row_sums(low.astype(F32))
            grad_anchor[span] += grad * update[layer, span]
        for span in spans:
            grad_current[span] += times(layer, span, right_ref.at[layer])
    for span in spans:
        grad_anchor[span] += grad_current[span]
    dense_grad_ref[...] = grad_anchor[0:16]
    slots_ref[...] = jnp.zeros_like(slots_ref)
    for field in range(field_count):
        first = dense_width + field * embed_dim
        slots_ref[place_ref[field], :embed_dim] = grad_anchor[first : first + embed_dim].astype(BF)


def dense_step(arrived, starts, place, dense_in, labels, weights, cols, out_b, layer_count, width):
    tab_count, _, pad_dim, count = arrived[0].shape
    slot_count = tab_count * sum(part.shape[1] for part in arrived)
    dense_width = dense_in.shape[1]
    size = weights.shape[1]
    matrix_count = layer_count + 2
    dense_rows = jnp.pad(dense_in.T.astype(F32), ((0, 16 - dense_width), (0, 0)))
    vmem = pl.BlockSpec(memory_space=pltpu.VMEM)
    smem = pl.BlockSpec(memory_space=pltpu.SMEM)
    flat = pltpu.VMEM((size, count), F32)
    return pl.pallas_call(
        functools.partial(dense_kernel, dense_width, width, starts),
        in_specs=[smem, smem] + [vmem] * (len(arrived) + 2) + [ pl.BlockSpec(memory_space=pl.ANY), vmem],
        out_specs=[vmem] * 6,
        out_shape=[
            jax.ShapeDtypeStruct((1, count), F32),
            jax.ShapeDtypeStruct((16, count), F32),
            jax.ShapeDtypeStruct((slot_count, pad_dim, count), BF),
            jax.ShapeDtypeStruct((matrix_count, size, count), BF),
            jax.ShapeDtypeStruct((matrix_count, size, count), BF),
            jax.ShapeDtypeStruct((8, size), F32),
        ],
        scratch_shapes=[
            pltpu.VMEM(weights.shape, BF),
            flat,
            flat,
            pltpu.VMEM((layer_count, size, count), F32),
            flat,
            flat,
            flat,
            flat,
            pltpu.SemaphoreType.DMA((matrix_count,)),
        ],
        compiler_params=params(60),
        cost_estimate=cost(4 * matrix_count * size * size * count, 2 * weights.size + 30 * size * count),
        name="dense",
    )(
        place,
        out_b.astype(F32).reshape(1),
        *arrived,
        dense_rows,
        labels.astype(F32).reshape(1, count),
        weights,
        cols,
    )


def chunk_place(piece, swapped):
    if not swapped:
        return piece
    return (piece & 3) | ((piece & 4) << 1) | ((piece & 8) >> 1)


def weight_kernel(own_ref, left_ref, right_ref, *refs):
    keep_refs, send_refs = refs[:4], refs[4:8]
    strip_ref, moved = refs[8:]
    pieces = MAIN // PIECE
    rows = PIECE // 2
    half = MAIN // 2
    right = right_ref[0, :MAIN, :]
    for above in range(2):
        for at in range(pieces):
            first = pl.multiple_of((at ^ own_ref[0]) * PIECE + above * rows, rows)
            moved[(above * pieces + at) * rows : (above * pieces + at + 1) * rows] = left_ref[
                0, pl.ds(first, rows), :
            ]
    for above in range(2):
        product = lax.dot_general(
            moved[above * half : (above + 1) * half], right, NT, preferred_element_type=F32
        )
        for lane in range(2):
            part = product[:, lane * half : (lane + 1) * half]
            for at in range(pieces // 2):
                to = chunk_place(at, lane == 1)
                keep_refs[2 * above + lane][to, 0] = part[at * rows : (at + 1) * rows]
                other = (pieces // 2 + at) * rows
                send_refs[2 * above + lane][to, 0] = part[other : other + rows].astype(BF)
    below = lax.dot_general(left_ref[0, MAIN : MAIN + 16, :], right_ref[0], NT, preferred_element_type=F32)
    beside = lax.dot_general(right_ref[0, MAIN : MAIN + 16, :], left_ref[0], NT, preferred_element_type=F32)
    strip_ref[0, 0:3] = below[0:3]
    strip_ref[0, 3:6] = beside[0:3]
    strip_ref[0, 6:8] = jnp.zeros((2, strip_ref.shape[2]), F32)


def weight_parts(left, right, own):
    matrix_count, size, count = left.shape
    half = MAIN // 2
    pieces = MAIN // PIECE // 2
    chunk = pl.BlockSpec((pieces, 1, PIECE // 2, half), lambda m: (0, m, 0, 0))
    shape = (pieces, matrix_count, PIECE // 2, half)
    outs = pl.pallas_call(
        weight_kernel,
        grid=(matrix_count,),
        in_specs=[
            pl.BlockSpec(memory_space=pltpu.SMEM),
            pl.BlockSpec((1, size, count), lambda m: (m, 0, 0)),
            pl.BlockSpec((1, size, count), lambda m: (m, 0, 0)),
        ],
        out_specs=[chunk] * 8 + [pl.BlockSpec((1, 8, size), lambda m: (m, 0, 0))],
        out_shape=[jax.ShapeDtypeStruct(shape, F32)] * 4
        + [jax.ShapeDtypeStruct(shape, BF)] * 4
        + [jax.ShapeDtypeStruct((matrix_count, 8, size), F32)],
        scratch_shapes=[pltpu.VMEM((MAIN, count), BF)],
        compiler_params=params(40),
        cost_estimate=cost(2 * matrix_count * size * size * count, 10 * matrix_count * size * size),
        name="weight_parts",
    )(own, left, right)
    parts = (2, 2, 2, 2, matrix_count, PIECE // 2, half)
    return [v.reshape(parts) for v in outs[:4]], [v.reshape(parts) for v in outs[4:8]], outs[8]


def halving(swapped):
    order = [("rep", 2), ("tab", 1)]
    return order[::-1] if swapped else order


def sum_start(total, step, swapped):
    axis, mask = halving(swapped)[step]
    return total[0], swap(total[1].astype(BF), axis, mask)


def sum_end(kept, token):
    value = kept[0] + token
    for other in kept[1:]:
        value = value + other.astype(F32)
    return value


def far_start(total):
    sent = [
        swap(total[high, low].astype(BF), "tab", 4 * high + 2 * low)
        for high, low in ((0, 1), (1, 0), (1, 1))
    ]
    return (total[0, 0], *sent)


def far_end(kept, token):
    piece = sum_end(kept, token).astype(BF)
    for axis, known in (("rep", 2), ("tab", 3)):
        for mask in masks_of(axis)[known:]:
            piece = (piece.astype(F32) + swap(piece, axis, mask).astype(F32)).astype(BF)
    return piece


def spread_far(piece):
    return (piece, swap(piece, "tab", 2), swap(piece, "tab", 4), swap(piece, "tab", 6))


def spread_near(value, step, swapped):
    axis, mask = halving(swapped)[step]
    return value, swap(value, axis, mask)


def join(parts, token):
    one = (1.0 + token).astype(BF)
    return jnp.stack((parts[0] * one,) + tuple(parts[1:]))


def assemble_kernel(layer_count, chunk_count, own_ref, *refs):
    chunks = refs[: 2 * chunk_count]
    strip_ref, cross_ref, first_ref, second_ref = refs[2 * chunk_count :]
    matrix = pl.program_id(0)
    lanes_count = chunk_count // 2

    def fill(out_ref):
        for chunk in range(chunk_count):
            above, lane = divmod(chunk, lanes_count)
            for core in range(2):
                ref = chunks[2 * chunk + core]
                count, _, rows, lanes = ref.shape
                for at in range(count):
                    piece = (core * count + at) ^ own_ref[0]
                    first = pl.multiple_of(piece * PIECE + above * rows, rows)
                    out_ref[0, pl.ds(first, rows), lane * lanes : (lane + 1) * lanes] = ref[
                        chunk_place(at, lane == 1), 0
                    ].astype(F32)
        height, width = out_ref.shape[1:]
        if width > MAIN:
            extra = width - MAIN
            for first in range(0, MAIN, 128):
                turned = strip_ref[0, :, first : first + 128].T
                out_ref[0, first : first + 128, MAIN:] = turned[:, 3 : 3 + extra]
        if height > MAIN:
            out_ref[0, MAIN:, :] = strip_ref[0, 0 : height - MAIN, :width]

    @pl.when(matrix < layer_count)
    def _():
        fill(cross_ref)

    @pl.when(matrix == layer_count)
    def _():
        fill(first_ref)

    @pl.when(matrix == layer_count + 1)
    def _():
        fill(second_ref)


def assemble(chunks, strips, own, layer_count, width, hidden):
    matrix_count = layer_count + 2
    size = strips.shape[2]
    specs = []
    for chunk in chunks:
        specs.append(pl.BlockSpec((chunk.shape[0], 1) + chunk.shape[2:], lambda m: (0, m, 0, 0)))
    return pl.pallas_call(
        functools.partial(assemble_kernel, layer_count, len(chunks) // 2),
        grid=(matrix_count,),
        in_specs=[pl.BlockSpec(memory_space=pltpu.SMEM)]
        + specs
        + [pl.BlockSpec((1, 8, size), lambda m: (m, 0, 0))],
        out_specs=[
            pl.BlockSpec((1, width, width), lambda m: (jnp.minimum(m, layer_count - 1), 0, 0)),
            pl.BlockSpec((1, width, hidden), lambda m: (0, 0, 0)),
            pl.BlockSpec((1, hidden, hidden), lambda m: (0, 0, 0)),
        ],
        out_shape=[
            jax.ShapeDtypeStruct((layer_count, width, width), F32),
            jax.ShapeDtypeStruct((1, width, hidden), F32),
            jax.ShapeDtypeStruct((1, hidden, hidden), F32),
        ],
        compiler_params=params(56),
        cost_estimate=cost(0, 6 * matrix_count * size * size),
        name="assemble",
    )(own, *chunks, strips)


def on_device(
    ids,
    table_rows,
    table_place,
    dense_in,
    labels,
    tables,
    cross_w,
    cross_b,
    tower1_w,
    tower1_b,
    tower2_w,
    tower2_b,
    out_w,
    out_b,
):
    tab_count = lax.axis_size("tab")
    rep_count = lax.axis_size("rep")
    slot_count, embed_dim, table_len = tables.shape
    row_count, dense_width = dense_in.shape
    field_count = ids.shape[1]
    layer_count, width = cross_w.shape[:2]
    hidden = tower1_w.shape[0]
    size = round_up(width, 128)
    all_slots = slot_count * tab_count
    tab_at = lax.axis_index("tab")
    rep_at = lax.axis_index("rep")

    matches = table_place[:, None] == jnp.arange(all_slots, dtype=I32)[None, :]
    effective = ids % table_rows[None, :]
    by_slot = jnp.sum(jnp.where(matches[:, :, None], effective.T[:, None, :], 0), axis=0)
    slot_rows = jnp.sum(jnp.where(matches, table_rows[:, None], 0), axis=0)
    own_rows = lax.dynamic_slice_in_dim(slot_rows, tab_at * slot_count, slot_count)
    wanted = lax.all_to_all(
        by_slot.reshape(tab_count, slot_count, row_count), "tab", split_axis=0, concat_axis=0, tiled=True
    )
    listed = jnp.transpose(wanted, (1, 0, 2)).reshape(-1)

    starts = list(range(0, slot_count, LOOK_SLOTS))
    arrived = []
    for begin in starts:
        looked = lookup(
            tables, listed, own_rows, tab_count, begin, min(LOOK_SLOTS, slot_count - begin)
        )
        ready = 1.0 + looked[0, 0, embed_dim, 0]
        arrived.append(lax.all_to_all(looked, "tab", split_axis=0, concat_axis=0, tiled=True))

    def padded(weight):
        return jnp.pad(weight * ready, ((0, size - weight.shape[0]), (0, size - weight.shape[1])))

    weights = jnp.stack(
        [padded(cross_w[at]) for at in range(layer_count)] + [padded(tower1_w.T), padded(tower2_w)]
    )
    vectors = [cross_b[at] for at in range(layer_count)]
    vectors += [tower1_b, tower2_b, out_w[:width], out_w[width:], out_w[:0]]
    cols = jnp.stack([jnp.pad(v.astype(F32), (0, size - v.shape[0])) for v in vectors], axis=1)

    logits, dense_grad, slots, left, right, sums = dense_step(
        arrived, starts, table_place, dense_in, labels, weights, cols, out_b, layer_count, width
    )
    returned = lax.all_to_all(
        slots.reshape(tab_count, slot_count, slots.shape[1], row_count),
        "tab",
        split_axis=0,
        concat_axis=0,
        tiled=True,
    )

    share = table_len // rep_count
    base = (rep_at * share).astype(I32).reshape(1)

    def near_parts(own):
        return [own, swap(own, "rep", 1)]

    def far_parts(own):
        bases = [own]
        for mask in masks_of("rep")[1:]:
            bases = bases + [swap(part, "rep", mask) for part in bases]
        return [part for far in bases[1:] for part in near_parts(far)]

    bits = [rep_at & 1, (rep_at >> 1) & 1, tab_at & 1, (tab_at >> 2) & 1, (tab_at >> 1) & 1]
    own = sum(bit << (4 - at) for at, bit in enumerate(bits)).astype(I32).reshape(1)
    keep, send, strips = weight_parts(left, right, own)
    matrix_count = layer_count + 2
    near_ids = near_parts(wanted)
    far_ids = far_parts(wanted)
    near_grads = near_parts(returned)
    far_grads = None
    table_grad = None
    waves = [(0, 1), (2, 3)]
    token = jnp.zeros((), F32)
    state = [None] * 4
    for at in range(4):
        total = keep[at] + swap(send[at], "rep", 1).astype(F32)
        state[at] = sum_start(total, 0, at % 2 == 1)

    jobs = [(near_ids, True, slot) for slot in range(slot_count)]
    jobs += [(far_ids, False, slot) for slot in range(slot_count)]
    jobs = jobs[::-1]

    def add_next(after):
        nonlocal table_grad, token, far_grads
        if not jobs:
            return
        part_ids, near, slot = jobs.pop()
        if not near and far_grads is None:
            far_grads = far_parts(returned + token.astype(BF))
        table_grad, token = add_rows(
            near_grads if near else far_grads,
            part_ids,
            base,
            share,
            embed_dim,
            slot,
            table_grad,
            not near,
            after,
        )

    def start_far():
        nonlocal far_grads
        far_grads = far_parts(returned + token.astype(BF))

    def wave(chunks, act):
        for at in chunks:
            state[at] = act(at, state[at])

    def first_sum(at, kept):
        return sum_start(sum_end(kept, token), 1, at % 2 == 1)

    def second_sum(at, kept):
        return far_start(sum_end(kept, token))

    def last_sum(at, kept):
        return spread_far(far_end(kept, token))

    def far_join(at, parts):
        value = join(parts, token)
        return spread_near(value.reshape((2, 2) + value.shape[1:]), 1, at % 2 == 1)

    def second_join(at, parts):
        return spread_near(join(parts, token), 0, at % 2 == 1)

    def first_join(at, parts):
        value = join(parts, token)
        value = value.reshape((MAIN // PIECE // 2,) + value.shape[4:])
        return value, swap(value, "rep", 1)

    add_next([state[1][0]])
    wave(waves[0], first_sum)
    add_next([state[1][0]])
    wave(waves[1], first_sum)
    start_far()
    add_next([state[3][0]])
    wave(waves[0], second_sum)
    add_next([state[1][0]])
    wave(waves[1], second_sum)
    add_next([state[3][0]])
    wave(waves[0], last_sum)
    wave(waves[1], last_sum)
    add_next([state[3][0]])
    wave(waves[0], far_join)
    add_next([state[1][0]])
    wave(waves[1], far_join)
    add_next([state[3][0]])
    wave(waves[0], second_join)
    add_next([state[1][0]])
    wave(waves[1], second_join)
    while jobs:
        add_next([state[3][0]])
    wave(waves[0], first_join)
    wave(waves[1], first_join)
    chunks = [part for at in range(4) for part in state[at]]

    small = jnp.concatenate([strips.reshape(matrix_count * 8, size), sums], axis=0)
    for axis in ("rep", "tab"):
        for mask in masks_of(axis):
            small = small + swap(small, axis, mask)
    strips = small[:-8].reshape(matrix_count, 8, size)
    sums = small[-8:]
    cross_w_grad, tower1_w_grad, tower2_w_grad = assemble(
        chunks, strips, own, layer_count, width, hidden
    )
    scalars = sums[layer_count + 4]
    return (
        scalars[0] / (row_count * tab_count * rep_count),
        logits.reshape(row_count),
        dense_grad[:dense_width].T,
        cross_w_grad,
        sums[:layer_count, :width],
        tower1_w_grad[0].T,
        sums[layer_count, :hidden],
        tower2_w_grad[0],
        sums[layer_count + 1, :hidden],
        jnp.concatenate([sums[layer_count + 2, :width], sums[layer_count + 3, :hidden]]),
        scalars[128],
        table_grad,
    )


def solution(mesh):
    placed = (
        P(("tab", "rep"), None),
        P(),
        P(),
        P(("tab", "rep"), None),
        P(("tab", "rep")),
        P("tab", None, None),
        P(),
        P(),
        P(),
        P(),
        P(),
        P(),
        P(),
        P(),
    )
    return jax.shard_map(
        on_device,
        mesh=mesh,
        in_specs=placed,
        out_specs=(
            P(),
            P(("tab", "rep")),
            P(("tab", "rep"), None),
            P(),
            P(),
            P(),
            P(),
            P(),
            P(),
            P(),
            P(),
            P("tab", None, "rep"),
        ),
        check_vma=False,
    )
```

```python
import functools

import jax
import jax.numpy as jnp
from jax import lax
from jax.experimental import pallas as pl
from jax.experimental.pallas import tpu as pltpu
from jax.sharding import PartitionSpec as P

BF = jnp.bfloat16
F32 = jnp.float32
I32 = jnp.int32
LOOK_SLOTS = 3
LOOK_LANES = 40
LOOK_BLOCKS = 8
LOOK_ROWS = 32
ADD_LOW = 512
MAIN = 1024
CHUNK = 384
PIECE = 32
MIB = 1024 * 1024
NT = (((1,), (1,)), ((), ()))
TN = (((0,), (0,)), ((), ()))


def round_up(size, unit):
    return -(-size // unit) * unit


def params(mib):
    return pltpu.CompilerParams(vmem_limit_bytes=mib * MIB)


def cost(flops, size):
    return pl.CostEstimate(flops=flops // 1000, bytes_accessed=size // 1000, transcendentals=0)


def swap(value, axis, mask):
    return lax.ppermute(value, axis, [(at, at ^ mask) for at in range(lax.axis_size(axis))])


def masks_of(axis):
    size = lax.axis_size(axis)
    return [1 << bit for bit in range(size.bit_length() - 1)]


def lookup_kernel(first_slot, ids_ref, rows_ref, table_hbm, out_ref, raw, stack, major, picked, sems):
    tab_count, slot_count, pad_dim, count = out_ref.shape
    embed_dim = raw.shape[1]
    total = tab_count * count
    copies = [
        pltpu.make_async_copy(table_hbm.at[first_slot + at], raw.at[at], sems.at[at])
        for at in range(slot_count)
    ]
    for copy in copies:
        copy.start()
    lane = lax.broadcasted_iota(I32, (1, 128), 1)
    stack[...] = jnp.zeros_like(stack)
    most = jnp.maximum(rows_ref[first_slot], 1)
    for at in range(1, slot_count):
        most = jnp.maximum(most, rows_ref[first_slot + at])
    for copy in copies:
        copy.wait()
    unit = 128 * LOOK_BLOCKS

    @pl.loop(0, (most + unit - 1) // unit)
    def _(step):
        for block in range(LOOK_BLOCKS):
            first = pl.multiple_of((step * LOOK_BLOCKS + block) * 128, 128)
            for at in range(slot_count):
                stack[block, at * LOOK_LANES : at * LOOK_LANES + embed_dim, :] = raw[
                    at, :, pl.ds(first, 128)
                ].astype(F32)
            major[pl.ds(first, 128), :] = stack[block].T

    @pl.loop(0, total // LOOK_ROWS)
    def _(step):
        base = step * LOOK_ROWS
        starts = [(first_slot + at) * total + base for at in range(slot_count)]
        for row in range(LOOK_ROWS):
            value = None
            for at in reversed(range(slot_count)):
                one = major[pl.ds(ids_ref[starts[at] + row], 1), :]
                value = one if value is None else jnp.where(lane < (at + 1) * LOOK_LANES, one, value)
            picked[pl.ds(base + row, 1), :] = value

    @pl.loop(0, tab_count)
    def _(tab):
        for block in range(0, count, 128):
            turned = picked[pl.ds(pl.multiple_of(tab * count + block, 128), 128), :].T
            for at in range(slot_count):
                rows = turned[at * LOOK_LANES : at * LOOK_LANES + pad_dim]
                out_ref[tab, at, :, block : block + 128] = rows.astype(BF)


def lookup(tables, wanted, own_rows, tab_count, first_slot, slot_count):
    all_count, embed_dim, table_len = tables.shape
    count = wanted.shape[0] // (all_count * tab_count)
    smem = pl.BlockSpec(memory_space=pltpu.SMEM)
    return pl.pallas_call(
        functools.partial(lookup_kernel, first_slot),
        in_specs=[smem, smem, pl.BlockSpec(memory_space=pl.ANY)],
        out_specs=pl.BlockSpec(memory_space=pltpu.VMEM),
        out_shape=jax.ShapeDtypeStruct((tab_count, slot_count, round_up(embed_dim, 8), count), BF),
        scratch_shapes=[
            pltpu.VMEM((slot_count, embed_dim, table_len), BF),
            pltpu.VMEM((LOOK_BLOCKS, 128, 128), F32),
            pltpu.VMEM((table_len, 128), F32),
            pltpu.VMEM((tab_count * count, 128), F32),
            pltpu.SemaphoreType.DMA((slot_count,)),
        ],
        compiler_params=params(56),
        cost_estimate=cost(
            600 * tab_count * count * table_len * slot_count // 8,
            2 * slot_count * embed_dim * (table_len + tab_count * count),
        ),
        name="lookup",
    )(wanted, own_rows, tables)


def add_kernel(part_count, has_before, base_ref, *refs):
    ids_refs = refs[:part_count]
    grad_refs = refs[part_count : 2 * part_count]
    before_ref = refs[2 * part_count] if has_before else None
    out_ref, token_ref, total = refs[-3:]
    step = pl.program_id(0)
    embed_dim = out_ref.shape[1]
    cols = grad_refs[0].shape[3]
    high_count = total.shape[1] // embed_dim

    @pl.when(step == 0)
    def _():
        total[...] = jnp.zeros_like(total)
        token_ref[...] = jnp.zeros_like(token_ref)

    high_iota = lax.broadcasted_iota(I32, (high_count, cols), 0)
    low_iota = lax.broadcasted_iota(I32, (ADD_LOW, cols), 0)
    product = None
    for ids_ref, grad_ref in zip(ids_refs, grad_refs):
        local = ids_ref[0, 0] - base_ref[0]
        high = lax.shift_right_arithmetic(local, ADD_LOW.bit_length() - 1)
        low = local & (ADD_LOW - 1)
        high_hot = jnp.where(high_iota == high, 1.0, 0.0)
        low_hot = jnp.where(low_iota == low, 1.0, 0.0).astype(BF)
        grads = grad_ref[0, 0, :embed_dim].astype(F32)
        left = (grads[:, None, :] * high_hot[None, :, :]).astype(BF)
        left = left.reshape(embed_dim * high_count, cols)
        term = lax.dot_general(left, low_hot, NT, preferred_element_type=F32)
        product = term if product is None else product + term
    for lane in range(ADD_LOW // 128):
        total[lane] += product[:, lane * 128 : (lane + 1) * 128]

    @pl.when(step == pl.num_programs(0) - 1)
    def _():
        for at in range(high_count):
            for part in range(0, embed_dim, 8):
                size = min(8, embed_dim - part)
                for lane in range(ADD_LOW // 128):
                    first = at * ADD_LOW + lane * 128
                    value = total[lane, pl.ds(part * high_count + at, size, stride=high_count), :]
                    if before_ref is not None:
                        value = value + before_ref[0, part : part + size, first : first + 128]
                    out_ref[0, part : part + size, first : first + 128] = value


def add_rows(grads, wanted, base, share, embed_dim, slot, so_far, accumulate, after):
    tab_count, slot_count, pad_dim, count = grads[0].shape
    part_count = len(grads)
    anywhere = pl.BlockSpec(memory_space=pl.ANY)
    block = pl.BlockSpec((1, embed_dim, share), lambda t: (slot, 0, 0))
    whole = [] if so_far is None else [so_far]
    table_grad, token = pl.pallas_call(
        functools.partial(add_kernel, part_count, accumulate),
        grid=(tab_count,),
        in_specs=[pl.BlockSpec(memory_space=pltpu.SMEM)]
        + [pl.BlockSpec((1, 1, 1, count), lambda t: (t, slot, 0, 0))] * part_count
        + [pl.BlockSpec((1, 1, pad_dim, count), lambda t: (t, slot, 0, 0))] * part_count
        + [block if accumulate else anywhere] * len(whole)
        + [anywhere] * len(after),
        out_specs=[block, pl.BlockSpec((8, 128), lambda t: (0, 0))],
        scratch_shapes=[pltpu.VMEM((ADD_LOW // 128, embed_dim * (share // ADD_LOW), 128), F32)],
        out_shape=[
            jax.ShapeDtypeStruct((slot_count, embed_dim, share), F32),
            jax.ShapeDtypeStruct((8, 128), F32),
        ],
        input_output_aliases={1 + 2 * part_count: 0} if whole else {},
        compiler_params=params(40),
        cost_estimate=cost(
            2 * part_count * tab_count * count * share * embed_dim,
            2 * embed_dim * (2 * share + part_count * tab_count * count),
        ),
        name="add_rows",
    )(base, *[part[:, :, None, :] for part in wanted], *grads, *whole, *after)
    return table_grad, token[0, 0]


def row_sums(value):
    part = value[:, :128]
    for first in range(128, value.shape[1], 128):
        part = part + value[:, first : first + 128]
    return jnp.sum(part.T, axis=0, keepdims=True)


def dense_kernel(
    dense_width,
    width,
    starts,
    place_ref,
    bias_ref,
    *refs,
):
    group_count = len(starts)
    arrived_refs = refs[:group_count]
    dense_refs = refs[group_count:]
    dense_body(dense_width, width, starts, place_ref, bias_ref, arrived_refs, *dense_refs)


def dense_body(
    dense_width,
    width,
    starts,
    place_ref,
    bias_ref,
    arrived_refs,
    dense_ref,
    label_ref,
    weight_hbm,
    cols_ref,
    logits_ref,
    dense_grad_ref,
    slots_ref,
    left_ref,
    right_ref,
    sums_ref,
    weight,
    anchor,
    current,
    update,
    first_pre,
    second_pre,
    grad_anchor,
    grad_current,
    sems,
):
    layer_count = update.shape[0]
    tower1, tower2 = layer_count, layer_count + 1
    pad_dim = arrived_refs[0].shape[2]
    field_count = place_ref.shape[0]
    embed_dim = (width - dense_width) // field_count
    slot_count = sum(ref.shape[1] for ref in arrived_refs)
    size, cols = anchor.shape
    spans = [pl.ds(first, CHUNK) for first in range(0, size, CHUNK)]
    copies = [
        pltpu.make_async_copy(weight_hbm.at[at], weight.at[at], sems.at[at])
        for at in range(layer_count + 2)
    ]
    for copy in copies:
        copy.start()

    def column(at, span):
        return cols_ref[span, at : at + 1]

    def times(at, span, operand):
        return jnp.dot(weight[at, span, :], operand[...], preferred_element_type=F32)

    def transposed_times(at, span, operand):
        return lax.dot_general(weight[at, :, span], operand[...], TN, preferred_element_type=F32)

    anchor[0:16] = dense_ref[...]
    tail = width // 8 * 8
    anchor[tail:] = jnp.zeros((size - tail, cols), F32)
    for field in range(field_count):
        first = dense_width + field * embed_dim
        tab = place_ref[field] // slot_count
        slot = place_ref[field] - tab * slot_count
        value = arrived_refs[0][tab, jnp.minimum(slot, arrived_refs[0].shape[1] - 1)]
        for begin, ref in zip(starts[1:], arrived_refs[1:]):
            other = ref[tab, jnp.clip(slot - begin, 0, ref.shape[1] - 1)]
            value = jnp.where(slot >= begin, other, value)
        anchor[first : first + embed_dim] = value.astype(F32)[:embed_dim]
    for span in spans:
        left_ref[0, span] = anchor[span].astype(BF)
        left_ref[tower1, span] = anchor[span].astype(BF)
    for layer in range(layer_count):
        copies[layer].wait()
        for span in spans:
            value = transposed_times(layer, span, left_ref.at[layer]) + column(layer, span)
            update[layer, span] = value
            before = anchor if layer == 0 else current
            after = anchor[span] * value + before[span]
            current[span] = after
            if layer + 1 < layer_count:
                left_ref[layer + 1, span] = after.astype(BF)
    copies[tower1].wait()
    for span in spans:
        value = transposed_times(tower1, span, left_ref.at[0]) + column(tower1, span)
        first_pre[span] = value
        left_ref[tower2, span] = (value * jax.nn.sigmoid(value)).astype(BF)
    copies[tower2].wait()
    logits = jnp.full((1, cols), bias_ref[0], F32)
    for span in spans:
        value = transposed_times(tower2, span, left_ref.at[tower2]) + column(tower2, span)
        second_pre[span] = value
        act = value * jax.nn.sigmoid(value)
        terms = current[span] * column(layer_count + 2, span) + act * column(layer_count + 3, span)
        logits = logits + jnp.sum(terms, axis=0, keepdims=True)
    logits_ref[...] = logits
    target = label_ref[...]
    residue = jax.nn.sigmoid(logits) - target
    softplus = jnp.maximum(logits, 0.0) + jnp.log1p(jnp.exp(-jnp.abs(logits)))
    sums_ref[layer_count + 4 :, :] = jnp.zeros((sums_ref.shape[0] - layer_count - 4, size), F32)
    loss_row = jnp.sum(softplus - target * logits, axis=1, keepdims=True)
    bias_row = jnp.sum(residue, axis=1, keepdims=True)
    sums_ref[layer_count + 4 : layer_count + 5, 0:128] = jnp.broadcast_to(loss_row, (1, 128))
    sums_ref[layer_count + 4 : layer_count + 5, 128:256] = jnp.broadcast_to(bias_row, (1, 128))
    for span in spans:
        value = second_pre[span]
        sig = jax.nn.sigmoid(value)
        act = value * sig
        grad = residue * column(layer_count + 3, span) * (sig * (1.0 + value * (1.0 - sig)))
        low = grad.astype(BF)
        right_ref[tower2, span] = low
        sums_ref[tower2 : tower2 + 1, span] = row_sums(low.astype(F32))
        sums_ref[layer_count + 3 : layer_count + 4, span] = row_sums(residue * act)
        sums_ref[layer_count + 2 : layer_count + 3, span] = row_sums(residue * current[span])
        grad_current[span] = residue * column(layer_count + 2, span)
    for span in spans:
        value = first_pre[span]
        sig = jax.nn.sigmoid(value)
        grad = times(tower2, span, right_ref.at[tower2]) * (sig * (1.0 + value * (1.0 - sig)))
        low = grad.astype(BF)
        right_ref[tower1, span] = low
        sums_ref[tower1 : tower1 + 1, span] = row_sums(low.astype(F32))
    for span in spans:
        grad_anchor[span] = times(tower1, span, right_ref.at[tower1])
    for layer in reversed(range(layer_count)):
        for span in spans:
            grad = grad_current[span]
            low = (anchor[span] * grad).astype(BF)
            right_ref[layer, span] = low
            sums_ref[layer : layer + 1, span] = row_sums(low.astype(F32))
            grad_anchor[span] += grad * update[layer, span]
        for span in spans:
            grad_current[span] += times(layer, span, right_ref.at[layer])
    for span in spans:
        grad_anchor[span] += grad_current[span]
    dense_grad_ref[...] = grad_anchor[0:16]
    slots_ref[...] = jnp.zeros_like(slots_ref)
    for field in range(field_count):
        first = dense_width + field * embed_dim
        slots_ref[place_ref[field], :embed_dim] = grad_anchor[first : first + embed_dim].astype(BF)


def dense_step(arrived, starts, place, dense_in, labels, weights, cols, out_b, layer_count, width):
    tab_count, _, pad_dim, count = arrived[0].shape
    slot_count = tab_count * sum(part.shape[1] for part in arrived)
    dense_width = dense_in.shape[1]
    size = weights.shape[1]
    matrix_count = layer_count + 2
    dense_rows = jnp.pad(dense_in.T.astype(F32), ((0, 16 - dense_width), (0, 0)))
    vmem = pl.BlockSpec(memory_space=pltpu.VMEM)
    smem = pl.BlockSpec(memory_space=pltpu.SMEM)
    flat = pltpu.VMEM((size, count), F32)
    return pl.pallas_call(
        functools.partial(dense_kernel, dense_width, width, starts),
        in_specs=[smem, smem] + [vmem] * (len(arrived) + 2) + [ pl.BlockSpec(memory_space=pl.ANY), vmem],
        out_specs=[vmem] * 6,
        out_shape=[
            jax.ShapeDtypeStruct((1, count), F32),
            jax.ShapeDtypeStruct((16, count), F32),
            jax.ShapeDtypeStruct((slot_count, pad_dim, count), BF),
            jax.ShapeDtypeStruct((matrix_count, size, count), BF),
            jax.ShapeDtypeStruct((matrix_count, size, count), BF),
            jax.ShapeDtypeStruct((8, size), F32),
        ],
        scratch_shapes=[
            pltpu.VMEM(weights.shape, BF),
            flat,
            flat,
            pltpu.VMEM((layer_count, size, count), F32),
            flat,
            flat,
            flat,
            flat,
            pltpu.SemaphoreType.DMA((matrix_count,)),
        ],
        compiler_params=params(60),
        cost_estimate=cost(4 * matrix_count * size * size * count, 2 * weights.size + 30 * size * count),
        name="dense",
    )(
        place,
        out_b.astype(F32).reshape(1),
        *arrived,
        dense_rows,
        labels.astype(F32).reshape(1, count),
        weights,
        cols,
    )


def chunk_place(piece, swapped):
    if not swapped:
        return piece
    return (piece & 3) | ((piece & 4) << 1) | ((piece & 8) >> 1)


def weight_kernel(own_ref, left_ref, right_ref, keep_ref, send_ref, strip_ref, moved):
    pieces = MAIN // PIECE // 2
    half = MAIN // 2
    right = right_ref[0, :MAIN, :]
    for at in range(2 * pieces):
        first = pl.multiple_of((at ^ own_ref[0]) * PIECE, PIECE)
        moved[at * PIECE : (at + 1) * PIECE] = left_ref[0, pl.ds(first, PIECE), :]
    for core, out_ref in ((1, send_ref), (0, keep_ref)):
        product = lax.dot_general(
            moved[core * half : (core + 1) * half], right, NT, preferred_element_type=F32
        ).astype(out_ref.dtype)
        for chunk in range(2):
            for at in range(pieces):
                out_ref[chunk, chunk_place(at, chunk == 1), 0] = product[
                    at * PIECE : (at + 1) * PIECE, chunk * half : (chunk + 1) * half
                ]
    below = lax.dot_general(left_ref[0, MAIN : MAIN + 16, :], right_ref[0], NT, preferred_element_type=F32)
    beside = lax.dot_general(right_ref[0, MAIN : MAIN + 16, :], left_ref[0], NT, preferred_element_type=F32)
    strip_ref[0, 0:3] = below[0:3]
    strip_ref[0, 3:6] = beside[0:3]
    strip_ref[0, 6:8] = jnp.zeros((2, strip_ref.shape[2]), F32)


def weight_parts(left, right, own):
    matrix_count, size, count = left.shape
    half = MAIN // 2
    pieces = MAIN // PIECE // 2
    chunk = pl.BlockSpec((2, pieces, 1, PIECE, half), lambda m: (0, 0, m, 0, 0))
    shape = (2, pieces, matrix_count, PIECE, half)
    keep, send, strips = pl.pallas_call(
        weight_kernel,
        grid=(matrix_count,),
        in_specs=[
            pl.BlockSpec(memory_space=pltpu.SMEM),
            pl.BlockSpec((1, size, count), lambda m: (m, 0, 0)),
            pl.BlockSpec((1, size, count), lambda m: (m, 0, 0)),
        ],
        out_specs=[chunk, chunk, pl.BlockSpec((1, 8, size), lambda m: (m, 0, 0))],
        out_shape=[
            jax.ShapeDtypeStruct(shape, F32),
            jax.ShapeDtypeStruct(shape, BF),
            jax.ShapeDtypeStruct((matrix_count, 8, size), F32),
        ],
        scratch_shapes=[pltpu.VMEM((MAIN, count), BF)],
        compiler_params=params(40),
        cost_estimate=cost(2 * matrix_count * size * size * count, 10 * matrix_count * size * size),
        name="weight_parts",
    )(own, left, right)
    parts = (2, 2, 2, 2, 2, matrix_count, PIECE, half)
    return keep.reshape(parts), send.reshape(parts), strips


HALVES = [[("rep", 2), ("tab", 1)], [("tab", 1), ("rep", 2)]]
FAR = [(0, 1), (1, 0), (1, 1)]


def added(parts, index, token=None):
    value = parts[0][index].astype(F32)
    for other in parts[1:]:
        value = value + other[index].astype(F32)
    return value if token is None else value + token


def joined(parts, token):
    one = (1.0 + token).astype(BF)
    return jnp.concatenate([parts[0] * one] + list(parts[1:]))


def assemble_kernel(layer_count, own_ref, *refs):
    blocks = refs[:8]
    strip_ref, cross_ref, first_ref, second_ref = refs[8:]
    matrix = pl.program_id(0)

    def fill(out_ref):
        for block, ref in enumerate(blocks):
            chunk, core, upper = block >> 2, (block >> 1) & 1, block & 1
            count, _, rows, lanes = ref.shape
            for at in range(count):
                piece = 2 * count * core + chunk_place(count * upper + at, chunk == 1)
                first = pl.multiple_of((piece ^ own_ref[0]) * rows, rows)
                out_ref[0, pl.ds(first, rows), chunk * lanes : (chunk + 1) * lanes] = ref[at, 0].astype(F32)
        height, width = out_ref.shape[1:]
        if width > MAIN:
            extra = width - MAIN
            for first in range(0, MAIN, 128):
                turned = strip_ref[0, :, first : first + 128].T
                out_ref[0, first : first + 128, MAIN:] = turned[:, 3 : 3 + extra]
        if height > MAIN:
            out_ref[0, MAIN:, :] = strip_ref[0, 0 : height - MAIN, :width]

    @pl.when(matrix < layer_count)
    def _():
        fill(cross_ref)

    @pl.when(matrix == layer_count)
    def _():
        fill(first_ref)

    @pl.when(matrix == layer_count + 1)
    def _():
        fill(second_ref)


def assemble(blocks, strips, own, layer_count, width, hidden):
    matrix_count = layer_count + 2
    size = strips.shape[2]
    shape = blocks[0].shape
    block = pl.BlockSpec(shape[:1] + (1,) + shape[2:], lambda m: (0, m, 0, 0))
    return pl.pallas_call(
        functools.partial(assemble_kernel, layer_count),
        grid=(matrix_count,),
        in_specs=[pl.BlockSpec(memory_space=pltpu.SMEM)]
        + [block] * 8
        + [pl.BlockSpec((1, 8, size), lambda m: (m, 0, 0))],
        out_specs=[
            pl.BlockSpec((1, width, width), lambda m: (jnp.minimum(m, layer_count - 1), 0, 0)),
            pl.BlockSpec((1, width, hidden), lambda m: (0, 0, 0)),
            pl.BlockSpec((1, hidden, hidden), lambda m: (0, 0, 0)),
        ],
        out_shape=[
            jax.ShapeDtypeStruct((layer_count, width, width), F32),
            jax.ShapeDtypeStruct((1, width, hidden), F32),
            jax.ShapeDtypeStruct((1, hidden, hidden), F32),
        ],
        compiler_params=params(56),
        cost_estimate=cost(0, 6 * matrix_count * size * size),
        name="assemble",
    )(own, *blocks, strips)


def on_device(
    ids,
    table_rows,
    table_place,
    dense_in,
    labels,
    tables,
    cross_w,
    cross_b,
    tower1_w,
    tower1_b,
    tower2_w,
    tower2_b,
    out_w,
    out_b,
):
    tab_count = lax.axis_size("tab")
    rep_count = lax.axis_size("rep")
    slot_count, embed_dim, table_len = tables.shape
    row_count, dense_width = dense_in.shape
    field_count = ids.shape[1]
    layer_count, width = cross_w.shape[:2]
    hidden = tower1_w.shape[0]
    size = round_up(width, 128)
    all_slots = slot_count * tab_count
    tab_at = lax.axis_index("tab")
    rep_at = lax.axis_index("rep")

    matches = table_place[:, None] == jnp.arange(all_slots, dtype=I32)[None, :]
    effective = ids % table_rows[None, :]
    by_slot = jnp.sum(jnp.where(matches[:, :, None], effective.T[:, None, :], 0), axis=0)
    slot_rows = jnp.sum(jnp.where(matches, table_rows[:, None], 0), axis=0)
    own_rows = lax.dynamic_slice_in_dim(slot_rows, tab_at * slot_count, slot_count)
    wanted = lax.all_to_all(
        by_slot.reshape(tab_count, slot_count, row_count), "tab", split_axis=0, concat_axis=0, tiled=True
    )
    listed = jnp.transpose(wanted, (1, 0, 2)).reshape(-1)

    starts = list(range(0, slot_count, LOOK_SLOTS))
    arrived = []
    for begin in starts:
        looked = lookup(
            tables, listed, own_rows, tab_count, begin, min(LOOK_SLOTS, slot_count - begin)
        )
        arrived.append(lax.all_to_all(looked, "tab", split_axis=0, concat_axis=0, tiled=True))

    ready = 1.0 + arrived[0][0, 0, embed_dim, 0]

    def padded(weight):
        return jnp.pad(weight * ready, ((0, size - weight.shape[0]), (0, size - weight.shape[1])))

    weights = jnp.stack(
        [padded(cross_w[at]) for at in range(layer_count)] + [padded(tower1_w.T), padded(tower2_w)]
    )
    vectors = [cross_b[at] for at in range(layer_count)]
    vectors += [tower1_b, tower2_b, out_w[:width], out_w[width:], out_w[:0]]
    cols = jnp.stack(
        [jnp.pad((v * ready).astype(F32), (0, size - v.shape[0])) for v in vectors], axis=1
    )

    logits, dense_grad, slots, left, right, sums = dense_step(
        arrived, starts, table_place, dense_in, labels, weights, cols, out_b, layer_count, width
    )
    returned = lax.all_to_all(
        slots.reshape(tab_count, slot_count, slots.shape[1], row_count),
        "tab",
        split_axis=0,
        concat_axis=0,
        tiled=True,
    )

    share = table_len // rep_count
    base = (rep_at * share).astype(I32).reshape(1)

    def near_parts(own):
        return [own, swap(own, "rep", 1)]

    def far_bases(own):
        bases = [own]
        for mask in masks_of("rep")[1:]:
            bases = bases + [swap(part, "rep", mask) for part in bases]
        return bases[1:]

    def far_parts(bases):
        return [part for far in bases for part in near_parts(far)]

    def gate(value, result):
        return value * (1.0 + 0.0 * result.astype(F32)).astype(value.dtype)

    bits = [rep_at & 1, (rep_at >> 1) & 1, tab_at & 1, (tab_at >> 2) & 1, (tab_at >> 1) & 1]
    own = sum(bit << (4 - at) for at, bit in enumerate(bits)).astype(I32).reshape(1)
    keep, send, strips = weight_parts(left, right, own)
    matrix_count = layer_count + 2
    near_ids = near_parts(wanted)
    far_ids = far_parts(far_bases(wanted))
    far_grads = None
    table_grad = None
    token = jnp.zeros((), F32)
    jobs = [(near_ids, True, slot) for slot in range(slot_count)]
    jobs += [(far_ids, False, slot) for slot in range(slot_count)]
    jobs = jobs[::-1]

    def add_next(times, after):
        nonlocal table_grad, token
        for _ in range(min(times, len(jobs))):
            part_ids, near, slot = jobs.pop()
            table_grad, token = add_rows(
                near_grads if near else far_grads,
                part_ids,
                base,
                share,
                embed_dim,
                slot,
                table_grad,
                not near,
                after,
            )

    small = jnp.concatenate([strips.reshape(matrix_count * 8, size), sums], axis=0)
    for axis in ("rep", "tab"):
        for mask in masks_of(axis):
            small = small + swap(small, axis, mask)

    got = swap(send, "rep", 1)
    sent = [swap(added((keep, got), (at, 1)).astype(BF), *HALVES[at][0]) for at in range(2)]
    kept = [added((keep, got), (at, 0)) for at in range(2)]
    parts = [(kept[at], sent[at]) for at in range(2)]
    sent = [swap(added(parts[at], 1).astype(BF), *HALVES[at][1]) for at in range(2)]
    kept = [added(parts[at], 0) for at in range(2)]
    returned = gate(returned, kept[0][0, 0, 0, 0, 0])
    near_grads = near_parts(returned)
    add_next(1, kept + [small])
    parts = [(kept[at], sent[at]) for at in range(2)]
    sent = [
        swap(
            jnp.stack([added(part, (high, low), token) for part in parts]).astype(BF),
            "tab",
            4 * high + 2 * low,
        )
        for high, low in FAR
    ]
    kept = jnp.stack([added(part, (0, 0), token) for part in parts])
    bases = far_bases(gate(returned, kept[0, 0, 0, 0]))
    add_next(slot_count - 2, [kept])
    piece = added((kept, *sent), slice(None), token).astype(BF)
    for axis, known in (("rep", 2), ("tab", 3)):
        for mask in masks_of(axis)[known:]:
            piece = (piece.astype(F32) + swap(piece, axis, mask).astype(F32)).astype(BF)
    parts = [piece, swap(piece, "tab", 2), swap(piece, "tab", 4), swap(piece, "tab", 6)]
    far_grads = far_parts([gate(part, piece[0, 0, 0, 0]) for part in bases])
    add_next(2, [piece])
    values = [joined([part[at : at + 1] for part in parts], token) for at in range(2)]
    sent = [swap(values[at], *HALVES[at][1]) for at in range(2)]
    add_next(1, values)
    values = [joined((values[at], sent[at]), token) for at in range(2)]
    sent = [swap(values[at], *HALVES[at][0]) for at in range(2)]
    blocks = [[values[at], None, swap(values[at], "rep", 1), None] for at in range(2)]
    add_next(slot_count, values)
    for at in range(2):
        blocks[at][1] = sent[at]
        blocks[at][3] = swap(sent[at], "rep", 1)
    blocks = blocks[0] + blocks[1]

    strips = small[:-8].reshape(matrix_count, 8, size)
    sums = small[-8:]
    cross_w_grad, tower1_w_grad, tower2_w_grad = assemble(
        blocks, strips, own, layer_count, width, hidden
    )
    scalars = sums[layer_count + 4]
    return (
        scalars[0] / (row_count * tab_count * rep_count),
        logits.reshape(row_count),
        dense_grad[:dense_width].T,
        cross_w_grad,
        sums[:layer_count, :width],
        tower1_w_grad[0].T,
        sums[layer_count, :hidden],
        tower2_w_grad[0],
        sums[layer_count + 1, :hidden],
        jnp.concatenate([sums[layer_count + 2, :width], sums[layer_count + 3, :hidden]]),
        scalars[128],
        table_grad,
    )


def solution(mesh):
    placed = (
        P(("tab", "rep"), None),
        P(),
        P(),
        P(("tab", "rep"), None),
        P(("tab", "rep")),
        P("tab", None, None),
        P(),
        P(),
        P(),
        P(),
        P(),
        P(),
        P(),
        P(),
    )
    return jax.shard_map(
        on_device,
        mesh=mesh,
        in_specs=placed,
        out_specs=(
            P(),
            P(("tab", "rep")),
            P(("tab", "rep"), None),
            P(),
            P(),
            P(),
            P(),
            P(),
            P(),
            P(),
            P(),
            P("tab", None, "rep"),
        ),
        check_vma=False,
    )
```

```python
import functools

import jax
import jax.numpy as jnp
from jax import lax
from jax.experimental import pallas as pl
from jax.experimental.pallas import tpu as pltpu
from jax.sharding import PartitionSpec as P

BF = jnp.bfloat16
F32 = jnp.float32
I32 = jnp.int32
LOOK_SLOTS = 3
LOOK_LANES = 40
LOOK_BLOCKS = 8
LOOK_ROWS = 32
ADD_LOW = 512
ADD_TABS = 4
MAIN = 1024
CHUNK = 384
PIECE = 32
MIB = 1024 * 1024
NT = (((1,), (1,)), ((), ()))
TN = (((0,), (0,)), ((), ()))


def round_up(size, unit):
    return -(-size // unit) * unit


def params(mib):
    return pltpu.CompilerParams(vmem_limit_bytes=mib * MIB)


def cost(flops, size):
    return pl.CostEstimate(flops=flops // 1000, bytes_accessed=size // 1000, transcendentals=0)


def swap(value, axis, mask):
    return lax.ppermute(value, axis, [(at, at ^ mask) for at in range(lax.axis_size(axis))])


def masks_of(axis):
    size = lax.axis_size(axis)
    return [1 << bit for bit in range(size.bit_length() - 1)]


def lookup_kernel(first_slot, ids_ref, rows_ref, table_hbm, out_ref, raw, stack, major, picked, sems):
    tab_count, slot_count, pad_dim, count = out_ref.shape
    embed_dim = raw.shape[1]
    total = tab_count * count
    copies = [
        pltpu.make_async_copy(table_hbm.at[first_slot + at], raw.at[at], sems.at[at])
        for at in range(slot_count)
    ]
    for copy in copies:
        copy.start()
    lane = lax.broadcasted_iota(I32, (1, 128), 1)
    stack[...] = jnp.zeros_like(stack)
    most = jnp.maximum(rows_ref[first_slot], 1)
    for at in range(1, slot_count):
        most = jnp.maximum(most, rows_ref[first_slot + at])
    for copy in copies:
        copy.wait()
    unit = 128 * LOOK_BLOCKS

    @pl.loop(0, (most + unit - 1) // unit)
    def _(step):
        for block in range(LOOK_BLOCKS):
            first = pl.multiple_of((step * LOOK_BLOCKS + block) * 128, 128)
            for at in range(slot_count):
                stack[block, at * LOOK_LANES : at * LOOK_LANES + embed_dim, :] = raw[
                    at, :, pl.ds(first, 128)
                ].astype(F32)
            major[pl.ds(first, 128), :] = stack[block].T

    @pl.loop(0, total // LOOK_ROWS)
    def _(step):
        base = step * LOOK_ROWS
        starts = [(first_slot + at) * total + base for at in range(slot_count)]
        for row in range(LOOK_ROWS):
            value = None
            for at in reversed(range(slot_count)):
                one = major[pl.ds(ids_ref[starts[at] + row], 1), :]
                value = one if value is None else jnp.where(lane < (at + 1) * LOOK_LANES, one, value)
            picked[pl.ds(base + row, 1), :] = value

    @pl.loop(0, tab_count)
    def _(tab):
        for block in range(0, count, 128):
            turned = picked[pl.ds(pl.multiple_of(tab * count + block, 128), 128), :].T
            for at in range(slot_count):
                rows = turned[at * LOOK_LANES : at * LOOK_LANES + pad_dim]
                out_ref[tab, at, :, block : block + 128] = rows.astype(BF)


def lookup(tables, wanted, own_rows, tab_count, first_slot, slot_count):
    all_count, embed_dim, table_len = tables.shape
    count = wanted.shape[0] // (all_count * tab_count)
    smem = pl.BlockSpec(memory_space=pltpu.SMEM)
    return pl.pallas_call(
        functools.partial(lookup_kernel, first_slot),
        in_specs=[smem, smem, pl.BlockSpec(memory_space=pl.ANY)],
        out_specs=pl.BlockSpec(memory_space=pltpu.VMEM),
        out_shape=jax.ShapeDtypeStruct((tab_count, slot_count, round_up(embed_dim, 8), count), BF),
        scratch_shapes=[
            pltpu.VMEM((slot_count, embed_dim, table_len), BF),
            pltpu.VMEM((LOOK_BLOCKS, 128, 128), F32),
            pltpu.VMEM((table_len, 128), F32),
            pltpu.VMEM((tab_count * count, 128), F32),
            pltpu.SemaphoreType.DMA((slot_count,)),
        ],
        compiler_params=params(56),
        cost_estimate=cost(
            600 * tab_count * count * table_len * slot_count // 8,
            2 * slot_count * embed_dim * (table_len + tab_count * count),
        ),
        name="lookup",
    )(wanted, own_rows, tables)


def add_kernel(part_count, has_before, base_ref, *refs):
    ids_refs = refs[:part_count]
    grad_refs = refs[part_count : 2 * part_count]
    before_ref = refs[2 * part_count] if has_before else None
    out_ref, token_ref, total = refs[-3:]
    step = pl.program_id(0)
    embed_dim = out_ref.shape[1]
    cols = grad_refs[0].shape[3]
    high_count = total.shape[1] // embed_dim

    @pl.when(step == 0)
    def _():
        total[...] = jnp.zeros_like(total)
        token_ref[...] = jnp.zeros_like(token_ref)

    high_iota = lax.broadcasted_iota(I32, (high_count, cols), 0)
    low_iota = lax.broadcasted_iota(I32, (ADD_LOW, cols), 0)
    product = None
    for ids_ref, grad_ref in zip(ids_refs, grad_refs):
        for tab in range(ids_ref.shape[0]):
            local = ids_ref[tab, 0] - base_ref[0]
            high = lax.shift_right_arithmetic(local, ADD_LOW.bit_length() - 1)
            low = local & (ADD_LOW - 1)
            high_hot = jnp.where(high_iota == high, 1.0, 0.0)
            low_hot = jnp.where(low_iota == low, 1.0, 0.0).astype(BF)
            grads = grad_ref[tab, 0, :embed_dim].astype(F32)
            left = (grads[:, None, :] * high_hot[None, :, :]).astype(BF)
            left = left.reshape(embed_dim * high_count, cols)
            term = lax.dot_general(left, low_hot, NT, preferred_element_type=F32)
            product = term if product is None else product + term
    for lane in range(ADD_LOW // 128):
        total[lane] += product[:, lane * 128 : (lane + 1) * 128]

    @pl.when(step == pl.num_programs(0) - 1)
    def _():
        for at in range(high_count):
            for part in range(0, embed_dim, 8):
                size = min(8, embed_dim - part)
                for lane in range(ADD_LOW // 128):
                    first = at * ADD_LOW + lane * 128
                    value = total[lane, pl.ds(part * high_count + at, size, stride=high_count), :]
                    if before_ref is not None:
                        value = value + before_ref[0, part : part + size, first : first + 128]
                    out_ref[0, part : part + size, first : first + 128] = value


def add_rows(grads, wanted, base, share, embed_dim, slot, so_far, accumulate, after):
    tab_count, slot_count, pad_dim, count = grads[0].shape
    part_count = len(grads)
    anywhere = pl.BlockSpec(memory_space=pl.ANY)
    block = pl.BlockSpec((1, embed_dim, share), lambda t: (slot, 0, 0))
    whole = [] if so_far is None else [so_far]
    table_grad, token = pl.pallas_call(
        functools.partial(add_kernel, part_count, accumulate),
        grid=(tab_count // ADD_TABS,),
        in_specs=[pl.BlockSpec(memory_space=pltpu.SMEM)]
        + [pl.BlockSpec((ADD_TABS, 1, 1, count), lambda t: (t, slot, 0, 0))] * part_count
        + [pl.BlockSpec((ADD_TABS, 1, pad_dim, count), lambda t: (t, slot, 0, 0))] * part_count
        + [block if accumulate else anywhere] * len(whole)
        + [anywhere] * len(after),
        out_specs=[block, pl.BlockSpec((8, 128), lambda t: (0, 0))],
        scratch_shapes=[pltpu.VMEM((ADD_LOW // 128, embed_dim * (share // ADD_LOW), 128), F32)],
        out_shape=[
            jax.ShapeDtypeStruct((slot_count, embed_dim, share), F32),
            jax.ShapeDtypeStruct((8, 128), F32),
        ],
        input_output_aliases={1 + 2 * part_count: 0} if whole else {},
        compiler_params=params(40),
        cost_estimate=cost(
            2 * part_count * tab_count * count * share * embed_dim,
            2 * embed_dim * (2 * share + part_count * tab_count * count),
        ),
        name="add_rows",
    )(base, *[part[:, :, None, :] for part in wanted], *grads, *whole, *after)
    return table_grad, token[0, 0]


def row_sums(value):
    part = value[:, :128]
    for first in range(128, value.shape[1], 128):
        part = part + value[:, first : first + 128]
    return jnp.sum(part.T, axis=0, keepdims=True)


def dense_kernel(
    dense_width,
    width,
    starts,
    place_ref,
    bias_ref,
    *refs,
):
    group_count = len(starts)
    arrived_refs = refs[:group_count]
    dense_refs = refs[group_count:]
    dense_body(dense_width, width, starts, place_ref, bias_ref, arrived_refs, *dense_refs)


def dense_body(
    dense_width,
    width,
    starts,
    place_ref,
    bias_ref,
    arrived_refs,
    dense_ref,
    label_ref,
    weight_hbm,
    cols_ref,
    logits_ref,
    dense_grad_ref,
    slots_ref,
    left_ref,
    right_ref,
    sums_ref,
    weight,
    anchor,
    current,
    update,
    first_pre,
    second_pre,
    grad_anchor,
    grad_current,
    sems,
):
    layer_count = update.shape[0]
    tower1, tower2 = layer_count, layer_count + 1
    pad_dim = arrived_refs[0].shape[2]
    field_count = place_ref.shape[0]
    embed_dim = (width - dense_width) // field_count
    slot_count = sum(ref.shape[1] for ref in arrived_refs)
    size, cols = anchor.shape
    spans = [pl.ds(first, CHUNK) for first in range(0, size, CHUNK)]
    copies = [
        pltpu.make_async_copy(weight_hbm.at[at], weight.at[at], sems.at[at])
        for at in range(layer_count + 2)
    ]
    for copy in copies:
        copy.start()

    def column(at, span):
        return cols_ref[span, at : at + 1]

    def times(at, span, operand):
        return jnp.dot(weight[at, span, :], operand[...], preferred_element_type=F32)

    def transposed_times(at, span, operand):
        return lax.dot_general(weight[at, :, span], operand[...], TN, preferred_element_type=F32)

    anchor[0:16] = dense_ref[...]
    tail = width // 8 * 8
    anchor[tail:] = jnp.zeros((size - tail, cols), F32)
    for field in range(field_count):
        first = dense_width + field * embed_dim
        tab = place_ref[field] // slot_count
        slot = place_ref[field] - tab * slot_count
        value = arrived_refs[0][tab, jnp.minimum(slot, arrived_refs[0].shape[1] - 1)]
        for begin, ref in zip(starts[1:], arrived_refs[1:]):
            other = ref[tab, jnp.clip(slot - begin, 0, ref.shape[1] - 1)]
            value = jnp.where(slot >= begin, other, value)
        anchor[first : first + embed_dim] = value.astype(F32)[:embed_dim]
    for span in spans:
        left_ref[0, span] = anchor[span].astype(BF)
        left_ref[tower1, span] = anchor[span].astype(BF)
    for layer in range(layer_count):
        copies[layer].wait()
        for span in spans:
            value = transposed_times(layer, span, left_ref.at[layer]) + column(layer, span)
            update[layer, span] = value
            before = anchor if layer == 0 else current
            after = anchor[span] * value + before[span]
            current[span] = after
            if layer + 1 < layer_count:
                left_ref[layer + 1, span] = after.astype(BF)
    copies[tower1].wait()
    for span in spans:
        value = transposed_times(tower1, span, left_ref.at[0]) + column(tower1, span)
        first_pre[span] = value
        left_ref[tower2, span] = (value * jax.nn.sigmoid(value)).astype(BF)
    copies[tower2].wait()
    logits = jnp.full((1, cols), bias_ref[0], F32)
    for span in spans:
        value = transposed_times(tower2, span, left_ref.at[tower2]) + column(tower2, span)
        second_pre[span] = value
        act = value * jax.nn.sigmoid(value)
        terms = current[span] * column(layer_count + 2, span) + act * column(layer_count + 3, span)
        logits = logits + jnp.sum(terms, axis=0, keepdims=True)
    logits_ref[...] = logits
    target = label_ref[...]
    residue = jax.nn.sigmoid(logits) - target
    softplus = jnp.maximum(logits, 0.0) + jnp.log1p(jnp.exp(-jnp.abs(logits)))
    sums_ref[layer_count + 4 :, :] = jnp.zeros((sums_ref.shape[0] - layer_count - 4, size), F32)
    loss_row = jnp.sum(softplus - target * logits, axis=1, keepdims=True)
    bias_row = jnp.sum(residue, axis=1, keepdims=True)
    sums_ref[layer_count + 4 : layer_count + 5, 0:128] = jnp.broadcast_to(loss_row, (1, 128))
    sums_ref[layer_count + 4 : layer_count + 5, 128:256] = jnp.broadcast_to(bias_row, (1, 128))
    for span in spans:
        value = second_pre[span]
        sig = jax.nn.sigmoid(value)
        act = value * sig
        grad = residue * column(layer_count + 3, span) * (sig * (1.0 + value * (1.0 - sig)))
        low = grad.astype(BF)
        right_ref[tower2, span] = low
        sums_ref[tower2 : tower2 + 1, span] = row_sums(low.astype(F32))
        sums_ref[layer_count + 3 : layer_count + 4, span] = row_sums(residue * act)
        sums_ref[layer_count + 2 : layer_count + 3, span] = row_sums(residue * current[span])
        grad_current[span] = residue * column(layer_count + 2, span)
    for span in spans:
        value = first_pre[span]
        sig = jax.nn.sigmoid(value)
        grad = times(tower2, span, right_ref.at[tower2]) * (sig * (1.0 + value * (1.0 - sig)))
        low = grad.astype(BF)
        right_ref[tower1, span] = low
        sums_ref[tower1 : tower1 + 1, span] = row_sums(low.astype(F32))
    for span in spans:
        grad_anchor[span] = times(tower1, span, right_ref.at[tower1])
    for layer in reversed(range(layer_count)):
        for span in spans:
            grad = grad_current[span]
            low = (anchor[span] * grad).astype(BF)
            right_ref[layer, span] = low
            sums_ref[layer : layer + 1, span] = row_sums(low.astype(F32))
            grad_anchor[span] += grad * update[layer, span]
        for span in spans:
            grad_current[span] += times(layer, span, right_ref.at[layer])
    for span in spans:
        grad_anchor[span] += grad_current[span]
    dense_grad_ref[...] = grad_anchor[0:16]
    slots_ref[...] = jnp.zeros_like(slots_ref)
    for field in range(field_count):
        first = dense_width + field * embed_dim
        slots_ref[place_ref[field], :embed_dim] = grad_anchor[first : first + embed_dim].astype(BF)


def dense_step(arrived, starts, place, dense_in, labels, weights, cols, out_b, layer_count, width):
    tab_count, _, pad_dim, count = arrived[0].shape
    slot_count = tab_count * sum(part.shape[1] for part in arrived)
    dense_width = dense_in.shape[1]
    size = weights.shape[1]
    matrix_count = layer_count + 2
    dense_rows = jnp.pad(dense_in.T.astype(F32), ((0, 16 - dense_width), (0, 0)))
    vmem = pl.BlockSpec(memory_space=pltpu.VMEM)
    smem = pl.BlockSpec(memory_space=pltpu.SMEM)
    flat = pltpu.VMEM((size, count), F32)
    return pl.pallas_call(
        functools.partial(dense_kernel, dense_width, width, starts),
        in_specs=[smem, smem] + [vmem] * (len(arrived) + 2) + [ pl.BlockSpec(memory_space=pl.ANY), vmem],
        out_specs=[vmem] * 6,
        out_shape=[
            jax.ShapeDtypeStruct((1, count), F32),
            jax.ShapeDtypeStruct((16, count), F32),
            jax.ShapeDtypeStruct((slot_count, pad_dim, count), BF),
            jax.ShapeDtypeStruct((matrix_count, size, count), BF),
            jax.ShapeDtypeStruct((matrix_count, size, count), BF),
            jax.ShapeDtypeStruct((8, size), F32),
        ],
        scratch_shapes=[
            pltpu.VMEM(weights.shape, BF),
            flat,
            flat,
            pltpu.VMEM((layer_count, size, count), F32),
            flat,
            flat,
            flat,
            flat,
            pltpu.SemaphoreType.DMA((matrix_count,)),
        ],
        compiler_params=params(60),
        cost_estimate=cost(4 * matrix_count * size * size * count, 2 * weights.size + 30 * size * count),
        name="dense",
    )(
        place,
        out_b.astype(F32).reshape(1),
        *arrived,
        dense_rows,
        labels.astype(F32).reshape(1, count),
        weights,
        cols,
    )


def chunk_place(piece, swapped):
    if not swapped:
        return piece
    return (piece & 3) | ((piece & 4) << 1) | ((piece & 8) >> 1)


def weight_kernel(own_ref, left_ref, right_ref, keep_ref, send_ref, strip_ref, moved):
    pieces = MAIN // PIECE // 2
    half = MAIN // 2
    right = right_ref[0, :MAIN, :]
    for at in range(2 * pieces):
        first = pl.multiple_of((at ^ own_ref[0]) * PIECE, PIECE)
        moved[at * PIECE : (at + 1) * PIECE] = left_ref[0, pl.ds(first, PIECE), :]
    for core, out_ref in ((1, send_ref), (0, keep_ref)):
        product = lax.dot_general(
            moved[core * half : (core + 1) * half], right, NT, preferred_element_type=F32
        ).astype(out_ref.dtype)
        for chunk in range(2):
            for at in range(pieces):
                out_ref[chunk, chunk_place(at, chunk == 1), 0] = product[
                    at * PIECE : (at + 1) * PIECE, chunk * half : (chunk + 1) * half
                ]
    below = lax.dot_general(left_ref[0, MAIN : MAIN + 16, :], right_ref[0], NT, preferred_element_type=F32)
    beside = lax.dot_general(right_ref[0, MAIN : MAIN + 16, :], left_ref[0], NT, preferred_element_type=F32)
    strip_ref[0, 0:3] = below[0:3]
    strip_ref[0, 3:6] = beside[0:3]
    strip_ref[0, 6:8] = jnp.zeros((2, strip_ref.shape[2]), F32)


def weight_parts(left, right, own):
    matrix_count, size, count = left.shape
    half = MAIN // 2
    pieces = MAIN // PIECE // 2
    chunk = pl.BlockSpec((2, pieces, 1, PIECE, half), lambda m: (0, 0, m, 0, 0))
    shape = (2, pieces, matrix_count, PIECE, half)
    keep, send, strips = pl.pallas_call(
        weight_kernel,
        grid=(matrix_count,),
        in_specs=[
            pl.BlockSpec(memory_space=pltpu.SMEM),
            pl.BlockSpec((1, size, count), lambda m: (m, 0, 0)),
            pl.BlockSpec((1, size, count), lambda m: (m, 0, 0)),
        ],
        out_specs=[chunk, chunk, pl.BlockSpec((1, 8, size), lambda m: (m, 0, 0))],
        out_shape=[
            jax.ShapeDtypeStruct(shape, F32),
            jax.ShapeDtypeStruct(shape, BF),
            jax.ShapeDtypeStruct((matrix_count, 8, size), F32),
        ],
        scratch_shapes=[pltpu.VMEM((MAIN, count), BF)],
        compiler_params=params(40),
        cost_estimate=cost(2 * matrix_count * size * size * count, 10 * matrix_count * size * size),
        name="weight_parts",
    )(own, left, right)
    parts = (2, 2, 2, 2, 2, matrix_count, PIECE, half)
    return keep.reshape(parts), send.reshape(parts), strips


HALVES = [[("rep", 2), ("tab", 1)], [("tab", 1), ("rep", 2)]]
FAR = [(0, 1), (1, 0), (1, 1)]


def added(parts, *gates):
    value = parts[0].astype(F32)
    for other in parts[1:]:
        value = value + other.astype(F32)
    for gate in gates:
        value = value + gate
    return value


def joined(parts, token):
    one = (1.0 + token).astype(BF)
    return jnp.concatenate([parts[0] * one] + list(parts[1:]))


def assemble_kernel(layer_count, own_ref, *refs):
    blocks = refs[:8]
    strip_ref, cross_ref, first_ref, second_ref = refs[8:]
    matrix = pl.program_id(0)

    def fill(out_ref):
        for block, ref in enumerate(blocks):
            chunk, core, upper = block >> 2, (block >> 1) & 1, block & 1
            count, _, rows, lanes = ref.shape
            for at in range(count):
                piece = 2 * count * core + chunk_place(count * upper + at, chunk == 1)
                first = pl.multiple_of((piece ^ own_ref[0]) * rows, rows)
                out_ref[0, pl.ds(first, rows), chunk * lanes : (chunk + 1) * lanes] = ref[at, 0].astype(F32)
        height, width = out_ref.shape[1:]
        if width > MAIN:
            extra = width - MAIN
            for first in range(0, MAIN, 128):
                turned = strip_ref[0, :, first : first + 128].T
                out_ref[0, first : first + 128, MAIN:] = turned[:, 3 : 3 + extra]
        if height > MAIN:
            out_ref[0, MAIN:, :] = strip_ref[0, 0 : height - MAIN, :width]

    @pl.when(matrix < layer_count)
    def _():
        fill(cross_ref)

    @pl.when(matrix == layer_count)
    def _():
        fill(first_ref)

    @pl.when(matrix == layer_count + 1)
    def _():
        fill(second_ref)


def assemble(blocks, strips, own, layer_count, width, hidden):
    matrix_count = layer_count + 2
    size = strips.shape[2]
    shape = blocks[0].shape
    block = pl.BlockSpec(shape[:1] + (1,) + shape[2:], lambda m: (0, m, 0, 0))
    return pl.pallas_call(
        functools.partial(assemble_kernel, layer_count),
        grid=(matrix_count,),
        in_specs=[pl.BlockSpec(memory_space=pltpu.SMEM)]
        + [block] * 8
        + [pl.BlockSpec((1, 8, size), lambda m: (m, 0, 0))],
        out_specs=[
            pl.BlockSpec((1, width, width), lambda m: (jnp.minimum(m, layer_count - 1), 0, 0)),
            pl.BlockSpec((1, width, hidden), lambda m: (0, 0, 0)),
            pl.BlockSpec((1, hidden, hidden), lambda m: (0, 0, 0)),
        ],
        out_shape=[
            jax.ShapeDtypeStruct((layer_count, width, width), F32),
            jax.ShapeDtypeStruct((1, width, hidden), F32),
            jax.ShapeDtypeStruct((1, hidden, hidden), F32),
        ],
        compiler_params=params(56),
        cost_estimate=cost(0, 6 * matrix_count * size * size),
        name="assemble",
    )(own, *blocks, strips)


def on_device(
    ids,
    table_rows,
    table_place,
    dense_in,
    labels,
    tables,
    cross_w,
    cross_b,
    tower1_w,
    tower1_b,
    tower2_w,
    tower2_b,
    out_w,
    out_b,
):
    tab_count = lax.axis_size("tab")
    rep_count = lax.axis_size("rep")
    slot_count, embed_dim, table_len = tables.shape
    row_count, dense_width = dense_in.shape
    field_count = ids.shape[1]
    layer_count, width = cross_w.shape[:2]
    hidden = tower1_w.shape[0]
    size = round_up(width, 128)
    all_slots = slot_count * tab_count
    tab_at = lax.axis_index("tab")
    rep_at = lax.axis_index("rep")

    matches = table_place[:, None] == jnp.arange(all_slots, dtype=I32)[None, :]
    effective = ids % table_rows[None, :]
    by_slot = jnp.sum(jnp.where(matches[:, :, None], effective.T[:, None, :], 0), axis=0)
    slot_rows = jnp.sum(jnp.where(matches, table_rows[:, None], 0), axis=0)
    own_rows = lax.dynamic_slice_in_dim(slot_rows, tab_at * slot_count, slot_count)
    wanted = lax.all_to_all(
        by_slot.reshape(tab_count, slot_count, row_count), "tab", split_axis=0, concat_axis=0, tiled=True
    )
    listed = jnp.transpose(wanted, (1, 0, 2)).reshape(-1)

    first_size = slot_count % LOOK_SLOTS
    starts = ([0] if first_size else []) + list(range(first_size, slot_count, LOOK_SLOTS))
    arrived = []
    for begin in starts:
        looked = lookup(
            tables, listed, own_rows, tab_count, begin, LOOK_SLOTS if begin or not first_size else first_size
        )
        arrived.append(lax.all_to_all(looked, "tab", split_axis=0, concat_axis=0, tiled=True))

    ready = 1.0 + arrived[0][0, 0, embed_dim, 0]

    def padded(weight):
        return jnp.pad(weight * ready, ((0, size - weight.shape[0]), (0, size - weight.shape[1])))

    weights = jnp.stack(
        [padded(cross_w[at]) for at in range(layer_count)] + [padded(tower1_w.T), padded(tower2_w)]
    )
    vectors = [cross_b[at] for at in range(layer_count)]
    vectors += [tower1_b, tower2_b, out_w[:width], out_w[width:], out_w[:0]]
    cols = jnp.stack(
        [jnp.pad((v * ready).astype(F32), (0, size - v.shape[0])) for v in vectors], axis=1
    )

    logits, dense_grad, slots, left, right, sums = dense_step(
        arrived, starts, table_place, dense_in, labels, weights, cols, out_b, layer_count, width
    )
    returned = lax.all_to_all(
        slots.reshape(tab_count, slot_count, slots.shape[1], row_count),
        "tab",
        split_axis=0,
        concat_axis=0,
        tiled=True,
    )

    share = table_len // rep_count
    base = (rep_at * share).astype(I32).reshape(1)

    def near_parts(own):
        return [own, swap(own, "rep", 1)]

    def far_bases(own):
        bases = [own]
        for mask in masks_of("rep")[1:]:
            bases = bases + [swap(part, "rep", mask) for part in bases]
        return bases[1:]

    def far_parts(bases):
        return [part for far in bases for part in near_parts(far)]

    def gate(value, result):
        return value * (1.0 + 0.0 * result.astype(F32)).astype(value.dtype)

    bits = [rep_at & 1, (rep_at >> 1) & 1, tab_at & 1, (tab_at >> 2) & 1, (tab_at >> 1) & 1]
    own = sum(bit << (4 - at) for at, bit in enumerate(bits)).astype(I32).reshape(1)
    keep, send, strips = weight_parts(left, right, own)
    matrix_count = layer_count + 2
    near_ids = near_parts(wanted)
    far_ids = far_parts(far_bases(wanted))
    far_grads = None
    table_grad = None
    token = jnp.zeros((), F32)
    jobs = [(near_ids, True, slot) for slot in range(slot_count)]
    jobs += [(far_ids, False, slot) for slot in range(slot_count)]
    jobs = jobs[::-1]

    def add_next(times, after):
        nonlocal table_grad, token
        for _ in range(min(times, len(jobs))):
            part_ids, near, slot = jobs.pop()
            table_grad, token = add_rows(
                near_grads if near else far_grads,
                part_ids,
                base,
                share,
                embed_dim,
                slot,
                table_grad,
                not near,
                after,
            )

    small = jnp.concatenate([strips.reshape(matrix_count * 8, size), sums], axis=0)
    small_jobs = [(axis, mask) for axis in ("rep", "tab") for mask in masks_of(axis)]
    early = [job for job in small_jobs if job[1] < 4 and job != ("tab", 2)]
    late = [job for job in small_jobs if job not in early]

    def zero_of(value):
        return 0.0 * value.astype(F32)

    got = swap(send, "rep", 1)
    sources = [[keep[at], got[at]] for at in range(2)]

    def take(at, *index):
        whole = keep.ndim - 1
        return [part[index[whole - part.ndim :]] for part in sources[at]]

    sent = [swap(added(take(at, 1)).astype(BF), *HALVES[at][0]) for at in range(2)]
    for axis, mask in early:
        small = small + swap(small, axis, mask)
    ready = zero_of(small[0, 0])
    for at in range(2):
        sources[at].append(sent[at])
        ready = ready + zero_of(sent[at][0, 0, 0, 0, 0, 0])
    sent = [swap(added(take(at, 0, 1), ready).astype(BF), *HALVES[at][1]) for at in range(2)]
    returned = gate(returned, ready)
    near_grads = near_parts(returned)
    add_next(1, [sources[0][2]])
    for at in range(2):
        sources[at].append(sent[at])

    def take_far(high, low):
        both = [added(take(at, 0, 0, high, low), token) for at in range(2)]
        return jnp.stack(both)

    kept = take_far(0, 0)
    sends = [take_far(high, low).astype(BF) for high, low in FAR]
    far = [swap(value, "tab", 4 * high + 2 * low) for value, (high, low) in zip(sends, FAR)]
    bases = far_bases(gate(returned, sends[0][0, 0, 0, 0]))
    add_next(slot_count - 2, [kept] + sends)
    for axis, mask in late[:1]:
        small = small + swap(small, axis, mask)
    piece = added([kept, *far], token, zero_of(small[0, 0])).astype(BF)
    for axis, known in (("rep", 2), ("tab", 3)):
        for mask in masks_of(axis)[known:]:
            piece = (piece.astype(F32) + swap(piece, axis, mask).astype(F32)).astype(BF)
    parts = [piece, swap(piece, "tab", 2), swap(piece, "tab", 4), swap(piece, "tab", 6)]
    far_grads = far_parts([gate(part, piece[0, 0, 0, 0]) for part in bases])
    add_next(2, [piece])
    for axis, mask in late[1:]:
        small = small + swap(small, axis, mask)
    done = token + zero_of(small[0, 0])
    values = [joined([part[at : at + 1] for part in parts], done) for at in range(2)]
    sent = [swap(values[at], *HALVES[at][1]) for at in range(2)]
    add_next(1, values)
    values = [joined((values[at], sent[at]), token) for at in range(2)]
    sent = [swap(values[at], *HALVES[at][0]) for at in range(2)]
    blocks = [[values[at], None, swap(values[at], "rep", 1), None] for at in range(2)]
    add_next(slot_count, values)
    for at in range(2):
        blocks[at][1] = gate(sent[at], token)
        blocks[at][3] = swap(blocks[at][1], "rep", 1)
    blocks = blocks[0] + blocks[1]

    strips = small[:-8].reshape(matrix_count, 8, size)
    sums = small[-8:]
    cross_w_grad, tower1_w_grad, tower2_w_grad = assemble(
        blocks, strips, own, layer_count, width, hidden
    )
    scalars = sums[layer_count + 4]
    return (
        scalars[0] / (row_count * tab_count * rep_count),
        logits.reshape(row_count),
        dense_grad[:dense_width].T,
        cross_w_grad,
        sums[:layer_count, :width],
        tower1_w_grad[0].T,
        sums[layer_count, :hidden],
        tower2_w_grad[0],
        sums[layer_count + 1, :hidden],
        jnp.concatenate([sums[layer_count + 2, :width], sums[layer_count + 3, :hidden]]),
        scalars[128],
        table_grad,
    )


def solution(mesh):
    placed = (
        P(("tab", "rep"), None),
        P(),
        P(),
        P(("tab", "rep"), None),
        P(("tab", "rep")),
        P("tab", None, None),
        P(),
        P(),
        P(),
        P(),
        P(),
        P(),
        P(),
        P(),
    )
    return jax.shard_map(
        on_device,
        mesh=mesh,
        in_specs=placed,
        out_specs=(
            P(),
            P(("tab", "rep")),
            P(("tab", "rep"), None),
            P(),
            P(),
            P(),
            P(),
            P(),
            P(),
            P(),
            P(),
            P("tab", None, "rep"),
        ),
        check_vma=False,
    )
```

```python
import functools

import jax
import jax.numpy as jnp
from jax import lax
from jax.experimental import pallas as pl
from jax.experimental.pallas import tpu as pltpu
from jax.sharding import PartitionSpec as P

BF = jnp.bfloat16
F32 = jnp.float32
I32 = jnp.int32
LOOK_SLOTS = 3
LOOK_LANES = 40
LOOK_BLOCKS = 8
LOOK_ROWS = 32
ADD_LOW = 512
ADD_TABS = 4
MAIN = 1024
CHUNK = 384
PIECE = 32
MIB = 1024 * 1024
NT = (((1,), (1,)), ((), ()))
TN = (((0,), (0,)), ((), ()))


def round_up(size, unit):
    return -(-size // unit) * unit


def params(mib):
    return pltpu.CompilerParams(vmem_limit_bytes=mib * MIB)


def cost(flops, size):
    return pl.CostEstimate(flops=flops // 1000, bytes_accessed=size // 1000, transcendentals=0)


def swap(value, axis, mask):
    return lax.ppermute(value, axis, [(at, at ^ mask) for at in range(lax.axis_size(axis))])


def swap_both(value, rep_mask, tab_mask):
    rep_count = lax.axis_size("rep")
    perm = []
    for tab in range(lax.axis_size("tab")):
        for at in range(rep_count):
            perm.append((tab * rep_count + at, (tab ^ tab_mask) * rep_count + (at ^ rep_mask)))
    return lax.ppermute(value, ("tab", "rep"), perm)


def masks_of(axis):
    size = lax.axis_size(axis)
    return [1 << bit for bit in range(size.bit_length() - 1)]


def lookup_kernel(first_slot, ids_ref, rows_ref, table_hbm, out_ref, raw, stack, major, picked, sems):
    tab_count, slot_count, pad_dim, count = out_ref.shape
    embed_dim = raw.shape[1]
    total = tab_count * count
    copies = [
        pltpu.make_async_copy(table_hbm.at[first_slot + at], raw.at[at], sems.at[at])
        for at in range(slot_count)
    ]
    for copy in copies:
        copy.start()
    lane = lax.broadcasted_iota(I32, (1, 128), 1)
    stack[...] = jnp.zeros_like(stack)
    most = jnp.maximum(rows_ref[first_slot], 1)
    for at in range(1, slot_count):
        most = jnp.maximum(most, rows_ref[first_slot + at])
    for copy in copies:
        copy.wait()
    unit = 128 * LOOK_BLOCKS

    @pl.loop(0, (most + unit - 1) // unit)
    def _(step):
        for block in range(LOOK_BLOCKS):
            first = pl.multiple_of((step * LOOK_BLOCKS + block) * 128, 128)
            for at in range(slot_count):
                stack[block, at * LOOK_LANES : at * LOOK_LANES + embed_dim, :] = raw[
                    at, :, pl.ds(first, 128)
                ].astype(F32)
            major[pl.ds(first, 128), :] = stack[block].T

    @pl.loop(0, total // LOOK_ROWS)
    def _(step):
        base = step * LOOK_ROWS
        starts = [(first_slot + at) * total + base for at in range(slot_count)]
        for row in range(LOOK_ROWS):
            value = None
            for at in reversed(range(slot_count)):
                one = major[pl.ds(ids_ref[starts[at] + row], 1), :]
                value = one if value is None else jnp.where(lane < (at + 1) * LOOK_LANES, one, value)
            picked[pl.ds(base + row, 1), :] = value

    @pl.loop(0, tab_count)
    def _(tab):
        for block in range(0, count, 128):
            turned = picked[pl.ds(pl.multiple_of(tab * count + block, 128), 128), :].T
            for at in range(slot_count):
                rows = turned[at * LOOK_LANES : at * LOOK_LANES + pad_dim]
                out_ref[tab, at, :, block : block + 128] = rows.astype(BF)


def lookup(tables, wanted, own_rows, tab_count, first_slot, slot_count):
    all_count, embed_dim, table_len = tables.shape
    count = wanted.shape[0] // (all_count * tab_count)
    smem = pl.BlockSpec(memory_space=pltpu.SMEM)
    return pl.pallas_call(
        functools.partial(lookup_kernel, first_slot),
        in_specs=[smem, smem, pl.BlockSpec(memory_space=pl.ANY)],
        out_specs=pl.BlockSpec(memory_space=pltpu.VMEM),
        out_shape=jax.ShapeDtypeStruct((tab_count, slot_count, round_up(embed_dim, 8), count), BF),
        scratch_shapes=[
            pltpu.VMEM((slot_count, embed_dim, table_len), BF),
            pltpu.VMEM((LOOK_BLOCKS, 128, 128), F32),
            pltpu.VMEM((table_len, 128), F32),
            pltpu.VMEM((tab_count * count, 128), F32),
            pltpu.SemaphoreType.DMA((slot_count,)),
        ],
        compiler_params=params(56),
        cost_estimate=cost(
            600 * tab_count * count * table_len * slot_count // 8,
            2 * slot_count * embed_dim * (table_len + tab_count * count),
        ),
        name="lookup",
    )(wanted, own_rows, tables)


def add_kernel(part_count, has_before, base_ref, *refs):
    ids_refs = refs[:part_count]
    grad_refs = refs[part_count : 2 * part_count]
    before_ref = refs[2 * part_count] if has_before else None
    out_ref, token_ref, total = refs[-3:]
    step = pl.program_id(0)
    embed_dim = out_ref.shape[1]
    cols = grad_refs[0].shape[3]
    high_count = total.shape[1] // embed_dim

    @pl.when(step == 0)
    def _():
        total[...] = jnp.zeros_like(total)
        token_ref[...] = jnp.zeros_like(token_ref)

    high_iota = lax.broadcasted_iota(I32, (high_count, cols), 0)
    low_iota = lax.broadcasted_iota(I32, (ADD_LOW, cols), 0)
    product = None
    for ids_ref, grad_ref in zip(ids_refs, grad_refs):
        for tab in range(ids_ref.shape[0]):
            local = ids_ref[tab, 0] - base_ref[0]
            high = lax.shift_right_arithmetic(local, ADD_LOW.bit_length() - 1)
            low = local & (ADD_LOW - 1)
            high_hot = jnp.where(high_iota == high, 1.0, 0.0)
            low_hot = jnp.where(low_iota == low, 1.0, 0.0).astype(BF)
            grads = grad_ref[tab, 0, :embed_dim].astype(F32)
            left = (grads[:, None, :] * high_hot[None, :, :]).astype(BF)
            left = left.reshape(embed_dim * high_count, cols)
            term = lax.dot_general(left, low_hot, NT, preferred_element_type=F32)
            product = term if product is None else product + term
    for lane in range(ADD_LOW // 128):
        total[lane] += product[:, lane * 128 : (lane + 1) * 128]

    @pl.when(step == pl.num_programs(0) - 1)
    def _():
        for at in range(high_count):
            for part in range(0, embed_dim, 8):
                size = min(8, embed_dim - part)
                for lane in range(ADD_LOW // 128):
                    first = at * ADD_LOW + lane * 128
                    value = total[lane, pl.ds(part * high_count + at, size, stride=high_count), :]
                    if before_ref is not None:
                        value = value + before_ref[0, part : part + size, first : first + 128]
                    out_ref[0, part : part + size, first : first + 128] = value


def add_rows(grads, wanted, base, share, embed_dim, slot, so_far, accumulate, after):
    tab_count, slot_count, pad_dim, count = grads[0].shape
    part_count = len(grads)
    anywhere = pl.BlockSpec(memory_space=pl.ANY)
    block = pl.BlockSpec((1, embed_dim, share), lambda t: (slot, 0, 0))
    whole = [] if so_far is None else [so_far]
    table_grad, token = pl.pallas_call(
        functools.partial(add_kernel, part_count, accumulate),
        grid=(tab_count // ADD_TABS,),
        in_specs=[pl.BlockSpec(memory_space=pltpu.SMEM)]
        + [pl.BlockSpec((ADD_TABS, 1, 1, count), lambda t: (t, slot, 0, 0))] * part_count
        + [pl.BlockSpec((ADD_TABS, 1, pad_dim, count), lambda t: (t, slot, 0, 0))] * part_count
        + [block if accumulate else anywhere] * len(whole)
        + [anywhere] * len(after),
        out_specs=[block, pl.BlockSpec((8, 128), lambda t: (0, 0))],
        scratch_shapes=[pltpu.VMEM((ADD_LOW // 128, embed_dim * (share // ADD_LOW), 128), F32)],
        out_shape=[
            jax.ShapeDtypeStruct((slot_count, embed_dim, share), F32),
            jax.ShapeDtypeStruct((8, 128), F32),
        ],
        input_output_aliases={1 + 2 * part_count: 0} if whole else {},
        compiler_params=params(40),
        cost_estimate=cost(
            2 * part_count * tab_count * count * share * embed_dim,
            2 * embed_dim * (2 * share + part_count * tab_count * count),
        ),
        name="add_rows",
    )(base, *wanted, *grads, *whole, *after)
    return table_grad, token[0, 0]


def row_sums(value):
    part = value[:, :128]
    for first in range(128, value.shape[1], 128):
        part = part + value[:, first : first + 128]
    return jnp.sum(part.T, axis=0, keepdims=True)


def dense_kernel(
    dense_width,
    width,
    starts,
    after_count,
    place_ref,
    bias_ref,
    *refs,
):
    group_count = len(starts)
    arrived_refs = refs[:group_count]
    first = group_count + 4
    dense_refs = refs[group_count:first] + refs[first + after_count :]
    dense_body(dense_width, width, starts, place_ref, bias_ref, arrived_refs, *dense_refs)


def dense_body(
    dense_width,
    width,
    starts,
    place_ref,
    bias_ref,
    arrived_refs,
    dense_ref,
    label_ref,
    weight_hbm,
    cols_ref,
    logits_ref,
    dense_grad_ref,
    slots_ref,
    left_ref,
    right_ref,
    sums_ref,
    weight,
    anchor,
    current,
    update,
    first_pre,
    second_pre,
    grad_anchor,
    grad_current,
    sems,
):
    layer_count = update.shape[0]
    tower1, tower2 = layer_count, layer_count + 1
    pad_dim = arrived_refs[0].shape[2]
    field_count = place_ref.shape[0]
    embed_dim = (width - dense_width) // field_count
    slot_count = sum(ref.shape[1] for ref in arrived_refs)
    size, cols = anchor.shape
    spans = [pl.ds(first, CHUNK) for first in range(0, size, CHUNK)]
    copies = [
        pltpu.make_async_copy(weight_hbm.at[at], weight.at[at], sems.at[at])
        for at in range(layer_count + 2)
    ]
    for copy in copies:
        copy.start()

    def column(at, span):
        return cols_ref[span, at : at + 1]

    def times(at, span, operand):
        return jnp.dot(weight[at, span, :], operand[...], preferred_element_type=F32)

    def transposed_times(at, span, operand):
        return lax.dot_general(weight[at, :, span], operand[...], TN, preferred_element_type=F32)

    anchor[0:16] = dense_ref[...]
    tail = width // 8 * 8
    anchor[tail:] = jnp.zeros((size - tail, cols), F32)
    for field in range(field_count):
        first = dense_width + field * embed_dim
        tab = place_ref[field] // slot_count
        slot = place_ref[field] - tab * slot_count
        value = arrived_refs[0][tab, jnp.minimum(slot, arrived_refs[0].shape[1] - 1)]
        for begin, ref in zip(starts[1:], arrived_refs[1:]):
            other = ref[tab, jnp.clip(slot - begin, 0, ref.shape[1] - 1)]
            value = jnp.where(slot >= begin, other, value)
        anchor[first : first + embed_dim] = value.astype(F32)[:embed_dim]
    for span in spans:
        left_ref[0, span] = anchor[span].astype(BF)
        left_ref[tower1, span] = anchor[span].astype(BF)
    for layer in range(layer_count):
        copies[layer].wait()
        for span in spans:
            value = transposed_times(layer, span, left_ref.at[layer]) + column(layer, span)
            update[layer, span] = value
            before = anchor if layer == 0 else current
            after = anchor[span] * value + before[span]
            current[span] = after
            if layer + 1 < layer_count:
                left_ref[layer + 1, span] = after.astype(BF)
    copies[tower1].wait()
    for span in spans:
        value = transposed_times(tower1, span, left_ref.at[0]) + column(tower1, span)
        first_pre[span] = value
        left_ref[tower2, span] = (value * jax.nn.sigmoid(value)).astype(BF)
    copies[tower2].wait()
    logits = jnp.full((1, cols), bias_ref[0], F32)
    for span in spans:
        value = transposed_times(tower2, span, left_ref.at[tower2]) + column(tower2, span)
        second_pre[span] = value
        act = value * jax.nn.sigmoid(value)
        terms = current[span] * column(layer_count + 2, span) + act * column(layer_count + 3, span)
        logits = logits + jnp.sum(terms, axis=0, keepdims=True)
    logits_ref[...] = logits
    target = label_ref[...]
    residue = jax.nn.sigmoid(logits) - target
    softplus = jnp.maximum(logits, 0.0) + jnp.log1p(jnp.exp(-jnp.abs(logits)))
    sums_ref[layer_count + 4 :, :] = jnp.zeros((sums_ref.shape[0] - layer_count - 4, size), F32)
    loss_row = jnp.sum(softplus - target * logits, axis=1, keepdims=True)
    bias_row = jnp.sum(residue, axis=1, keepdims=True)
    sums_ref[layer_count + 4 : layer_count + 5, 0:128] = jnp.broadcast_to(loss_row, (1, 128))
    sums_ref[layer_count + 4 : layer_count + 5, 128:256] = jnp.broadcast_to(bias_row, (1, 128))
    for span in spans:
        value = second_pre[span]
        sig = jax.nn.sigmoid(value)
        act = value * sig
        grad = residue * column(layer_count + 3, span) * (sig * (1.0 + value * (1.0 - sig)))
        low = grad.astype(BF)
        right_ref[tower2, span] = low
        sums_ref[tower2 : tower2 + 1, span] = row_sums(low.astype(F32))
        sums_ref[layer_count + 3 : layer_count + 4, span] = row_sums(residue * act)
        sums_ref[layer_count + 2 : layer_count + 3, span] = row_sums(residue * current[span])
        grad_current[span] = residue * column(layer_count + 2, span)
    for span in spans:
        value = first_pre[span]
        sig = jax.nn.sigmoid(value)
        grad = times(tower2, span, right_ref.at[tower2]) * (sig * (1.0 + value * (1.0 - sig)))
        low = grad.astype(BF)
        right_ref[tower1, span] = low
        sums_ref[tower1 : tower1 + 1, span] = row_sums(low.astype(F32))
    for span in spans:
        grad_anchor[span] = times(tower1, span, right_ref.at[tower1])
    for layer in reversed(range(layer_count)):
        for span in spans:
            grad = grad_current[span]
            low = (anchor[span] * grad).astype(BF)
            right_ref[layer, span] = low
            sums_ref[layer : layer + 1, span] = row_sums(low.astype(F32))
            grad_anchor[span] += grad * update[layer, span]
        for span in spans:
            grad_current[span] += times(layer, span, right_ref.at[layer])
    for span in spans:
        grad_anchor[span] += grad_current[span]
    dense_grad_ref[...] = grad_anchor[0:16]
    slots_ref[...] = jnp.zeros_like(slots_ref)
    for field in range(field_count):
        first = dense_width + field * embed_dim
        slots_ref[place_ref[field], :embed_dim] = grad_anchor[first : first + embed_dim].astype(BF)


def dense_step(arrived, starts, place, dense_in, labels, weights, cols, out_b, layer_count, width, after):
    tab_count, _, pad_dim, count = arrived[0].shape
    slot_count = tab_count * sum(part.shape[1] for part in arrived)
    dense_width = dense_in.shape[1]
    size = weights.shape[1]
    matrix_count = layer_count + 2
    dense_rows = jnp.pad(dense_in.T.astype(F32), ((0, 16 - dense_width), (0, 0)))
    vmem = pl.BlockSpec(memory_space=pltpu.VMEM)
    smem = pl.BlockSpec(memory_space=pltpu.SMEM)
    flat = pltpu.VMEM((size, count), F32)
    return pl.pallas_call(
        functools.partial(dense_kernel, dense_width, width, starts, len(after)),
        in_specs=[smem, smem] + [vmem] * (len(arrived) + 2) + [ pl.BlockSpec(memory_space=pl.ANY), vmem]
        + [pl.BlockSpec(memory_space=pl.ANY)] * len(after),
        out_specs=[vmem] * 6,
        out_shape=[
            jax.ShapeDtypeStruct((1, count), F32),
            jax.ShapeDtypeStruct((16, count), F32),
            jax.ShapeDtypeStruct((slot_count, pad_dim, count), BF),
            jax.ShapeDtypeStruct((matrix_count, size, count), BF),
            jax.ShapeDtypeStruct((matrix_count, size, count), BF),
            jax.ShapeDtypeStruct((8, size), F32),
        ],
        scratch_shapes=[
            pltpu.VMEM(weights.shape, BF),
            flat,
            flat,
            pltpu.VMEM((layer_count, size, count), F32),
            flat,
            flat,
            flat,
            flat,
            pltpu.SemaphoreType.DMA((matrix_count,)),
        ],
        compiler_params=params(60),
        cost_estimate=cost(4 * matrix_count * size * size * count, 2 * weights.size + 30 * size * count),
        name="dense",
    )(
        place,
        out_b.astype(F32).reshape(1),
        *arrived,
        dense_rows,
        labels.astype(F32).reshape(1, count),
        weights,
        cols,
        *after,
    )


def chunk_place(piece, swapped):
    if not swapped:
        return piece
    return (piece & 3) | ((piece & 4) << 1) | ((piece & 8) >> 1)


def weight_kernel(own_ref, left_ref, right_ref, keep_ref, send_ref, strip_ref, moved):
    pieces = MAIN // PIECE // 2
    half = MAIN // 2
    right = right_ref[0, :MAIN, :]
    for at in range(2 * pieces):
        first = pl.multiple_of((at ^ own_ref[0]) * PIECE, PIECE)
        moved[at * PIECE : (at + 1) * PIECE] = left_ref[0, pl.ds(first, PIECE), :]
    for core, out_ref in ((1, send_ref), (0, keep_ref)):
        product = lax.dot_general(
            moved[core * half : (core + 1) * half], right, NT, preferred_element_type=F32
        ).astype(out_ref.dtype)
        for chunk in range(2):
            for at in range(pieces):
                out_ref[chunk, chunk_place(at, chunk == 1), 0] = product[
                    at * PIECE : (at + 1) * PIECE, chunk * half : (chunk + 1) * half
                ]
    below = lax.dot_general(left_ref[0, MAIN : MAIN + 16, :], right_ref[0], NT, preferred_element_type=F32)
    beside = lax.dot_general(right_ref[0, MAIN : MAIN + 16, :], left_ref[0], NT, preferred_element_type=F32)
    strip_ref[0, 0:3] = below[0:3]
    strip_ref[0, 3:6] = beside[0:3]
    strip_ref[0, 6:8] = jnp.zeros((2, strip_ref.shape[2]), F32)


def weight_parts(left, right, own):
    matrix_count, size, count = left.shape
    half = MAIN // 2
    pieces = MAIN // PIECE // 2
    chunk = pl.BlockSpec((2, pieces, 1, PIECE, half), lambda m: (0, 0, m, 0, 0))
    shape = (2, pieces, matrix_count, PIECE, half)
    keep, send, strips = pl.pallas_call(
        weight_kernel,
        grid=(matrix_count,),
        in_specs=[
            pl.BlockSpec(memory_space=pltpu.SMEM),
            pl.BlockSpec((1, size, count), lambda m: (m, 0, 0)),
            pl.BlockSpec((1, size, count), lambda m: (m, 0, 0)),
        ],
        out_specs=[chunk, chunk, pl.BlockSpec((1, 8, size), lambda m: (m, 0, 0))],
        out_shape=[
            jax.ShapeDtypeStruct(shape, F32),
            jax.ShapeDtypeStruct(shape, BF),
            jax.ShapeDtypeStruct((matrix_count, 8, size), F32),
        ],
        scratch_shapes=[pltpu.VMEM((MAIN, count), BF)],
        compiler_params=params(40),
        cost_estimate=cost(2 * matrix_count * size * size * count, 10 * matrix_count * size * size),
        name="weight_parts",
    )(own, left, right)
    parts = (2, 2, 2, 2, 2, matrix_count, PIECE, half)
    return keep.reshape(parts), send.reshape(parts), strips


HALVES = [[("rep", 2), ("tab", 1)], [("tab", 1), ("rep", 2)]]
FAR = [(0, 1), (1, 0), (1, 1)]


def added(parts, *gates):
    value = parts[0].astype(F32)
    for other in parts[1:]:
        value = value + other.astype(F32)
    for gate in gates:
        value = value + gate
    return value


def joined(parts, token):
    one = (1.0 + token).astype(BF)
    return jnp.concatenate([parts[0] * one] + list(parts[1:]))


def assemble_kernel(layer_count, own_ref, *refs):
    blocks = refs[:8]
    strip_ref, cross_ref, first_ref, second_ref = refs[8:]
    matrix = pl.program_id(0)

    def fill(out_ref):
        for block, ref in enumerate(blocks):
            chunk, core, upper = block >> 2, (block >> 1) & 1, block & 1
            count, _, rows, lanes = ref.shape
            for at in range(count):
                piece = 2 * count * core + chunk_place(count * upper + at, chunk == 1)
                first = pl.multiple_of((piece ^ own_ref[0]) * rows, rows)
                out_ref[0, pl.ds(first, rows), chunk * lanes : (chunk + 1) * lanes] = ref[at, 0].astype(F32)
        height, width = out_ref.shape[1:]
        if width > MAIN:
            extra = width - MAIN
            for first in range(0, MAIN, 128):
                turned = strip_ref[0, :, first : first + 128].T
                out_ref[0, first : first + 128, MAIN:] = turned[:, 3 : 3 + extra]
        if height > MAIN:
            out_ref[0, MAIN:, :] = strip_ref[0, 0 : height - MAIN, :width]

    @pl.when(matrix < layer_count)
    def _():
        fill(cross_ref)

    @pl.when(matrix == layer_count)
    def _():
        fill(first_ref)

    @pl.when(matrix == layer_count + 1)
    def _():
        fill(second_ref)


def assemble(blocks, strips, own, layer_count, width, hidden):
    matrix_count = layer_count + 2
    size = strips.shape[2]
    shape = blocks[0].shape
    block = pl.BlockSpec(shape[:1] + (1,) + shape[2:], lambda m: (0, m, 0, 0))
    return pl.pallas_call(
        functools.partial(assemble_kernel, layer_count),
        grid=(matrix_count,),
        in_specs=[pl.BlockSpec(memory_space=pltpu.SMEM)]
        + [block] * 8
        + [pl.BlockSpec((1, 8, size), lambda m: (m, 0, 0))],
        out_specs=[
            pl.BlockSpec((1, width, width), lambda m: (jnp.minimum(m, layer_count - 1), 0, 0)),
            pl.BlockSpec((1, width, hidden), lambda m: (0, 0, 0)),
            pl.BlockSpec((1, hidden, hidden), lambda m: (0, 0, 0)),
        ],
        out_shape=[
            jax.ShapeDtypeStruct((layer_count, width, width), F32),
            jax.ShapeDtypeStruct((1, width, hidden), F32),
            jax.ShapeDtypeStruct((1, hidden, hidden), F32),
        ],
        compiler_params=params(56),
        cost_estimate=cost(0, 6 * matrix_count * size * size),
        name="assemble",
    )(own, *blocks, strips)


def on_device(
    ids,
    table_rows,
    table_place,
    dense_in,
    labels,
    tables,
    cross_w,
    cross_b,
    tower1_w,
    tower1_b,
    tower2_w,
    tower2_b,
    out_w,
    out_b,
):
    tab_count = lax.axis_size("tab")
    rep_count = lax.axis_size("rep")
    slot_count, embed_dim, table_len = tables.shape
    row_count, dense_width = dense_in.shape
    field_count = ids.shape[1]
    layer_count, width = cross_w.shape[:2]
    hidden = tower1_w.shape[0]
    size = round_up(width, 128)
    all_slots = slot_count * tab_count
    tab_at = lax.axis_index("tab")
    rep_at = lax.axis_index("rep")

    matches = table_place[:, None] == jnp.arange(all_slots, dtype=I32)[None, :]
    effective = ids % table_rows[None, :]
    by_slot = jnp.sum(jnp.where(matches[:, :, None], effective.T[:, None, :], 0), axis=0)
    slot_rows = jnp.sum(jnp.where(matches, table_rows[:, None], 0), axis=0)
    own_rows = lax.dynamic_slice_in_dim(slot_rows, tab_at * slot_count, slot_count)
    wanted = lax.all_to_all(
        by_slot.reshape(tab_count, slot_count, row_count), "tab", split_axis=0, concat_axis=0, tiled=True
    )
    listed = jnp.transpose(wanted, (1, 0, 2)).reshape(-1)

    first_size = slot_count % LOOK_SLOTS
    starts = ([0] if first_size else []) + list(range(first_size, slot_count, LOOK_SLOTS))
    arrived = []
    for begin in starts:
        looked = lookup(
            tables, listed, own_rows, tab_count, begin, LOOK_SLOTS if begin or not first_size else first_size
        )
        arrived.append(lax.all_to_all(looked, "tab", split_axis=0, concat_axis=0, tiled=True))

    ready = 1.0 + arrived[0][0, 0, embed_dim, 0]

    def padded(weight):
        return jnp.pad(weight * ready, ((0, size - weight.shape[0]), (0, size - weight.shape[1])))

    weights = jnp.stack(
        [padded(cross_w[at]) for at in range(layer_count)] + [padded(tower1_w.T), padded(tower2_w)]
    )
    vectors = [cross_b[at] for at in range(layer_count)]
    vectors += [tower1_b, tower2_b, out_w[:width], out_w[width:], out_w[:0]]
    cols = jnp.stack(
        [jnp.pad((v * ready).astype(F32), (0, size - v.shape[0])) for v in vectors], axis=1
    )


    def near_parts(own):
        return [own, swap(own, "rep", 1)]

    def far_bases(own):
        bases = [own]
        for mask in masks_of("rep")[1:]:
            bases = bases + [swap(part, "rep", mask) for part in bases]
        return bases[1:]

    def far_parts(bases):
        return [part for far in bases for part in near_parts(far)]

    near_ids = [part[:, :, None, :] for part in near_parts(wanted)]
    far_ids = [part[:, :, None, :] for part in far_parts(far_bases(wanted))]
    logits, dense_grad, slots, left, right, sums = dense_step(
        arrived, starts, table_place, dense_in, labels, weights, cols, out_b, layer_count, width,
        near_ids + far_ids,
    )
    returned = lax.all_to_all(
        slots.reshape(tab_count, slot_count, slots.shape[1], row_count),
        "tab",
        split_axis=0,
        concat_axis=0,
        tiled=True,
    )

    share = table_len // rep_count
    base = (rep_at * share).astype(I32).reshape(1)

    def gate(value, result):
        return value * (1.0 + 0.0 * result.astype(F32)).astype(value.dtype)

    bits = [rep_at & 1, (rep_at >> 1) & 1, tab_at & 1, (tab_at >> 2) & 1, (tab_at >> 1) & 1]
    own = sum(bit << (4 - at) for at, bit in enumerate(bits)).astype(I32).reshape(1)
    keep, send, strips = weight_parts(left, right, own)
    matrix_count = layer_count + 2
    far_grads = None
    table_grad = None
    token = jnp.zeros((), F32)
    jobs = [(near_ids, True, slot) for slot in range(slot_count)]
    jobs += [(far_ids, False, slot) for slot in range(slot_count)]
    jobs = jobs[::-1]

    def add_next(times, after):
        nonlocal table_grad, token
        for _ in range(min(times, len(jobs))):
            part_ids, near, slot = jobs.pop()
            table_grad, token = add_rows(
                near_grads if near else far_grads,
                part_ids,
                base,
                share,
                embed_dim,
                slot,
                table_grad,
                not near,
                after,
            )

    small = jnp.concatenate([strips.reshape(matrix_count * 8, size), sums], axis=0)
    def zero_of(value):
        return 0.0 * value.astype(F32)

    got = swap(send, "rep", 1)
    small = small + swap(small, "rep", 1)
    sends = [added((keep[at, 1], got[at, 1])).astype(BF) for at in range(2)]
    sent = [swap(sends[at], *HALVES[at][0]) for at in range(2)]
    keep, got, sends = lax.optimization_barrier((keep, got, sends))
    kept = [added((keep[at, 0], got[at, 0])) for at in range(2)]
    for part in kept:
        small = small + zero_of(part[0, 0, 0, 0, 0, 0])
    small = added([small, swap(small, "rep", 2), swap(small, "tab", 1), swap_both(small, 2, 1)])
    sources = [[kept[at], sent[at]] for at in range(2)]
    ready = zero_of(small[0, 0])
    for part in kept + sent:
        ready = ready + zero_of(part[0, 0, 0, 0, 0, 0])

    def take(at, *index):
        whole = keep.ndim - 2
        return [part[index[whole - part.ndim :]] for part in sources[at]]

    sent = [swap(added(take(at, 1), ready).astype(BF), *HALVES[at][1]) for at in range(2)]
    returned = gate(returned, ready)
    near_grads = near_parts(returned)
    add_next(1, [sources[0][1]])
    for at in range(2):
        sources[at].append(sent[at])

    def take_far(high, low):
        both = [added(take(at, 0, high, low), token) for at in range(2)]
        return jnp.stack(both)

    kept = take_far(0, 0)
    sends = [take_far(high, low).astype(BF) for high, low in FAR]
    far = [swap(value, "tab", 4 * high + 2 * low) for value, (high, low) in zip(sends, FAR)]
    bases = far_bases(gate(returned, sends[0][0, 0, 0, 0]))
    add_next(slot_count - 2, [kept] + sends)
    small = added([small] + [swap(small, "tab", mask) for mask in (2, 4, 6)])
    for axis, known in (("rep", 2), ("tab", 3)):
        for mask in masks_of(axis)[known:]:
            small = small + swap(small, axis, mask)
    piece = added([kept, *far], token, zero_of(small[0, 0])).astype(BF)
    for axis, known in (("rep", 2), ("tab", 3)):
        for mask in masks_of(axis)[known:]:
            piece = (piece.astype(F32) + swap(piece, axis, mask).astype(F32)).astype(BF)
    parts = [piece, swap(piece, "tab", 2), swap(piece, "tab", 4), swap(piece, "tab", 6)]
    far_grads = far_parts([gate(part, piece[0, 0, 0, 0]) for part in bases])
    add_next(2, [piece])
    values = [joined([part[at : at + 1] for part in parts], token) for at in range(2)]
    sent = [swap(values[at], *HALVES[at][1]) for at in range(2)]
    add_next(1, values)
    values = [joined((values[at], sent[at]), token) for at in range(2)]
    sent = [swap(values[at], *HALVES[at][0]) for at in range(2)]
    blocks = [[values[at], None, swap(values[at], "rep", 1), None] for at in range(2)]
    add_next(slot_count, values)
    for at in range(2):
        blocks[at][1] = gate(sent[at], token)
        blocks[at][3] = swap(blocks[at][1], "rep", 1)
    blocks = blocks[0] + blocks[1]

    strips = small[:-8].reshape(matrix_count, 8, size)
    sums = small[-8:]
    cross_w_grad, tower1_w_grad, tower2_w_grad = assemble(
        blocks, strips, own, layer_count, width, hidden
    )
    scalars = sums[layer_count + 4]
    return (
        scalars[0] / (row_count * tab_count * rep_count),
        logits.reshape(row_count),
        dense_grad[:dense_width].T,
        cross_w_grad,
        sums[:layer_count, :width],
        tower1_w_grad[0].T,
        sums[layer_count, :hidden],
        tower2_w_grad[0],
        sums[layer_count + 1, :hidden],
        jnp.concatenate([sums[layer_count + 2, :width], sums[layer_count + 3, :hidden]]),
        scalars[128],
        table_grad,
    )


def solution(mesh):
    placed = (
        P(("tab", "rep"), None),
        P(),
        P(),
        P(("tab", "rep"), None),
        P(("tab", "rep")),
        P("tab", None, None),
        P(),
        P(),
        P(),
        P(),
        P(),
        P(),
        P(),
        P(),
    )
    return jax.shard_map(
        on_device,
        mesh=mesh,
        in_specs=placed,
        out_specs=(
            P(),
            P(("tab", "rep")),
            P(("tab", "rep"), None),
            P(),
            P(),
            P(),
            P(),
            P(),
            P(),
            P(),
            P(),
            P("tab", None, "rep"),
        ),
        check_vma=False,
    )
```

```python
import functools

import jax
import jax.numpy as jnp
from jax import lax
from jax.experimental import pallas as pl
from jax.experimental.pallas import tpu as pltpu
from jax.sharding import PartitionSpec as P

BF = jnp.bfloat16
F32 = jnp.float32
I32 = jnp.int32
LOOK_SLOTS = 3
LOOK_LANES = 40
LOOK_BLOCKS = 8
LOOK_ROWS = 32
ADD_LOW = 512
ADD_TABS = 4
NEAR_FIRST = 3
MAIN = 1024
CHUNK = 384
PIECE = 32
MIB = 1024 * 1024
NT = (((1,), (1,)), ((), ()))
TN = (((0,), (0,)), ((), ()))


def round_up(size, unit):
    return -(-size // unit) * unit


def params(mib):
    return pltpu.CompilerParams(vmem_limit_bytes=mib * MIB)


def cost(flops, size):
    return pl.CostEstimate(flops=flops // 1000, bytes_accessed=size // 1000, transcendentals=0)


def swap(value, axis, mask):
    return lax.ppermute(value, axis, [(at, at ^ mask) for at in range(lax.axis_size(axis))])


def swap_both(value, rep_mask, tab_mask):
    rep_count = lax.axis_size("rep")
    perm = []
    for tab in range(lax.axis_size("tab")):
        for at in range(rep_count):
            perm.append((tab * rep_count + at, (tab ^ tab_mask) * rep_count + (at ^ rep_mask)))
    return lax.ppermute(value, ("tab", "rep"), perm)


def masks_of(axis):
    size = lax.axis_size(axis)
    return [1 << bit for bit in range(size.bit_length() - 1)]


def lookup_kernel(first_slot, ids_ref, rows_ref, table_hbm, out_ref, raw, stack, major, picked, sems):
    tab_count, slot_count, pad_dim, count = out_ref.shape
    embed_dim = raw.shape[1]
    total = tab_count * count
    copies = [
        pltpu.make_async_copy(table_hbm.at[first_slot + at], raw.at[at], sems.at[at])
        for at in range(slot_count)
    ]
    for copy in copies:
        copy.start()
    lane = lax.broadcasted_iota(I32, (1, 128), 1)
    stack[...] = jnp.zeros_like(stack)
    most = jnp.maximum(rows_ref[first_slot], 1)
    for at in range(1, slot_count):
        most = jnp.maximum(most, rows_ref[first_slot + at])
    for copy in copies:
        copy.wait()
    unit = 128 * LOOK_BLOCKS

    @pl.loop(0, (most + unit - 1) // unit)
    def _(step):
        for block in range(LOOK_BLOCKS):
            first = pl.multiple_of((step * LOOK_BLOCKS + block) * 128, 128)
            for at in range(slot_count):
                stack[block, at * LOOK_LANES : at * LOOK_LANES + embed_dim, :] = raw[
                    at, :, pl.ds(first, 128)
                ].astype(F32)
            major[pl.ds(first, 128), :] = stack[block].T

    @pl.loop(0, total // LOOK_ROWS)
    def _(step):
        base = step * LOOK_ROWS
        starts = [(first_slot + at) * total + base for at in range(slot_count)]
        for row in range(LOOK_ROWS):
            value = None
            for at in reversed(range(slot_count)):
                one = major[pl.ds(ids_ref[starts[at] + row], 1), :]
                value = one if value is None else jnp.where(lane < (at + 1) * LOOK_LANES, one, value)
            picked[pl.ds(base + row, 1), :] = value

    @pl.loop(0, tab_count)
    def _(tab):
        for block in range(0, count, 128):
            turned = picked[pl.ds(pl.multiple_of(tab * count + block, 128), 128), :].T
            for at in range(slot_count):
                rows = turned[at * LOOK_LANES : at * LOOK_LANES + pad_dim]
                out_ref[tab, at, :, block : block + 128] = rows.astype(BF)


def lookup(tables, wanted, own_rows, tab_count, first_slot, slot_count):
    all_count, embed_dim, table_len = tables.shape
    count = wanted.shape[0] // (all_count * tab_count)
    smem = pl.BlockSpec(memory_space=pltpu.SMEM)
    return pl.pallas_call(
        functools.partial(lookup_kernel, first_slot),
        in_specs=[smem, smem, pl.BlockSpec(memory_space=pl.ANY)],
        out_specs=pl.BlockSpec(memory_space=pltpu.VMEM),
        out_shape=jax.ShapeDtypeStruct((tab_count, slot_count, round_up(embed_dim, 8), count), BF),
        scratch_shapes=[
            pltpu.VMEM((slot_count, embed_dim, table_len), BF),
            pltpu.VMEM((LOOK_BLOCKS, 128, 128), F32),
            pltpu.VMEM((table_len, 128), F32),
            pltpu.VMEM((tab_count * count, 128), F32),
            pltpu.SemaphoreType.DMA((slot_count,)),
        ],
        compiler_params=params(56),
        cost_estimate=cost(
            600 * tab_count * count * table_len * slot_count // 8,
            2 * slot_count * embed_dim * (table_len + tab_count * count),
        ),
        name="lookup",
    )(wanted, own_rows, tables)


def add_kernel(part_count, has_before, base_ref, *refs):
    ids_refs = refs[:part_count]
    grad_refs = refs[part_count : 2 * part_count]
    before_ref = refs[2 * part_count] if has_before else None
    out_ref, token_ref, total = refs[-3:]
    step = pl.program_id(0)
    embed_dim = out_ref.shape[1]
    cols = grad_refs[0].shape[3]
    high_count = total.shape[1] // embed_dim

    @pl.when(step == 0)
    def _():
        total[...] = jnp.zeros_like(total)
        token_ref[...] = jnp.zeros_like(token_ref)

    high_iota = lax.broadcasted_iota(I32, (high_count, cols), 0)
    low_iota = lax.broadcasted_iota(I32, (ADD_LOW, cols), 0)
    product = None
    for ids_ref, grad_ref in zip(ids_refs, grad_refs):
        for tab in range(ids_ref.shape[0]):
            local = ids_ref[tab, 0] - base_ref[0]
            high = lax.shift_right_arithmetic(local, ADD_LOW.bit_length() - 1)
            low = local & (ADD_LOW - 1)
            high_hot = jnp.where(high_iota == high, 1.0, 0.0)
            low_hot = jnp.where(low_iota == low, 1.0, 0.0).astype(BF)
            grads = grad_ref[tab, 0, :embed_dim].astype(F32)
            left = (grads[:, None, :] * high_hot[None, :, :]).astype(BF)
            left = left.reshape(embed_dim * high_count, cols)
            term = lax.dot_general(left, low_hot, NT, preferred_element_type=F32)
            product = term if product is None else product + term
    for lane in range(ADD_LOW // 128):
        total[lane] += product[:, lane * 128 : (lane + 1) * 128]

    @pl.when(step == pl.num_programs(0) - 1)
    def _():
        for at in range(high_count):
            for part in range(0, embed_dim, 8):
                size = min(8, embed_dim - part)
                for lane in range(ADD_LOW // 128):
                    first = at * ADD_LOW + lane * 128
                    value = total[lane, pl.ds(part * high_count + at, size, stride=high_count), :]
                    if before_ref is not None:
                        value = value + before_ref[0, part : part + size, first : first + 128]
                    out_ref[0, part : part + size, first : first + 128] = value


def add_rows(grads, wanted, base, share, embed_dim, slot, so_far, accumulate, after):
    tab_count, slot_count, pad_dim, count = grads[0].shape
    part_count = len(grads)
    anywhere = pl.BlockSpec(memory_space=pl.ANY)
    block = pl.BlockSpec((1, embed_dim, share), lambda t: (slot, 0, 0))
    whole = [] if so_far is None else [so_far]
    table_grad, token = pl.pallas_call(
        functools.partial(add_kernel, part_count, accumulate),
        grid=(tab_count // ADD_TABS,),
        in_specs=[pl.BlockSpec(memory_space=pltpu.SMEM)]
        + [pl.BlockSpec((ADD_TABS, 1, 1, count), lambda t: (t, slot, 0, 0))] * part_count
        + [pl.BlockSpec((ADD_TABS, 1, pad_dim, count), lambda t: (t, slot, 0, 0))] * part_count
        + [block if accumulate else anywhere] * len(whole)
        + [anywhere] * len(after),
        out_specs=[block, pl.BlockSpec((8, 128), lambda t: (0, 0))],
        scratch_shapes=[pltpu.VMEM((ADD_LOW // 128, embed_dim * (share // ADD_LOW), 128), F32)],
        out_shape=[
            jax.ShapeDtypeStruct((slot_count, embed_dim, share), F32),
            jax.ShapeDtypeStruct((8, 128), F32),
        ],
        input_output_aliases={1 + 2 * part_count: 0} if whole else {},
        compiler_params=params(40),
        cost_estimate=cost(
            2 * part_count * tab_count * count * share * embed_dim,
            2 * embed_dim * (2 * share + part_count * tab_count * count),
        ),
        name="add_rows",
    )(base, *wanted, *grads, *whole, *after)
    return table_grad, token[0, 0]


def row_sums(value):
    part = value[:, :128]
    for first in range(128, value.shape[1], 128):
        part = part + value[:, first : first + 128]
    return jnp.sum(part.T, axis=0, keepdims=True)


def dense_kernel(
    dense_width,
    width,
    starts,
    after_count,
    place_ref,
    bias_ref,
    *refs,
):
    group_count = len(starts)
    arrived_refs = refs[:group_count]
    first = group_count + 4
    dense_refs = refs[group_count:first] + refs[first + after_count :]
    dense_body(dense_width, width, starts, place_ref, bias_ref, arrived_refs, *dense_refs)


def dense_body(
    dense_width,
    width,
    starts,
    place_ref,
    bias_ref,
    arrived_refs,
    dense_ref,
    label_ref,
    weight_hbm,
    cols_ref,
    logits_ref,
    dense_grad_ref,
    slots_ref,
    left_ref,
    right_ref,
    sums_ref,
    weight,
    anchor,
    current,
    update,
    first_pre,
    second_pre,
    grad_anchor,
    grad_current,
    sems,
):
    layer_count = update.shape[0]
    tower1, tower2 = layer_count, layer_count + 1
    pad_dim = arrived_refs[0].shape[2]
    field_count = place_ref.shape[0]
    embed_dim = (width - dense_width) // field_count
    slot_count = sum(ref.shape[1] for ref in arrived_refs)
    size, cols = anchor.shape
    spans = [pl.ds(first, CHUNK) for first in range(0, size, CHUNK)]
    copies = [
        pltpu.make_async_copy(weight_hbm.at[at], weight.at[at], sems.at[at])
        for at in range(layer_count + 2)
    ]
    for copy in copies:
        copy.start()

    def column(at, span):
        return cols_ref[span, at : at + 1]

    def times(at, span, operand):
        return jnp.dot(weight[at, span, :], operand[...], preferred_element_type=F32)

    def transposed_times(at, span, operand):
        return lax.dot_general(weight[at, :, span], operand[...], TN, preferred_element_type=F32)

    anchor[0:16] = dense_ref[...]
    tail = width // 8 * 8
    anchor[tail:] = jnp.zeros((size - tail, cols), F32)
    for field in range(field_count):
        first = dense_width + field * embed_dim
        tab = place_ref[field] // slot_count
        slot = place_ref[field] - tab * slot_count
        value = arrived_refs[0][tab, jnp.minimum(slot, arrived_refs[0].shape[1] - 1)]
        for begin, ref in zip(starts[1:], arrived_refs[1:]):
            other = ref[tab, jnp.clip(slot - begin, 0, ref.shape[1] - 1)]
            value = jnp.where(slot >= begin, other, value)
        anchor[first : first + embed_dim] = value.astype(F32)[:embed_dim]
    for span in spans:
        left_ref[0, span] = anchor[span].astype(BF)
        left_ref[tower1, span] = anchor[span].astype(BF)
    for layer in range(layer_count):
        copies[layer].wait()
        for span in spans:
            value = transposed_times(layer, span, left_ref.at[layer]) + column(layer, span)
            update[layer, span] = value
            before = anchor if layer == 0 else current
            after = anchor[span] * value + before[span]
            current[span] = after
            if layer + 1 < layer_count:
                left_ref[layer + 1, span] = after.astype(BF)
    copies[tower1].wait()
    for span in spans:
        value = transposed_times(tower1, span, left_ref.at[0]) + column(tower1, span)
        first_pre[span] = value
        left_ref[tower2, span] = (value * jax.nn.sigmoid(value)).astype(BF)
    copies[tower2].wait()
    logits = jnp.full((1, cols), bias_ref[0], F32)
    for span in spans:
        value = transposed_times(tower2, span, left_ref.at[tower2]) + column(tower2, span)
        second_pre[span] = value
        act = value * jax.nn.sigmoid(value)
        terms = current[span] * column(layer_count + 2, span) + act * column(layer_count + 3, span)
        logits = logits + jnp.sum(terms, axis=0, keepdims=True)
    logits_ref[...] = logits
    target = label_ref[...]
    residue = jax.nn.sigmoid(logits) - target
    softplus = jnp.maximum(logits, 0.0) + jnp.log1p(jnp.exp(-jnp.abs(logits)))
    sums_ref[layer_count + 4 :, :] = jnp.zeros((sums_ref.shape[0] - layer_count - 4, size), F32)
    loss_row = jnp.sum(softplus - target * logits, axis=1, keepdims=True)
    bias_row = jnp.sum(residue, axis=1, keepdims=True)
    sums_ref[layer_count + 4 : layer_count + 5, 0:128] = jnp.broadcast_to(loss_row, (1, 128))
    sums_ref[layer_count + 4 : layer_count + 5, 128:256] = jnp.broadcast_to(bias_row, (1, 128))
    for span in spans:
        value = second_pre[span]
        sig = jax.nn.sigmoid(value)
        act = value * sig
        grad = residue * column(layer_count + 3, span) * (sig * (1.0 + value * (1.0 - sig)))
        low = grad.astype(BF)
        right_ref[tower2, span] = low
        sums_ref[tower2 : tower2 + 1, span] = row_sums(low.astype(F32))
        sums_ref[layer_count + 3 : layer_count + 4, span] = row_sums(residue * act)
        sums_ref[layer_count + 2 : layer_count + 3, span] = row_sums(residue * current[span])
        grad_current[span] = residue * column(layer_count + 2, span)
    for span in spans:
        value = first_pre[span]
        sig = jax.nn.sigmoid(value)
        grad = times(tower2, span, right_ref.at[tower2]) * (sig * (1.0 + value * (1.0 - sig)))
        low = grad.astype(BF)
        right_ref[tower1, span] = low
        sums_ref[tower1 : tower1 + 1, span] = row_sums(low.astype(F32))
    for span in spans:
        grad_anchor[span] = times(tower1, span, right_ref.at[tower1])
    for layer in reversed(range(layer_count)):
        for span in spans:
            grad = grad_current[span]
            low = (anchor[span] * grad).astype(BF)
            right_ref[layer, span] = low
            sums_ref[layer : layer + 1, span] = row_sums(low.astype(F32))
            grad_anchor[span] += grad * update[layer, span]
        for span in spans:
            grad_current[span] += times(layer, span, right_ref.at[layer])
    for span in spans:
        grad_anchor[span] += grad_current[span]
    dense_grad_ref[...] = grad_anchor[0:16]
    slots_ref[...] = jnp.zeros_like(slots_ref)
    for field in range(field_count):
        first = dense_width + field * embed_dim
        slots_ref[place_ref[field], :embed_dim] = grad_anchor[first : first + embed_dim].astype(BF)


def dense_step(arrived, starts, place, dense_in, labels, weights, cols, out_b, layer_count, width, after):
    tab_count, _, pad_dim, count = arrived[0].shape
    slot_count = tab_count * sum(part.shape[1] for part in arrived)
    dense_width = dense_in.shape[1]
    size = weights.shape[1]
    matrix_count = layer_count + 2
    dense_rows = jnp.pad(dense_in.T.astype(F32), ((0, 16 - dense_width), (0, 0)))
    vmem = pl.BlockSpec(memory_space=pltpu.VMEM)
    smem = pl.BlockSpec(memory_space=pltpu.SMEM)
    flat = pltpu.VMEM((size, count), F32)
    return pl.pallas_call(
        functools.partial(dense_kernel, dense_width, width, starts, len(after)),
        in_specs=[smem, smem] + [vmem] * (len(arrived) + 2) + [ pl.BlockSpec(memory_space=pl.ANY), vmem]
        + [pl.BlockSpec(memory_space=pl.ANY)] * len(after),
        out_specs=[vmem] * 6,
        out_shape=[
            jax.ShapeDtypeStruct((1, count), F32),
            jax.ShapeDtypeStruct((16, count), F32),
            jax.ShapeDtypeStruct((slot_count, pad_dim, count), BF),
            jax.ShapeDtypeStruct((matrix_count, size, count), BF),
            jax.ShapeDtypeStruct((matrix_count, size, count), BF),
            jax.ShapeDtypeStruct((8, size), F32),
        ],
        scratch_shapes=[
            pltpu.VMEM(weights.shape, BF),
            flat,
            flat,
            pltpu.VMEM((layer_count, size, count), F32),
            flat,
            flat,
            flat,
            flat,
            pltpu.SemaphoreType.DMA((matrix_count,)),
        ],
        compiler_params=params(60),
        cost_estimate=cost(4 * matrix_count * size * size * count, 2 * weights.size + 30 * size * count),
        name="dense",
    )(
        place,
        out_b.astype(F32).reshape(1),
        *arrived,
        dense_rows,
        labels.astype(F32).reshape(1, count),
        weights,
        cols,
        *after,
    )


def chunk_place(piece, swapped):
    if not swapped:
        return piece
    return (piece & 3) | ((piece & 4) << 1) | ((piece & 8) >> 1)


def weight_kernel(core, own_ref, left_ref, right_ref, out_ref, *refs):
    pieces = MAIN // PIECE // 2
    half = MAIN // 2
    moved = refs[-1]
    for at in range(pieces):
        first = pl.multiple_of(((core * pieces + at) ^ own_ref[0]) * PIECE, PIECE)
        moved[at * PIECE : (at + 1) * PIECE] = left_ref[0, pl.ds(first, PIECE), :]
    product = lax.dot_general(
        moved[...], right_ref[0, :MAIN, :], NT, preferred_element_type=F32
    ).astype(out_ref.dtype)
    for chunk in range(2):
        for at in range(pieces):
            out_ref[chunk, chunk_place(at, chunk == 1), 0] = product[
                at * PIECE : (at + 1) * PIECE, chunk * half : (chunk + 1) * half
            ]
    if core == 0:
        strip_ref = refs[0]
        below = lax.dot_general(
            left_ref[0, MAIN : MAIN + 16, :], right_ref[0], NT, preferred_element_type=F32
        )
        beside = lax.dot_general(
            right_ref[0, MAIN : MAIN + 16, :], left_ref[0], NT, preferred_element_type=F32
        )
        strip_ref[0, 0:3] = below[0:3]
        strip_ref[0, 3:6] = beside[0:3]
        strip_ref[0, 6:8] = jnp.zeros((2, strip_ref.shape[2]), F32)


def weight_parts(left, right, own, core):
    matrix_count, size, count = left.shape
    half = MAIN // 2
    pieces = MAIN // PIECE // 2
    out_specs = [pl.BlockSpec((2, pieces, 1, PIECE, half), lambda m: (0, 0, m, 0, 0))]
    shapes = [jax.ShapeDtypeStruct((2, pieces, matrix_count, PIECE, half), BF if core else F32)]
    if core == 0:
        out_specs.append(pl.BlockSpec((1, 8, size), lambda m: (m, 0, 0)))
        shapes.append(jax.ShapeDtypeStruct((matrix_count, 8, size), F32))
    outs = pl.pallas_call(
        functools.partial(weight_kernel, core),
        grid=(matrix_count,),
        in_specs=[
            pl.BlockSpec(memory_space=pltpu.SMEM),
            pl.BlockSpec((1, size, count), lambda m: (m, 0, 0)),
            pl.BlockSpec((1, size, count), lambda m: (m, 0, 0)),
        ],
        out_specs=out_specs,
        out_shape=shapes,
        scratch_shapes=[pltpu.VMEM((half, count), BF)],
        compiler_params=params(40),
        cost_estimate=cost(matrix_count * size * size * count, 5 * matrix_count * size * size),
        name="weight_parts",
    )(own, left, right)
    return [outs[0].reshape((2, 2, 2, 2, 2, matrix_count, PIECE, half))] + list(outs[1:])


HALVES = [[("rep", 2), ("tab", 1)], [("tab", 1), ("rep", 2)]]
FAR = [(0, 1), (1, 0), (1, 1)]


def added(parts, *gates):
    value = parts[0].astype(F32)
    for other in parts[1:]:
        value = value + other.astype(F32)
    for gate in gates:
        value = value + gate
    return value


def joined(parts, token):
    one = (1.0 + token).astype(BF)
    return jnp.concatenate([parts[0] * one] + list(parts[1:]))


def assemble_kernel(layer_count, own_ref, *refs):
    blocks = refs[:8]
    strip_ref, cross_ref, first_ref, second_ref = refs[8:]
    matrix = pl.program_id(0)

    def fill(out_ref):
        for block, ref in enumerate(blocks):
            chunk, core, upper = block >> 2, (block >> 1) & 1, block & 1
            count, _, rows, lanes = ref.shape
            for at in range(count):
                piece = 2 * count * core + chunk_place(count * upper + at, chunk == 1)
                first = pl.multiple_of((piece ^ own_ref[0]) * rows, rows)
                out_ref[0, pl.ds(first, rows), chunk * lanes : (chunk + 1) * lanes] = ref[at, 0].astype(F32)
        height, width = out_ref.shape[1:]
        if width > MAIN:
            extra = width - MAIN
            for first in range(0, MAIN, 128):
                turned = strip_ref[0, :, first : first + 128].T
                out_ref[0, first : first + 128, MAIN:] = turned[:, 3 : 3 + extra]
        if height > MAIN:
            out_ref[0, MAIN:, :] = strip_ref[0, 0 : height - MAIN, :width]

    @pl.when(matrix < layer_count)
    def _():
        fill(cross_ref)

    @pl.when(matrix == layer_count)
    def _():
        fill(first_ref)

    @pl.when(matrix == layer_count + 1)
    def _():
        fill(second_ref)


def assemble(blocks, strips, own, layer_count, width, hidden):
    matrix_count = layer_count + 2
    size = strips.shape[2]
    shape = blocks[0].shape
    block = pl.BlockSpec(shape[:1] + (1,) + shape[2:], lambda m: (0, m, 0, 0))
    return pl.pallas_call(
        functools.partial(assemble_kernel, layer_count),
        grid=(matrix_count,),
        in_specs=[pl.BlockSpec(memory_space=pltpu.SMEM)]
        + [block] * 8
        + [pl.BlockSpec((1, 8, size), lambda m: (m, 0, 0))],
        out_specs=[
            pl.BlockSpec((1, width, width), lambda m: (jnp.minimum(m, layer_count - 1), 0, 0)),
            pl.BlockSpec((1, width, hidden), lambda m: (0, 0, 0)),
            pl.BlockSpec((1, hidden, hidden), lambda m: (0, 0, 0)),
        ],
        out_shape=[
            jax.ShapeDtypeStruct((layer_count, width, width), F32),
            jax.ShapeDtypeStruct((1, width, hidden), F32),
            jax.ShapeDtypeStruct((1, hidden, hidden), F32),
        ],
        compiler_params=params(56),
        cost_estimate=cost(0, 6 * matrix_count * size * size),
        name="assemble",
    )(own, *blocks, strips)


def on_device(
    ids,
    table_rows,
    table_place,
    dense_in,
    labels,
    tables,
    cross_w,
    cross_b,
    tower1_w,
    tower1_b,
    tower2_w,
    tower2_b,
    out_w,
    out_b,
):
    tab_count = lax.axis_size("tab")
    rep_count = lax.axis_size("rep")
    slot_count, embed_dim, table_len = tables.shape
    row_count, dense_width = dense_in.shape
    field_count = ids.shape[1]
    layer_count, width = cross_w.shape[:2]
    hidden = tower1_w.shape[0]
    size = round_up(width, 128)
    all_slots = slot_count * tab_count
    tab_at = lax.axis_index("tab")
    rep_at = lax.axis_index("rep")

    matches = table_place[:, None] == jnp.arange(all_slots, dtype=I32)[None, :]
    effective = ids % table_rows[None, :]
    by_slot = jnp.sum(jnp.where(matches[:, :, None], effective.T[:, None, :], 0), axis=0)
    slot_rows = jnp.sum(jnp.where(matches, table_rows[:, None], 0), axis=0)
    own_rows = lax.dynamic_slice_in_dim(slot_rows, tab_at * slot_count, slot_count)
    wanted = lax.all_to_all(
        by_slot.reshape(tab_count, slot_count, row_count), "tab", split_axis=0, concat_axis=0, tiled=True
    )
    listed = jnp.transpose(wanted, (1, 0, 2)).reshape(-1)

    first_size = slot_count % LOOK_SLOTS
    starts = ([0] if first_size else []) + list(range(first_size, slot_count, LOOK_SLOTS))
    arrived = []
    for begin in starts:
        looked = lookup(
            tables, listed, own_rows, tab_count, begin, LOOK_SLOTS if begin or not first_size else first_size
        )
        arrived.append(lax.all_to_all(looked, "tab", split_axis=0, concat_axis=0, tiled=True))

    ready = 1.0 + arrived[0][0, 0, embed_dim, 0]

    def padded(weight):
        return jnp.pad(weight * ready, ((0, size - weight.shape[0]), (0, size - weight.shape[1])))

    weights = jnp.stack(
        [padded(cross_w[at]) for at in range(layer_count)] + [padded(tower1_w.T), padded(tower2_w)]
    )
    vectors = [cross_b[at] for at in range(layer_count)]
    vectors += [tower1_b, tower2_b, out_w[:width], out_w[width:], out_w[:0]]
    cols = jnp.stack(
        [jnp.pad((v * ready).astype(F32), (0, size - v.shape[0])) for v in vectors], axis=1
    )


    def near_parts(own):
        return [own, swap(own, "rep", 1)]

    def far_bases(own):
        bases = [own]
        for mask in masks_of("rep")[1:]:
            bases = bases + [swap(part, "rep", mask) for part in bases]
        return bases[1:]

    def far_parts(bases):
        return [part for far in bases for part in near_parts(far)]

    wanted = wanted + (ready - 1.0).astype(I32)
    near_ids = [part[:, :, None, :] for part in near_parts(wanted)]
    far_ids = [part[:, :, None, :] for part in far_parts(far_bases(wanted))]
    logits, dense_grad, slots, left, right, sums = dense_step(
        arrived, starts, table_place, dense_in, labels, weights, cols, out_b, layer_count, width,
        near_ids + far_ids,
    )
    returned = lax.all_to_all(
        slots.reshape(tab_count, slot_count, slots.shape[1], row_count),
        "tab",
        split_axis=0,
        concat_axis=0,
        tiled=True,
    )

    share = table_len // rep_count
    base = (rep_at * share).astype(I32).reshape(1)

    def gate(value, result):
        return value * (1.0 + 0.0 * result.astype(F32)).astype(value.dtype)

    bits = [rep_at & 1, (rep_at >> 1) & 1, tab_at & 1, (tab_at >> 2) & 1, (tab_at >> 1) & 1]
    own = sum(bit << (4 - at) for at, bit in enumerate(bits)).astype(I32).reshape(1)
    (send,) = weight_parts(left, right, own, 1)
    keep, strips = weight_parts(left, right, own, 0)
    matrix_count = layer_count + 2
    far_grads = None
    table_grad = None
    token = jnp.zeros((), F32)
    near_jobs = list(range(slot_count))[::-1]
    far_jobs = list(range(slot_count))[::-1]

    def add_next(near, times, after):
        nonlocal table_grad, token
        jobs = near_jobs if near else far_jobs
        for _ in range(min(times, len(jobs))):
            table_grad, token = add_rows(
                near_grads if near else far_grads,
                near_ids if near else far_ids,
                base,
                share,
                embed_dim,
                jobs.pop(),
                table_grad,
                not near,
                after,
            )

    def zero_of(value):
        return 0.0 * value.astype(F32)

    small = jnp.concatenate([strips.reshape(matrix_count * 8, size), sums], axis=0)
    got = swap(send, "rep", 1)
    small = small + swap(small, "rep", 1)
    ahead = [added((keep[at, 1, 1], got[at, 1, 1])).astype(BF) for at in range(2)]
    first = [swap(ahead[at], *HALVES[at][0]) for at in range(2)]
    keep, got, _ = lax.optimization_barrier((keep, got, ahead))
    behind = [added((keep[at, 1, 0], got[at, 1, 0])).astype(BF) for at in range(2)]
    later = [swap(behind[at], *HALVES[at][0]) for at in range(2)]
    keep, got, _ = lax.optimization_barrier((keep, got, behind))
    kept = [added((keep[at, 0], got[at, 0])) for at in range(2)]
    sends = [added((kept[at][1], first[at])).astype(BF) for at in range(2)]
    sent = [swap(sends[at], *HALVES[at][1]) for at in range(2)]
    small = small + zero_of(sends[0][0, 0, 0, 0, 0])
    small = added([small] + [swap(small, "tab", mask) for mask in (2, 4, 6)])
    returned = gate(returned, sends[0][0, 0, 0, 0, 0] + sends[1][0, 0, 0, 0, 0])
    near_grads = near_parts(returned)
    add_next(True, 1, behind + sends)
    bases = far_bases(gate(returned, token))
    add_next(True, NEAR_FIRST - 1, sends)
    sources = [[kept[at][0], later[at], sent[at]] for at in range(2)]

    token = token + zero_of(small[0, 0])

    def take_far(high, low):
        both = [added([part[high, low] for part in sources[at]], token) for at in range(2)]
        return jnp.stack(both)

    kept = take_far(0, 0)
    sends = [take_far(high, low).astype(BF) for high, low in FAR]
    far = [swap(value, "tab", 4 * high + 2 * low) for value, (high, low) in zip(sends, FAR)]
    add_next(True, slot_count - NEAR_FIRST - 1, [kept] + sends)
    piece = added([kept, *far], token).astype(BF)
    for axis, known in (("rep", 2), ("tab", 3)):
        for mask in masks_of(axis)[known:]:
            piece = (piece.astype(F32) + swap(piece, axis, mask).astype(F32)).astype(BF)
    parts = [piece, swap(piece, "tab", 2), swap(piece, "tab", 4), swap(piece, "tab", 6)]
    add_next(True, slot_count, [piece])
    far_grads = far_parts([gate(part, piece[0, 0, 0, 0]) for part in bases])
    add_next(False, 1, [piece])
    values = [joined([part[at : at + 1] for part in parts], token) for at in range(2)]
    sent = [swap(values[at], *HALVES[at][1]) for at in range(2)]
    small = small + zero_of(values[1][0, 0, 0, 0])
    small = added([small, swap(small, "rep", 2), swap(small, "tab", 1), swap_both(small, 2, 1)])
    for axis, known in (("rep", 2), ("tab", 3)):
        for mask in masks_of(axis)[known:]:
            small = small + swap(small, axis, mask)
    add_next(False, 1, values)
    token = token + zero_of(small[0, 0])
    values = [joined((values[at], sent[at]), token) for at in range(2)]
    sent = [swap(values[at], *HALVES[at][0]) for at in range(2)]
    blocks = [[values[at], None, swap(values[at], "rep", 1), None] for at in range(2)]
    add_next(False, slot_count, values)
    for at in range(2):
        blocks[at][1] = gate(sent[at], token)
        blocks[at][3] = swap(blocks[at][1], "rep", 1)
    blocks = blocks[0] + blocks[1]

    strips = small[:-8].reshape(matrix_count, 8, size)
    sums = small[-8:]
    cross_w_grad, tower1_w_grad, tower2_w_grad = assemble(
        blocks, strips, own, layer_count, width, hidden
    )
    scalars = sums[layer_count + 4]
    return (
        scalars[0] / (row_count * tab_count * rep_count),
        logits.reshape(row_count),
        dense_grad[:dense_width].T,
        cross_w_grad,
        sums[:layer_count, :width],
        tower1_w_grad[0].T,
        sums[layer_count, :hidden],
        tower2_w_grad[0],
        sums[layer_count + 1, :hidden],
        jnp.concatenate([sums[layer_count + 2, :width], sums[layer_count + 3, :hidden]]),
        scalars[128],
        table_grad,
    )


def solution(mesh):
    placed = (
        P(("tab", "rep"), None),
        P(),
        P(),
        P(("tab", "rep"), None),
        P(("tab", "rep")),
        P("tab", None, None),
        P(),
        P(),
        P(),
        P(),
        P(),
        P(),
        P(),
        P(),
    )
    return jax.shard_map(
        on_device,
        mesh=mesh,
        in_specs=placed,
        out_specs=(
            P(),
            P(("tab", "rep")),
            P(("tab", "rep"), None),
            P(),
            P(),
            P(),
            P(),
            P(),
            P(),
            P(),
            P(),
            P("tab", None, "rep"),
        ),
        check_vma=False,
    )
```

```python
import functools

import jax
import jax.numpy as jnp
from jax import lax
from jax.experimental import pallas as pl
from jax.experimental.pallas import tpu as pltpu
from jax.sharding import PartitionSpec as P

BF = jnp.bfloat16
F32 = jnp.float32
I32 = jnp.int32
LOOK_SLOTS = 3
LOOK_LANES = 40
LOOK_BLOCKS = 8
LOOK_ROWS = 32
ADD_LOW = 512
ADD_TABS = 4
NEAR_FIRST = 2
FAR_FIRST = 2
MAIN = 1024
CHUNK = 384
PIECE = 32
MIB = 1024 * 1024
NT = (((1,), (1,)), ((), ()))
TN = (((0,), (0,)), ((), ()))


def round_up(size, unit):
    return -(-size // unit) * unit


def params(mib):
    return pltpu.CompilerParams(vmem_limit_bytes=mib * MIB)


def cost(flops, size):
    return pl.CostEstimate(flops=flops // 1000, bytes_accessed=size // 1000, transcendentals=0)


def swap(value, axis, mask):
    return lax.ppermute(value, axis, [(at, at ^ mask) for at in range(lax.axis_size(axis))])


def swap_both(value, rep_mask, tab_mask):
    rep_count = lax.axis_size("rep")
    perm = []
    for tab in range(lax.axis_size("tab")):
        for at in range(rep_count):
            perm.append((tab * rep_count + at, (tab ^ tab_mask) * rep_count + (at ^ rep_mask)))
    return lax.ppermute(value, ("tab", "rep"), perm)


def masks_of(axis):
    size = lax.axis_size(axis)
    return [1 << bit for bit in range(size.bit_length() - 1)]


def lookup_kernel(first_slot, ids_ref, rows_ref, table_hbm, out_ref, raw, stack, major, picked, sems):
    tab_count, slot_count, pad_dim, count = out_ref.shape
    embed_dim = raw.shape[1]
    total = tab_count * count
    copies = [
        pltpu.make_async_copy(table_hbm.at[first_slot + at], raw.at[at], sems.at[at])
        for at in range(slot_count)
    ]
    for copy in copies:
        copy.start()
    lane = lax.broadcasted_iota(I32, (1, 128), 1)
    stack[...] = jnp.zeros_like(stack)
    most = jnp.maximum(rows_ref[first_slot], 1)
    for at in range(1, slot_count):
        most = jnp.maximum(most, rows_ref[first_slot + at])
    for copy in copies:
        copy.wait()
    unit = 128 * LOOK_BLOCKS

    @pl.loop(0, (most + unit - 1) // unit)
    def _(step):
        for block in range(LOOK_BLOCKS):
            first = pl.multiple_of((step * LOOK_BLOCKS + block) * 128, 128)
            for at in range(slot_count):
                stack[block, at * LOOK_LANES : at * LOOK_LANES + embed_dim, :] = raw[
                    at, :, pl.ds(first, 128)
                ].astype(F32)
            major[pl.ds(first, 128), :] = stack[block].T

    @pl.loop(0, total // LOOK_ROWS)
    def _(step):
        base = step * LOOK_ROWS
        starts = [(first_slot + at) * total + base for at in range(slot_count)]
        for row in range(LOOK_ROWS):
            value = None
            for at in reversed(range(slot_count)):
                one = major[pl.ds(ids_ref[starts[at] + row], 1), :]
                value = one if value is None else jnp.where(lane < (at + 1) * LOOK_LANES, one, value)
            picked[pl.ds(base + row, 1), :] = value

    @pl.loop(0, tab_count)
    def _(tab):
        for block in range(0, count, 128):
            turned = picked[pl.ds(pl.multiple_of(tab * count + block, 128), 128), :].T
            for at in range(slot_count):
                rows = turned[at * LOOK_LANES : at * LOOK_LANES + pad_dim]
                out_ref[tab, at, :, block : block + 128] = rows.astype(BF)


def lookup(tables, wanted, own_rows, tab_count, first_slot, slot_count):
    all_count, embed_dim, table_len = tables.shape
    count = wanted.shape[0] // (all_count * tab_count)
    smem = pl.BlockSpec(memory_space=pltpu.SMEM)
    return pl.pallas_call(
        functools.partial(lookup_kernel, first_slot),
        in_specs=[smem, smem, pl.BlockSpec(memory_space=pl.ANY)],
        out_specs=pl.BlockSpec(memory_space=pltpu.VMEM),
        out_shape=jax.ShapeDtypeStruct((tab_count, slot_count, round_up(embed_dim, 8), count), BF),
        scratch_shapes=[
            pltpu.VMEM((slot_count, embed_dim, table_len), BF),
            pltpu.VMEM((LOOK_BLOCKS, 128, 128), F32),
            pltpu.VMEM((table_len, 128), F32),
            pltpu.VMEM((tab_count * count, 128), F32),
            pltpu.SemaphoreType.DMA((slot_count,)),
        ],
        compiler_params=params(56),
        cost_estimate=cost(
            600 * tab_count * count * table_len * slot_count // 8,
            2 * slot_count * embed_dim * (table_len + tab_count * count),
        ),
        name="lookup",
    )(wanted, own_rows, tables)


def add_kernel(part_count, has_before, base_ref, *refs):
    ids_refs = refs[:part_count]
    grad_refs = refs[part_count : 2 * part_count]
    before_ref = refs[2 * part_count] if has_before else None
    out_ref, token_ref, total = refs[-3:]
    step = pl.program_id(0)
    embed_dim = out_ref.shape[1]
    cols = grad_refs[0].shape[3]
    high_count = total.shape[1] // embed_dim

    @pl.when(step == 0)
    def _():
        total[...] = jnp.zeros_like(total)
        token_ref[...] = jnp.zeros_like(token_ref)

    high_iota = lax.broadcasted_iota(I32, (high_count, cols), 0)
    low_iota = lax.broadcasted_iota(I32, (ADD_LOW, cols), 0)
    product = None
    for ids_ref, grad_ref in zip(ids_refs, grad_refs):
        for tab in range(ids_ref.shape[0]):
            local = ids_ref[tab, 0] - base_ref[0]
            high = lax.shift_right_arithmetic(local, ADD_LOW.bit_length() - 1)
            low = local & (ADD_LOW - 1)
            high_hot = jnp.where(high_iota == high, 1.0, 0.0)
            low_hot = jnp.where(low_iota == low, 1.0, 0.0).astype(BF)
            grads = grad_ref[tab, 0, :embed_dim].astype(F32)
            left = (grads[:, None, :] * high_hot[None, :, :]).astype(BF)
            left = left.reshape(embed_dim * high_count, cols)
            term = lax.dot_general(left, low_hot, NT, preferred_element_type=F32)
            product = term if product is None else product + term
    for lane in range(ADD_LOW // 128):
        total[lane] += product[:, lane * 128 : (lane + 1) * 128]

    @pl.when(step == pl.num_programs(0) - 1)
    def _():
        for at in range(high_count):
            for part in range(0, embed_dim, 8):
                size = min(8, embed_dim - part)
                for lane in range(ADD_LOW // 128):
                    first = at * ADD_LOW + lane * 128
                    value = total[lane, pl.ds(part * high_count + at, size, stride=high_count), :]
                    if before_ref is not None:
                        value = value + before_ref[0, part : part + size, first : first + 128]
                    out_ref[0, part : part + size, first : first + 128] = value


def add_rows(grads, wanted, base, share, embed_dim, slot, so_far, accumulate, after):
    tab_count, slot_count, pad_dim, count = grads[0].shape
    part_count = len(grads)
    anywhere = pl.BlockSpec(memory_space=pl.ANY)
    block = pl.BlockSpec((1, embed_dim, share), lambda t: (slot, 0, 0))
    whole = [] if so_far is None else [so_far]
    table_grad, token = pl.pallas_call(
        functools.partial(add_kernel, part_count, accumulate),
        grid=(tab_count // ADD_TABS,),
        in_specs=[pl.BlockSpec(memory_space=pltpu.SMEM)]
        + [pl.BlockSpec((ADD_TABS, 1, 1, count), lambda t: (t, slot, 0, 0))] * part_count
        + [pl.BlockSpec((ADD_TABS, 1, pad_dim, count), lambda t: (t, slot, 0, 0))] * part_count
        + [block if accumulate else anywhere] * len(whole)
        + [anywhere] * len(after),
        out_specs=[block, pl.BlockSpec((8, 128), lambda t: (0, 0))],
        scratch_shapes=[pltpu.VMEM((ADD_LOW // 128, embed_dim * (share // ADD_LOW), 128), F32)],
        out_shape=[
            jax.ShapeDtypeStruct((slot_count, embed_dim, share), F32),
            jax.ShapeDtypeStruct((8, 128), F32),
        ],
        input_output_aliases={1 + 2 * part_count: 0} if whole else {},
        compiler_params=params(40),
        cost_estimate=cost(
            2 * part_count * tab_count * count * share * embed_dim,
            2 * embed_dim * (2 * share + part_count * tab_count * count),
        ),
        name="add_rows",
    )(base, *wanted, *grads, *whole, *after)
    return table_grad, token[0, 0]


def row_sums(value):
    part = value[:, :128]
    for first in range(128, value.shape[1], 128):
        part = part + value[:, first : first + 128]
    return jnp.sum(part.T, axis=0, keepdims=True)


def dense_kernel(
    dense_width,
    width,
    starts,
    after_count,
    place_ref,
    bias_ref,
    *refs,
):
    group_count = len(starts)
    arrived_refs = refs[:group_count]
    first = group_count + 4
    dense_refs = refs[group_count:first] + refs[first + after_count :]
    dense_body(dense_width, width, starts, place_ref, bias_ref, arrived_refs, *dense_refs)


def dense_body(
    dense_width,
    width,
    starts,
    place_ref,
    bias_ref,
    arrived_refs,
    dense_ref,
    label_ref,
    weight_hbm,
    cols_ref,
    logits_ref,
    dense_grad_ref,
    slots_ref,
    left_ref,
    right_ref,
    sums_ref,
    weight,
    anchor,
    current,
    update,
    first_pre,
    second_pre,
    grad_anchor,
    grad_current,
    sems,
):
    layer_count = update.shape[0]
    tower1, tower2 = layer_count, layer_count + 1
    pad_dim = arrived_refs[0].shape[2]
    field_count = place_ref.shape[0]
    embed_dim = (width - dense_width) // field_count
    slot_count = sum(ref.shape[1] for ref in arrived_refs)
    size, cols = anchor.shape
    spans = [pl.ds(first, CHUNK) for first in range(0, size, CHUNK)]
    copies = [
        pltpu.make_async_copy(weight_hbm.at[at], weight.at[at], sems.at[at])
        for at in range(layer_count + 2)
    ]
    for copy in copies:
        copy.start()

    def column(at, span):
        return cols_ref[span, at : at + 1]

    def times(at, span, operand):
        return jnp.dot(weight[at, span, :], operand[...], preferred_element_type=F32)

    def transposed_times(at, span, operand):
        return lax.dot_general(weight[at, :, span], operand[...], TN, preferred_element_type=F32)

    anchor[0:16] = dense_ref[...]
    tail = width // 8 * 8
    anchor[tail:] = jnp.zeros((size - tail, cols), F32)
    for field in range(field_count):
        first = dense_width + field * embed_dim
        tab = place_ref[field] // slot_count
        slot = place_ref[field] - tab * slot_count
        value = arrived_refs[0][tab, jnp.minimum(slot, arrived_refs[0].shape[1] - 1)]
        for begin, ref in zip(starts[1:], arrived_refs[1:]):
            other = ref[tab, jnp.clip(slot - begin, 0, ref.shape[1] - 1)]
            value = jnp.where(slot >= begin, other, value)
        anchor[first : first + embed_dim] = value.astype(F32)[:embed_dim]
    for span in spans:
        left_ref[0, span] = anchor[span].astype(BF)
        left_ref[tower1, span] = anchor[span].astype(BF)
    for layer in range(layer_count):
        copies[layer].wait()
        for span in spans:
            value = transposed_times(layer, span, left_ref.at[layer]) + column(layer, span)
            update[layer, span] = value
            before = anchor if layer == 0 else current
            after = anchor[span] * value + before[span]
            current[span] = after
            if layer + 1 < layer_count:
                left_ref[layer + 1, span] = after.astype(BF)
    copies[tower1].wait()
    for span in spans:
        value = transposed_times(tower1, span, left_ref.at[0]) + column(tower1, span)
        first_pre[span] = value
        left_ref[tower2, span] = (value * jax.nn.sigmoid(value)).astype(BF)
    copies[tower2].wait()
    logits = jnp.full((1, cols), bias_ref[0], F32)
    for span in spans:
        value = transposed_times(tower2, span, left_ref.at[tower2]) + column(tower2, span)
        second_pre[span] = value
        act = value * jax.nn.sigmoid(value)
        terms = current[span] * column(layer_count + 2, span) + act * column(layer_count + 3, span)
        logits = logits + jnp.sum(terms, axis=0, keepdims=True)
    logits_ref[...] = logits
    target = label_ref[...]
    residue = jax.nn.sigmoid(logits) - target
    softplus = jnp.maximum(logits, 0.0) + jnp.log1p(jnp.exp(-jnp.abs(logits)))
    sums_ref[layer_count + 4 :, :] = jnp.zeros((sums_ref.shape[0] - layer_count - 4, size), F32)
    loss_row = jnp.sum(softplus - target * logits, axis=1, keepdims=True)
    bias_row = jnp.sum(residue, axis=1, keepdims=True)
    sums_ref[layer_count + 4 : layer_count + 5, 0:128] = jnp.broadcast_to(loss_row, (1, 128))
    sums_ref[layer_count + 4 : layer_count + 5, 128:256] = jnp.broadcast_to(bias_row, (1, 128))
    for span in spans:
        value = second_pre[span]
        sig = jax.nn.sigmoid(value)
        act = value * sig
        grad = residue * column(layer_count + 3, span) * (sig * (1.0 + value * (1.0 - sig)))
        low = grad.astype(BF)
        right_ref[tower2, span] = low
        sums_ref[tower2 : tower2 + 1, span] = row_sums(low.astype(F32))
        sums_ref[layer_count + 3 : layer_count + 4, span] = row_sums(residue * act)
        sums_ref[layer_count + 2 : layer_count + 3, span] = row_sums(residue * current[span])
        grad_current[span] = residue * column(layer_count + 2, span)
    for span in spans:
        value = first_pre[span]
        sig = jax.nn.sigmoid(value)
        grad = times(tower2, span, right_ref.at[tower2]) * (sig * (1.0 + value * (1.0 - sig)))
        low = grad.astype(BF)
        right_ref[tower1, span] = low
        sums_ref[tower1 : tower1 + 1, span] = row_sums(low.astype(F32))
    for span in spans:
        grad_anchor[span] = times(tower1, span, right_ref.at[tower1])
    for layer in reversed(range(layer_count)):
        for span in spans:
            grad = grad_current[span]
            low = (anchor[span] * grad).astype(BF)
            right_ref[layer, span] = low
            sums_ref[layer : layer + 1, span] = row_sums(low.astype(F32))
            grad_anchor[span] += grad * update[layer, span]
        for span in spans:
            grad_current[span] += times(layer, span, right_ref.at[layer])
    for span in spans:
        grad_anchor[span] += grad_current[span]
    dense_grad_ref[...] = grad_anchor[0:16]
    slots_ref[...] = jnp.zeros_like(slots_ref)
    for field in range(field_count):
        first = dense_width + field * embed_dim
        slots_ref[place_ref[field], :embed_dim] = grad_anchor[first : first + embed_dim].astype(BF)


def dense_step(arrived, starts, place, dense_in, labels, weights, cols, out_b, layer_count, width, after):
    tab_count, _, pad_dim, count = arrived[0].shape
    slot_count = tab_count * sum(part.shape[1] for part in arrived)
    dense_width = dense_in.shape[1]
    size = weights.shape[1]
    matrix_count = layer_count + 2
    dense_rows = jnp.pad(dense_in.T.astype(F32), ((0, 16 - dense_width), (0, 0)))
    vmem = pl.BlockSpec(memory_space=pltpu.VMEM)
    smem = pl.BlockSpec(memory_space=pltpu.SMEM)
    flat = pltpu.VMEM((size, count), F32)
    return pl.pallas_call(
        functools.partial(dense_kernel, dense_width, width, starts, len(after)),
        in_specs=[smem, smem] + [vmem] * (len(arrived) + 2) + [ pl.BlockSpec(memory_space=pl.ANY), vmem]
        + [pl.BlockSpec(memory_space=pl.ANY)] * len(after),
        out_specs=[vmem] * 6,
        out_shape=[
            jax.ShapeDtypeStruct((1, count), F32),
            jax.ShapeDtypeStruct((16, count), F32),
            jax.ShapeDtypeStruct((slot_count, pad_dim, count), BF),
            jax.ShapeDtypeStruct((matrix_count, size, count), BF),
            jax.ShapeDtypeStruct((matrix_count, size, count), BF),
            jax.ShapeDtypeStruct((8, size), F32),
        ],
        scratch_shapes=[
            pltpu.VMEM(weights.shape, BF),
            flat,
            flat,
            pltpu.VMEM((layer_count, size, count), F32),
            flat,
            flat,
            flat,
            flat,
            pltpu.SemaphoreType.DMA((matrix_count,)),
        ],
        compiler_params=params(60),
        cost_estimate=cost(4 * matrix_count * size * size * count, 2 * weights.size + 30 * size * count),
        name="dense",
    )(
        place,
        out_b.astype(F32).reshape(1),
        *arrived,
        dense_rows,
        labels.astype(F32).reshape(1, count),
        weights,
        cols,
        *after,
    )


def chunk_place(piece, swapped):
    if not swapped:
        return piece
    return (piece & 3) | ((piece & 4) << 1) | ((piece & 8) >> 1)


def weight_kernel(core, own_ref, left_ref, right_ref, out_ref, *refs):
    pieces = MAIN // PIECE // 2
    half = MAIN // 2
    moved = refs[-1]
    for at in range(pieces):
        first = pl.multiple_of(((core * pieces + at) ^ own_ref[0]) * PIECE, PIECE)
        moved[at * PIECE : (at + 1) * PIECE] = left_ref[0, pl.ds(first, PIECE), :]
    product = lax.dot_general(
        moved[...], right_ref[0, :MAIN, :], NT, preferred_element_type=F32
    ).astype(out_ref.dtype)
    for chunk in range(2):
        for at in range(pieces):
            out_ref[chunk, chunk_place(at, chunk == 1), 0] = product[
                at * PIECE : (at + 1) * PIECE, chunk * half : (chunk + 1) * half
            ]
    if core == 0:
        strip_ref = refs[0]
        below = lax.dot_general(
            left_ref[0, MAIN : MAIN + 16, :], right_ref[0], NT, preferred_element_type=F32
        )
        beside = lax.dot_general(
            right_ref[0, MAIN : MAIN + 16, :], left_ref[0], NT, preferred_element_type=F32
        )
        strip_ref[0, 0:3] = below[0:3]
        strip_ref[0, 3:6] = beside[0:3]
        strip_ref[0, 6:8] = jnp.zeros((2, strip_ref.shape[2]), F32)


def weight_parts(left, right, own, core):
    matrix_count, size, count = left.shape
    half = MAIN // 2
    pieces = MAIN // PIECE // 2
    out_specs = [pl.BlockSpec((2, pieces, 1, PIECE, half), lambda m: (0, 0, m, 0, 0))]
    shapes = [jax.ShapeDtypeStruct((2, pieces, matrix_count, PIECE, half), BF if core else F32)]
    if core == 0:
        out_specs.append(pl.BlockSpec((1, 8, size), lambda m: (m, 0, 0)))
        shapes.append(jax.ShapeDtypeStruct((matrix_count, 8, size), F32))
    outs = pl.pallas_call(
        functools.partial(weight_kernel, core),
        grid=(matrix_count,),
        in_specs=[
            pl.BlockSpec(memory_space=pltpu.SMEM),
            pl.BlockSpec((1, size, count), lambda m: (m, 0, 0)),
            pl.BlockSpec((1, size, count), lambda m: (m, 0, 0)),
        ],
        out_specs=out_specs,
        out_shape=shapes,
        scratch_shapes=[pltpu.VMEM((half, count), BF)],
        compiler_params=params(60),
        cost_estimate=cost(matrix_count * size * size * count, 5 * matrix_count * size * size),
        name="weight_parts",
    )(own, left, right)
    return [outs[0].reshape((2, 2, 2, 2, 2, matrix_count, PIECE, half))] + list(outs[1:])


HALVES = [[("rep", 2), ("tab", 1)], [("tab", 1), ("rep", 2)]]
FAR = [(0, 1), (1, 0), (1, 1)]


def added(parts, *gates):
    value = parts[0].astype(F32)
    for other in parts[1:]:
        value = value + other.astype(F32)
    for gate in gates:
        value = value + gate
    return value


def joined(parts, token):
    one = (1.0 + token).astype(BF)
    return jnp.concatenate([part * one for part in parts])


def assemble_kernel(layer_count, own_ref, *refs):
    blocks = refs[:16]
    strip_ref, cross_ref, first_ref, second_ref = refs[16:]
    matrix = pl.program_id(0)

    def fill(out_ref):
        for block, ref in enumerate(blocks):
            chunk, core, upper = block >> 3, (block >> 2) & 1, block & 3
            count, _, rows, lanes = ref.shape
            for at in range(count):
                piece = 4 * count * core + chunk_place(count * upper + at, chunk == 1)
                first = pl.multiple_of((piece ^ own_ref[0]) * rows, rows)
                out_ref[0, pl.ds(first, rows), chunk * lanes : (chunk + 1) * lanes] = ref[at, 0].astype(F32)
        height, width = out_ref.shape[1:]
        if width > MAIN:
            extra = width - MAIN
            for first in range(0, MAIN, 128):
                turned = strip_ref[0, :, first : first + 128].T
                out_ref[0, first : first + 128, MAIN:] = turned[:, 3 : 3 + extra]
        if height > MAIN:
            out_ref[0, MAIN:, :] = strip_ref[0, 0 : height - MAIN, :width]

    @pl.when(matrix < layer_count)
    def _():
        fill(cross_ref)

    @pl.when(matrix == layer_count)
    def _():
        fill(first_ref)

    @pl.when(matrix == layer_count + 1)
    def _():
        fill(second_ref)


def assemble(blocks, strips, own, layer_count, width, hidden):
    matrix_count = layer_count + 2
    size = strips.shape[2]
    shape = blocks[0].shape
    block = pl.BlockSpec(shape[:1] + (1,) + shape[2:], lambda m: (0, m, 0, 0))
    return pl.pallas_call(
        functools.partial(assemble_kernel, layer_count),
        grid=(matrix_count,),
        in_specs=[pl.BlockSpec(memory_space=pltpu.SMEM)]
        + [block] * 16
        + [pl.BlockSpec((1, 8, size), lambda m: (m, 0, 0))],
        out_specs=[
            pl.BlockSpec((1, width, width), lambda m: (jnp.minimum(m, layer_count - 1), 0, 0)),
            pl.BlockSpec((1, width, hidden), lambda m: (0, 0, 0)),
            pl.BlockSpec((1, hidden, hidden), lambda m: (0, 0, 0)),
        ],
        out_shape=[
            jax.ShapeDtypeStruct((layer_count, width, width), F32),
            jax.ShapeDtypeStruct((1, width, hidden), F32),
            jax.ShapeDtypeStruct((1, hidden, hidden), F32),
        ],
        compiler_params=params(56),
        cost_estimate=cost(0, 6 * matrix_count * size * size),
        name="assemble",
    )(own, *blocks, strips)


def on_device(
    ids,
    table_rows,
    table_place,
    dense_in,
    labels,
    tables,
    cross_w,
    cross_b,
    tower1_w,
    tower1_b,
    tower2_w,
    tower2_b,
    out_w,
    out_b,
):
    tab_count = lax.axis_size("tab")
    rep_count = lax.axis_size("rep")
    slot_count, embed_dim, table_len = tables.shape
    row_count, dense_width = dense_in.shape
    field_count = ids.shape[1]
    layer_count, width = cross_w.shape[:2]
    hidden = tower1_w.shape[0]
    size = round_up(width, 128)
    all_slots = slot_count * tab_count
    tab_at = lax.axis_index("tab")
    rep_at = lax.axis_index("rep")

    matches = table_place[:, None] == jnp.arange(all_slots, dtype=I32)[None, :]
    effective = ids % table_rows[None, :]
    by_slot = jnp.sum(jnp.where(matches[:, :, None], effective.T[:, None, :], 0), axis=0)
    slot_rows = jnp.sum(jnp.where(matches, table_rows[:, None], 0), axis=0)
    own_rows = lax.dynamic_slice_in_dim(slot_rows, tab_at * slot_count, slot_count)
    wanted = lax.all_to_all(
        by_slot.reshape(tab_count, slot_count, row_count), "tab", split_axis=0, concat_axis=0, tiled=True
    )
    listed = jnp.transpose(wanted, (1, 0, 2)).reshape(-1)

    first_size = slot_count % LOOK_SLOTS
    starts = ([0] if first_size else []) + list(range(first_size, slot_count, LOOK_SLOTS))
    arrived = []
    for begin in starts:
        looked = lookup(
            tables, listed, own_rows, tab_count, begin, LOOK_SLOTS if begin or not first_size else first_size
        )
        arrived.append(lax.all_to_all(looked, "tab", split_axis=0, concat_axis=0, tiled=True))

    ready = 1.0 + arrived[0][0, 0, embed_dim, 0]

    def padded(weight):
        return jnp.pad(weight * ready, ((0, size - weight.shape[0]), (0, size - weight.shape[1])))

    weights = jnp.stack(
        [padded(cross_w[at]) for at in range(layer_count)] + [padded(tower1_w.T), padded(tower2_w)]
    )
    vectors = [cross_b[at] for at in range(layer_count)]
    vectors += [tower1_b, tower2_b, out_w[:width], out_w[width:], out_w[:0]]
    cols = jnp.stack(
        [jnp.pad((v * ready).astype(F32), (0, size - v.shape[0])) for v in vectors], axis=1
    )


    def near_parts(own):
        return [own, swap(own, "rep", 1)]

    def far_bases(own):
        bases = [own]
        for mask in masks_of("rep")[1:]:
            bases = bases + [swap(part, "rep", mask) for part in bases]
        return bases[1:]

    def far_parts(bases):
        return [part for far in bases for part in near_parts(far)]

    wanted = wanted + (ready - 1.0).astype(I32)
    near_ids = [part[:, :, None, :] for part in near_parts(wanted)]
    far_ids = [part[:, :, None, :] for part in far_parts(far_bases(wanted))]
    logits, dense_grad, slots, left, right, sums = dense_step(
        arrived, starts, table_place, dense_in, labels, weights, cols, out_b, layer_count, width,
        near_ids + far_ids,
    )
    returned = lax.all_to_all(
        slots.reshape(tab_count, slot_count, slots.shape[1], row_count),
        "tab",
        split_axis=0,
        concat_axis=0,
        tiled=True,
    )

    share = table_len // rep_count
    base = (rep_at * share).astype(I32).reshape(1)

    def gate(value, result):
        return value * (1.0 + 0.0 * result.astype(F32)).astype(value.dtype)

    bits = [rep_at & 1, (rep_at >> 1) & 1, tab_at & 1, (tab_at >> 2) & 1, (tab_at >> 1) & 1]
    own = sum(bit << (4 - at) for at, bit in enumerate(bits)).astype(I32).reshape(1)
    (send,) = weight_parts(left, right, own, 1)
    keep, strips = weight_parts(left, right, own, 0)
    matrix_count = layer_count + 2
    far_grads = None
    table_grad = None
    token = jnp.zeros((), F32)
    near_jobs = list(range(slot_count))[::-1]
    far_jobs = list(range(slot_count))[::-1]

    def add_next(near, times, after):
        nonlocal table_grad, token
        jobs = near_jobs if near else far_jobs
        for _ in range(min(times, len(jobs))):
            table_grad, token = add_rows(
                near_grads if near else far_grads,
                near_ids if near else far_ids,
                base,
                share,
                embed_dim,
                jobs.pop(),
                table_grad,
                not near,
                after,
            )

    def zero_of(value):
        return 0.0 * value.astype(F32)

    small = jnp.concatenate([strips.reshape(matrix_count * 8, size), sums], axis=0)
    got = swap(send, "rep", 1)
    small = small + swap(small, "rep", 1)
    ahead = [added((keep[at, 1, 1], got[at, 1, 1])).astype(BF) for at in range(2)]
    first = [swap(ahead[at], *HALVES[at][0]) for at in range(2)]
    keep, got, _ = lax.optimization_barrier((keep, got, ahead))
    behind = [added((keep[at, 1, 0], got[at, 1, 0])).astype(BF) for at in range(2)]
    later = [swap(behind[at], *HALVES[at][0]) for at in range(2)]
    keep, got, _ = lax.optimization_barrier((keep, got, behind))
    kept = [added((keep[at, 0], got[at, 0])) for at in range(2)]
    sends = [added((kept[at][1], first[at])).astype(BF) for at in range(2)]
    sent = [swap(sends[at], *HALVES[at][1]) for at in range(2)]
    small = small + zero_of(sends[0][0, 0, 0, 0, 0])
    small = added([small] + [swap(small, "tab", mask) for mask in (2, 4, 6)])
    returned = gate(returned, sends[0][0, 0, 0, 0, 0] + sends[1][0, 0, 0, 0, 0])
    near_grads = near_parts(returned)
    add_next(True, 1, behind + sends)
    bases = far_bases(gate(returned, token))
    add_next(True, NEAR_FIRST - 1, sends)
    sources = [[kept[at][0], later[at], sent[at]] for at in range(2)]

    token = token + zero_of(small[0, 0])

    def take_far(high, low):
        both = [added([part[high, low] for part in sources[at]], token) for at in range(2)]
        return jnp.stack(both)

    kept = take_far(0, 0)
    sends = [take_far(high, low).astype(BF) for high, low in FAR]
    far = [swap(value, "tab", 4 * high + 2 * low) for value, (high, low) in zip(sends, FAR)]
    add_next(True, slot_count, [kept] + sends)
    piece = added([kept, *far], token).astype(BF)
    for axis, known in (("rep", 2), ("tab", 3)):
        for mask in masks_of(axis)[known:]:
            piece = (piece.astype(F32) + swap(piece, axis, mask).astype(F32)).astype(BF)
    parts = [piece, swap(piece, "tab", 2), swap(piece, "tab", 4), swap(piece, "tab", 6)]
    far_grads = far_parts([gate(part, piece[0, 0, 0, 0]) for part in bases])
    add_next(False, FAR_FIRST, [piece])
    values = [joined([part[at : at + 1] for part in parts], token) for at in range(2)]
    near = [swap(values[at], *HALVES[at][1]) for at in range(2)]
    across = [swap(values[at], *HALVES[at][0]) for at in range(2)]
    add_next(False, 1, values)
    both = [swap(near[at], *HALVES[at][0]) for at in range(2)]
    add_next(False, 1, near)
    small = small + zero_of(token)
    small = added([small, swap(small, "rep", 2), swap(small, "tab", 1), swap_both(small, 2, 1)])
    for axis, known in (("rep", 2), ("tab", 3)):
        for mask in masks_of(axis)[known:]:
            small = small + swap(small, axis, mask)
    other = []
    for at in range(2):
        other.append([swap(part, "rep", 1) for part in (values[at], near[at], across[at])])
    add_next(False, slot_count, other[0] + other[1])
    blocks = []
    for at in range(2):
        last = gate(both[at], token)
        blocks += [values[at], near[at], across[at], last] + other[at] + [swap(last, "rep", 1)]

    strips = small[:-8].reshape(matrix_count, 8, size)
    sums = small[-8:]
    cross_w_grad, tower1_w_grad, tower2_w_grad = assemble(
        blocks, strips, own, layer_count, width, hidden
    )
    scalars = sums[layer_count + 4]
    return (
        scalars[0] / (row_count * tab_count * rep_count),
        logits.reshape(row_count),
        dense_grad[:dense_width].T,
        cross_w_grad,
        sums[:layer_count, :width],
        tower1_w_grad[0].T,
        sums[layer_count, :hidden],
        tower2_w_grad[0],
        sums[layer_count + 1, :hidden],
        jnp.concatenate([sums[layer_count + 2, :width], sums[layer_count + 3, :hidden]]),
        scalars[128],
        table_grad,
    )


def solution(mesh):
    placed = (
        P(("tab", "rep"), None),
        P(),
        P(),
        P(("tab", "rep"), None),
        P(("tab", "rep")),
        P("tab", None, None),
        P(),
        P(),
        P(),
        P(),
        P(),
        P(),
        P(),
        P(),
    )
    return jax.shard_map(
        on_device,
        mesh=mesh,
        in_specs=placed,
        out_specs=(
            P(),
            P(("tab", "rep")),
            P(("tab", "rep"), None),
            P(),
            P(),
            P(),
            P(),
            P(),
            P(),
            P(),
            P(),
            P("tab", None, "rep"),
        ),
        check_vma=False,
    )
```

```python
import functools

import jax
import jax.numpy as jnp
from jax import lax
from jax.experimental import pallas as pl
from jax.experimental.pallas import tpu as pltpu
from jax.sharding import PartitionSpec as P

BF = jnp.bfloat16
F32 = jnp.float32
I32 = jnp.int32
LOOK_SLOTS = 3
LOOK_LANES = 40
LOOK_BLOCKS = 8
LOOK_ROWS = 32
ADD_LOW = 512
ADD_TABS = 4
NEAR_FIRST = 2
FAR_FIRST = 2
MAIN = 1024
CHUNK = 384
PIECE = 32
MIB = 1024 * 1024
NT = (((1,), (1,)), ((), ()))
TN = (((0,), (0,)), ((), ()))


def round_up(size, unit):
    return -(-size // unit) * unit


def params(mib):
    return pltpu.CompilerParams(vmem_limit_bytes=mib * MIB)


def cost(flops, size):
    return pl.CostEstimate(flops=flops // 1000, bytes_accessed=size // 1000, transcendentals=0)


def swap(value, axis, mask):
    return lax.ppermute(value, axis, [(at, at ^ mask) for at in range(lax.axis_size(axis))])


def swap_both(value, rep_mask, tab_mask):
    rep_count = lax.axis_size("rep")
    perm = []
    for tab in range(lax.axis_size("tab")):
        for at in range(rep_count):
            perm.append((tab * rep_count + at, (tab ^ tab_mask) * rep_count + (at ^ rep_mask)))
    return lax.ppermute(value, ("tab", "rep"), perm)


def masks_of(axis):
    size = lax.axis_size(axis)
    return [1 << bit for bit in range(size.bit_length() - 1)]


def lookup_kernel(first_slot, ids_ref, rows_ref, table_hbm, out_ref, raw, stack, major, picked, sems):
    tab_count, slot_count, pad_dim, count = out_ref.shape
    embed_dim = raw.shape[1]
    total = tab_count * count
    copies = [
        pltpu.make_async_copy(table_hbm.at[first_slot + at], raw.at[at], sems.at[at])
        for at in range(slot_count)
    ]
    for copy in copies:
        copy.start()
    lane = lax.broadcasted_iota(I32, (1, 128), 1)
    stack[...] = jnp.zeros_like(stack)
    most = jnp.maximum(rows_ref[first_slot], 1)
    for at in range(1, slot_count):
        most = jnp.maximum(most, rows_ref[first_slot + at])
    for copy in copies:
        copy.wait()
    unit = 128 * LOOK_BLOCKS

    @pl.loop(0, (most + unit - 1) // unit)
    def _(step):
        for block in range(LOOK_BLOCKS):
            first = pl.multiple_of((step * LOOK_BLOCKS + block) * 128, 128)
            for at in range(slot_count):
                stack[block, at * LOOK_LANES : at * LOOK_LANES + embed_dim, :] = raw[
                    at, :, pl.ds(first, 128)
                ].astype(F32)
            major[pl.ds(first, 128), :] = stack[block].T

    @pl.loop(0, total // LOOK_ROWS)
    def _(step):
        base = step * LOOK_ROWS
        starts = [(first_slot + at) * total + base for at in range(slot_count)]
        for row in range(LOOK_ROWS):
            value = None
            for at in reversed(range(slot_count)):
                one = major[pl.ds(ids_ref[starts[at] + row], 1), :]
                value = one if value is None else jnp.where(lane < (at + 1) * LOOK_LANES, one, value)
            picked[pl.ds(base + row, 1), :] = value

    @pl.loop(0, tab_count)
    def _(tab):
        for block in range(0, count, 128):
            turned = picked[pl.ds(pl.multiple_of(tab * count + block, 128), 128), :].T
            for at in range(slot_count):
                rows = turned[at * LOOK_LANES : at * LOOK_LANES + pad_dim]
                out_ref[tab, at, :, block : block + 128] = rows.astype(BF)


def lookup(tables, wanted, own_rows, tab_count, first_slot, slot_count):
    all_count, embed_dim, table_len = tables.shape
    count = wanted.shape[0] // (all_count * tab_count)
    smem = pl.BlockSpec(memory_space=pltpu.SMEM)
    return pl.pallas_call(
        functools.partial(lookup_kernel, first_slot),
        in_specs=[smem, smem, pl.BlockSpec(memory_space=pl.ANY)],
        out_specs=pl.BlockSpec(memory_space=pltpu.VMEM),
        out_shape=jax.ShapeDtypeStruct((tab_count, slot_count, round_up(embed_dim, 8), count), BF),
        scratch_shapes=[
            pltpu.VMEM((slot_count, embed_dim, table_len), BF),
            pltpu.VMEM((LOOK_BLOCKS, 128, 128), F32),
            pltpu.VMEM((table_len, 128), F32),
            pltpu.VMEM((tab_count * count, 128), F32),
            pltpu.SemaphoreType.DMA((slot_count,)),
        ],
        compiler_params=params(56),
        cost_estimate=cost(
            600 * tab_count * count * table_len * slot_count // 8,
            2 * slot_count * embed_dim * (table_len + tab_count * count),
        ),
        name="lookup",
    )(wanted, own_rows, tables)


def add_kernel(part_count, has_before, base_ref, *refs):
    ids_refs = refs[:part_count]
    grad_refs = refs[part_count : 2 * part_count]
    before_ref = refs[2 * part_count] if has_before else None
    out_ref, token_ref, total = refs[-3:]
    step = pl.program_id(0)
    embed_dim = out_ref.shape[1]
    cols = grad_refs[0].shape[3]
    high_count = total.shape[1] // embed_dim

    @pl.when(step == 0)
    def _():
        total[...] = jnp.zeros_like(total)
        token_ref[...] = jnp.zeros_like(token_ref)

    high_iota = lax.broadcasted_iota(I32, (high_count, cols), 0)
    low_iota = lax.broadcasted_iota(I32, (ADD_LOW, cols), 0)
    product = None
    for ids_ref, grad_ref in zip(ids_refs, grad_refs):
        for tab in range(ids_ref.shape[0]):
            local = ids_ref[tab, 0] - base_ref[0]
            high = lax.shift_right_arithmetic(local, ADD_LOW.bit_length() - 1)
            low = local & (ADD_LOW - 1)
            high_hot = jnp.where(high_iota == high, 1.0, 0.0)
            low_hot = jnp.where(low_iota == low, 1.0, 0.0).astype(BF)
            grads = grad_ref[tab, 0, :embed_dim].astype(F32)
            left = (grads[:, None, :] * high_hot[None, :, :]).astype(BF)
            left = left.reshape(embed_dim * high_count, cols)
            term = lax.dot_general(left, low_hot, NT, preferred_element_type=F32)
            product = term if product is None else product + term
    for lane in range(ADD_LOW // 128):
        total[lane] += product[:, lane * 128 : (lane + 1) * 128]

    @pl.when(step == pl.num_programs(0) - 1)
    def _():
        for at in range(high_count):
            for part in range(0, embed_dim, 8):
                size = min(8, embed_dim - part)
                for lane in range(ADD_LOW // 128):
                    first = at * ADD_LOW + lane * 128
                    value = total[lane, pl.ds(part * high_count + at, size, stride=high_count), :]
                    if before_ref is not None:
                        value = value + before_ref[0, part : part + size, first : first + 128]
                    out_ref[0, part : part + size, first : first + 128] = value


def add_rows(grads, wanted, base, share, embed_dim, slot, so_far, accumulate, after):
    tab_count, slot_count, pad_dim, count = grads[0].shape
    part_count = len(grads)
    anywhere = pl.BlockSpec(memory_space=pl.ANY)
    block = pl.BlockSpec((1, embed_dim, share), lambda t: (slot, 0, 0))
    whole = [] if so_far is None else [so_far]
    table_grad, token = pl.pallas_call(
        functools.partial(add_kernel, part_count, accumulate),
        grid=(tab_count // ADD_TABS,),
        in_specs=[pl.BlockSpec(memory_space=pltpu.SMEM)]
        + [pl.BlockSpec((ADD_TABS, 1, 1, count), lambda t: (t, slot, 0, 0))] * part_count
        + [pl.BlockSpec((ADD_TABS, 1, pad_dim, count), lambda t: (t, slot, 0, 0))] * part_count
        + [block if accumulate else anywhere] * len(whole)
        + [anywhere] * len(after),
        out_specs=[block, pl.BlockSpec((8, 128), lambda t: (0, 0))],
        scratch_shapes=[pltpu.VMEM((ADD_LOW // 128, embed_dim * (share // ADD_LOW), 128), F32)],
        out_shape=[
            jax.ShapeDtypeStruct((slot_count, embed_dim, share), F32),
            jax.ShapeDtypeStruct((8, 128), F32),
        ],
        input_output_aliases={1 + 2 * part_count: 0} if whole else {},
        compiler_params=params(40),
        cost_estimate=cost(
            2 * part_count * tab_count * count * share * embed_dim,
            2 * embed_dim * (2 * share + part_count * tab_count * count),
        ),
        name="add_rows",
    )(base, *wanted, *grads, *whole, *after)
    return table_grad, token[0, 0]


def row_sums(value):
    part = value[:, :128]
    for first in range(128, value.shape[1], 128):
        part = part + value[:, first : first + 128]
    return jnp.sum(part.T, axis=0, keepdims=True)


def dense_kernel(
    dense_width,
    width,
    starts,
    after_count,
    place_ref,
    bias_ref,
    *refs,
):
    group_count = len(starts)
    arrived_refs = refs[:group_count]
    first = group_count + 4
    dense_refs = refs[group_count:first] + refs[first + after_count :]
    dense_body(dense_width, width, starts, place_ref, bias_ref, arrived_refs, *dense_refs)


def dense_body(
    dense_width,
    width,
    starts,
    place_ref,
    bias_ref,
    arrived_refs,
    dense_ref,
    label_ref,
    weight_hbm,
    cols_ref,
    logits_ref,
    dense_grad_ref,
    slots_ref,
    left_ref,
    right_ref,
    sums_ref,
    weight,
    anchor,
    current,
    update,
    first_pre,
    second_pre,
    grad_anchor,
    grad_current,
    sems,
):
    layer_count = update.shape[0]
    tower1, tower2 = layer_count, layer_count + 1
    pad_dim = arrived_refs[0].shape[2]
    field_count = place_ref.shape[0]
    embed_dim = (width - dense_width) // field_count
    slot_count = sum(ref.shape[1] for ref in arrived_refs)
    size, cols = anchor.shape
    spans = [pl.ds(first, CHUNK) for first in range(0, size, CHUNK)]
    copies = [
        pltpu.make_async_copy(weight_hbm.at[at], weight.at[at], sems.at[at])
        for at in range(layer_count + 2)
    ]
    for copy in copies:
        copy.start()

    def column(at, span):
        return cols_ref[span, at : at + 1]

    def times(at, span, operand):
        return jnp.dot(weight[at, span, :], operand[...], preferred_element_type=F32)

    def transposed_times(at, span, operand):
        return lax.dot_general(weight[at, :, span], operand[...], TN, preferred_element_type=F32)

    anchor[0:16] = dense_ref[...]
    tail = width // 8 * 8
    anchor[tail:] = jnp.zeros((size - tail, cols), F32)
    for field in range(field_count):
        first = dense_width + field * embed_dim
        tab = place_ref[field] // slot_count
        slot = place_ref[field] - tab * slot_count
        value = arrived_refs[0][tab, jnp.minimum(slot, arrived_refs[0].shape[1] - 1)]
        for begin, ref in zip(starts[1:], arrived_refs[1:]):
            other = ref[tab, jnp.clip(slot - begin, 0, ref.shape[1] - 1)]
            value = jnp.where(slot >= begin, other, value)
        anchor[first : first + embed_dim] = value.astype(F32)[:embed_dim]
    for span in spans:
        left_ref[0, span] = anchor[span].astype(BF)
        left_ref[tower1, span] = anchor[span].astype(BF)
    for layer in range(layer_count):
        copies[layer].wait()
        for span in spans:
            value = transposed_times(layer, span, left_ref.at[layer]) + column(layer, span)
            update[layer, span] = value
            before = anchor if layer == 0 else current
            after = anchor[span] * value + before[span]
            current[span] = after
            if layer + 1 < layer_count:
                left_ref[layer + 1, span] = after.astype(BF)
    copies[tower1].wait()
    for span in spans:
        value = transposed_times(tower1, span, left_ref.at[0]) + column(tower1, span)
        first_pre[span] = value
        left_ref[tower2, span] = (value * jax.nn.sigmoid(value)).astype(BF)
    copies[tower2].wait()
    logits = jnp.full((1, cols), bias_ref[0], F32)
    for span in spans:
        value = transposed_times(tower2, span, left_ref.at[tower2]) + column(tower2, span)
        second_pre[span] = value
        act = value * jax.nn.sigmoid(value)
        terms = current[span] * column(layer_count + 2, span) + act * column(layer_count + 3, span)
        logits = logits + jnp.sum(terms, axis=0, keepdims=True)
    logits_ref[...] = logits
    target = label_ref[...]
    residue = jax.nn.sigmoid(logits) - target
    softplus = jnp.maximum(logits, 0.0) + jnp.log1p(jnp.exp(-jnp.abs(logits)))
    sums_ref[layer_count + 4 :, :] = jnp.zeros((sums_ref.shape[0] - layer_count - 4, size), F32)
    loss_row = jnp.sum(softplus - target * logits, axis=1, keepdims=True)
    bias_row = jnp.sum(residue, axis=1, keepdims=True)
    sums_ref[layer_count + 4 : layer_count + 5, 0:128] = jnp.broadcast_to(loss_row, (1, 128))
    sums_ref[layer_count + 4 : layer_count + 5, 128:256] = jnp.broadcast_to(bias_row, (1, 128))
    for span in spans:
        value = second_pre[span]
        sig = jax.nn.sigmoid(value)
        act = value * sig
        grad = residue * column(layer_count + 3, span) * (sig * (1.0 + value * (1.0 - sig)))
        low = grad.astype(BF)
        right_ref[tower2, span] = low
        sums_ref[tower2 : tower2 + 1, span] = row_sums(low.astype(F32))
        sums_ref[layer_count + 3 : layer_count + 4, span] = row_sums(residue * act)
        sums_ref[layer_count + 2 : layer_count + 3, span] = row_sums(residue * current[span])
        grad_current[span] = residue * column(layer_count + 2, span)
    for span in spans:
        value = first_pre[span]
        sig = jax.nn.sigmoid(value)
        grad = times(tower2, span, right_ref.at[tower2]) * (sig * (1.0 + value * (1.0 - sig)))
        low = grad.astype(BF)
        right_ref[tower1, span] = low
        sums_ref[tower1 : tower1 + 1, span] = row_sums(low.astype(F32))
    for span in spans:
        grad_anchor[span] = times(tower1, span, right_ref.at[tower1])
    for layer in reversed(range(layer_count)):
        for span in spans:
            grad = grad_current[span]
            low = (anchor[span] * grad).astype(BF)
            right_ref[layer, span] = low
            sums_ref[layer : layer + 1, span] = row_sums(low.astype(F32))
            grad_anchor[span] += grad * update[layer, span]
        for span in spans:
            grad_current[span] += times(layer, span, right_ref.at[layer])
    for span in spans:
        grad_anchor[span] += grad_current[span]
    dense_grad_ref[...] = grad_anchor[0:16]
    slots_ref[...] = jnp.zeros_like(slots_ref)
    for field in range(field_count):
        first = dense_width + field * embed_dim
        slots_ref[place_ref[field], :embed_dim] = grad_anchor[first : first + embed_dim].astype(BF)


def dense_step(arrived, starts, place, dense_in, labels, weights, cols, out_b, layer_count, width, after):
    tab_count, _, pad_dim, count = arrived[0].shape
    slot_count = tab_count * sum(part.shape[1] for part in arrived)
    dense_width = dense_in.shape[1]
    size = weights.shape[1]
    matrix_count = layer_count + 2
    dense_rows = jnp.pad(dense_in.T.astype(F32), ((0, 16 - dense_width), (0, 0)))
    vmem = pl.BlockSpec(memory_space=pltpu.VMEM)
    smem = pl.BlockSpec(memory_space=pltpu.SMEM)
    flat = pltpu.VMEM((size, count), F32)
    return pl.pallas_call(
        functools.partial(dense_kernel, dense_width, width, starts, len(after)),
        in_specs=[smem, smem] + [vmem] * (len(arrived) + 2) + [ pl.BlockSpec(memory_space=pl.ANY), vmem]
        + [pl.BlockSpec(memory_space=pl.ANY)] * len(after),
        out_specs=[vmem] * 6,
        out_shape=[
            jax.ShapeDtypeStruct((1, count), F32),
            jax.ShapeDtypeStruct((16, count), F32),
            jax.ShapeDtypeStruct((slot_count, pad_dim, count), BF),
            jax.ShapeDtypeStruct((matrix_count, size, count), BF),
            jax.ShapeDtypeStruct((matrix_count, size, count), BF),
            jax.ShapeDtypeStruct((8, size), F32),
        ],
        scratch_shapes=[
            pltpu.VMEM(weights.shape, BF),
            flat,
            flat,
            pltpu.VMEM((layer_count, size, count), F32),
            flat,
            flat,
            flat,
            flat,
            pltpu.SemaphoreType.DMA((matrix_count,)),
        ],
        compiler_params=params(60),
        cost_estimate=cost(4 * matrix_count * size * size * count, 2 * weights.size + 30 * size * count),
        name="dense",
    )(
        place,
        out_b.astype(F32).reshape(1),
        *arrived,
        dense_rows,
        labels.astype(F32).reshape(1, count),
        weights,
        cols,
        *after,
    )


def chunk_place(piece, swapped):
    if not swapped:
        return piece
    return (piece & 3) | ((piece & 4) << 1) | ((piece & 8) >> 1)


def weight_kernel(core, own_ref, left_ref, right_ref, out_ref, *refs):
    pieces = MAIN // PIECE // 2
    half = MAIN // 2
    moved = refs[-1]
    for at in range(pieces):
        first = pl.multiple_of(((core * pieces + at) ^ own_ref[0]) * PIECE, PIECE)
        moved[at * PIECE : (at + 1) * PIECE] = left_ref[0, pl.ds(first, PIECE), :]
    product = lax.dot_general(
        moved[...], right_ref[0, :MAIN, :], NT, preferred_element_type=F32
    ).astype(out_ref.dtype)
    for chunk in range(2):
        for at in range(pieces):
            out_ref[chunk, chunk_place(at, chunk == 1), 0] = product[
                at * PIECE : (at + 1) * PIECE, chunk * half : (chunk + 1) * half
            ]
    if core == 0:
        strip_ref = refs[0]
        below = lax.dot_general(
            left_ref[0, MAIN : MAIN + 16, :], right_ref[0], NT, preferred_element_type=F32
        )
        beside = lax.dot_general(
            right_ref[0, MAIN : MAIN + 16, :], left_ref[0], NT, preferred_element_type=F32
        )
        strip_ref[0, 0:3] = below[0:3]
        strip_ref[0, 3:6] = beside[0:3]
        strip_ref[0, 6:8] = jnp.zeros((2, strip_ref.shape[2]), F32)


def weight_parts(left, right, own, core):
    matrix_count, size, count = left.shape
    half = MAIN // 2
    pieces = MAIN // PIECE // 2
    out_specs = [pl.BlockSpec((2, pieces, 1, PIECE, half), lambda m: (0, 0, m, 0, 0))]
    shapes = [jax.ShapeDtypeStruct((2, pieces, matrix_count, PIECE, half), BF if core else F32)]
    if core == 0:
        out_specs.append(pl.BlockSpec((1, 8, size), lambda m: (m, 0, 0)))
        shapes.append(jax.ShapeDtypeStruct((matrix_count, 8, size), F32))
    outs = pl.pallas_call(
        functools.partial(weight_kernel, core),
        grid=(matrix_count,),
        in_specs=[
            pl.BlockSpec(memory_space=pltpu.SMEM),
            pl.BlockSpec((1, size, count), lambda m: (m, 0, 0)),
            pl.BlockSpec((1, size, count), lambda m: (m, 0, 0)),
        ],
        out_specs=out_specs,
        out_shape=shapes,
        scratch_shapes=[pltpu.VMEM((half, count), BF)],
        compiler_params=params(60),
        cost_estimate=cost(matrix_count * size * size * count, 5 * matrix_count * size * size),
        name="weight_parts",
    )(own, left, right)
    return [outs[0].reshape((2, 2, 2, 2, 2, matrix_count, PIECE, half))] + list(outs[1:])


HALVES = [[("rep", 2), ("tab", 1)], [("tab", 1), ("rep", 2)]]
FAR = [(0, 1), (1, 0), (1, 1)]


def added(parts, *gates):
    value = parts[0].astype(F32)
    for other in parts[1:]:
        value = value + other.astype(F32)
    for gate in gates:
        value = value + gate
    return value


def joined(parts, token):
    one = (1.0 + token).astype(BF)
    return jnp.stack([part * one for part in parts], axis=1)


def pack(small, total_rows):
    rounded = lax.reduce_precision(small, 8, 7)
    rest = small[-total_rows:] - rounded[-total_rows:]
    return jnp.concatenate([rounded.astype(BF), rest.astype(BF)], axis=0)


def small_sum(small, total_rows, sends):
    packed = pack(small, total_rows)
    rounded = lax.reduce_precision(small, 8, 7)
    rest = lax.reduce_precision(small[-total_rows:] - rounded[-total_rows:], 8, 7)
    terms = [(rounded, rest)]
    for send in sends:
        got = send(packed).astype(F32)
        terms.append((got[:-total_rows], got[-total_rows:]))
    while len(terms) > 1:
        terms = [
            (left[0] + right[0], left[1] + right[1]) for left, right in zip(terms[::2], terms[1::2])
        ]
    total, rest = terms[0]
    return jnp.concatenate([total[:-total_rows], total[-total_rows:] + rest], axis=0)


def assemble_kernel(layer_count, own_ref, *refs):
    blocks = refs[:10]
    strip_ref, cross_ref, first_ref, second_ref = refs[10:]
    matrix = pl.program_id(0)

    def fill(out_ref):
        def put(core, chunk, upper, at, value):
            rows, lanes = value.shape
            piece = 16 * core + chunk_place(4 * upper + at, chunk == 1)
            first = pl.multiple_of((piece ^ own_ref[0]) * rows, rows)
            out_ref[0, pl.ds(first, rows), chunk * lanes : (chunk + 1) * lanes] = value.astype(F32)

        for core in range(2):
            refs_here = blocks[5 * core : 5 * core + 5]
            for at in range(4):
                for ref, uppers in zip(refs_here[:3], ((0, 0), (1, 2), (2, 1))):
                    for chunk in range(2):
                        put(core, chunk, uppers[chunk], at, ref[chunk, at, 0])
                for chunk in range(2):
                    put(core, chunk, 3, at, refs_here[3 + chunk][at, 0])
        height, width = out_ref.shape[1:]
        if width > MAIN:
            extra = width - MAIN
            for first in range(0, MAIN, 128):
                turned = strip_ref[0, :, first : first + 128].T
                out_ref[0, first : first + 128, MAIN:] = turned[:, 3 : 3 + extra]
        if height > MAIN:
            out_ref[0, MAIN:, :] = strip_ref[0, 0 : height - MAIN, :width]

    @pl.when(matrix < layer_count)
    def _():
        fill(cross_ref)

    @pl.when(matrix == layer_count)
    def _():
        fill(first_ref)

    @pl.when(matrix == layer_count + 1)
    def _():
        fill(second_ref)


def assemble(blocks, strips, own, layer_count, width, hidden):
    matrix_count = layer_count + 2
    size = strips.shape[2]
    both = pl.BlockSpec(blocks[0].shape[:2] + (1,) + blocks[0].shape[3:], lambda m: (0, 0, m, 0, 0))
    single = pl.BlockSpec(blocks[3].shape[:1] + (1,) + blocks[3].shape[2:], lambda m: (0, m, 0, 0))
    return pl.pallas_call(
        functools.partial(assemble_kernel, layer_count),
        grid=(matrix_count,),
        in_specs=[pl.BlockSpec(memory_space=pltpu.SMEM)]
        + ([both] * 3 + [single] * 2) * 2
        + [pl.BlockSpec((1, 8, size), lambda m: (m, 0, 0))],
        out_specs=[
            pl.BlockSpec((1, width, width), lambda m: (jnp.minimum(m, layer_count - 1), 0, 0)),
            pl.BlockSpec((1, width, hidden), lambda m: (0, 0, 0)),
            pl.BlockSpec((1, hidden, hidden), lambda m: (0, 0, 0)),
        ],
        out_shape=[
            jax.ShapeDtypeStruct((layer_count, width, width), F32),
            jax.ShapeDtypeStruct((1, width, hidden), F32),
            jax.ShapeDtypeStruct((1, hidden, hidden), F32),
        ],
        compiler_params=params(56),
        cost_estimate=cost(0, 6 * matrix_count * size * size),
        name="assemble",
    )(own, *blocks, strips)


def on_device(
    ids,
    table_rows,
    table_place,
    dense_in,
    labels,
    tables,
    cross_w,
    cross_b,
    tower1_w,
    tower1_b,
    tower2_w,
    tower2_b,
    out_w,
    out_b,
):
    tab_count = lax.axis_size("tab")
    rep_count = lax.axis_size("rep")
    slot_count, embed_dim, table_len = tables.shape
    row_count, dense_width = dense_in.shape
    field_count = ids.shape[1]
    layer_count, width = cross_w.shape[:2]
    hidden = tower1_w.shape[0]
    size = round_up(width, 128)
    all_slots = slot_count * tab_count
    tab_at = lax.axis_index("tab")
    rep_at = lax.axis_index("rep")

    matches = table_place[:, None] == jnp.arange(all_slots, dtype=I32)[None, :]
    effective = ids % table_rows[None, :]
    by_slot = jnp.sum(jnp.where(matches[:, :, None], effective.T[:, None, :], 0), axis=0)
    slot_rows = jnp.sum(jnp.where(matches, table_rows[:, None], 0), axis=0)
    own_rows = lax.dynamic_slice_in_dim(slot_rows, tab_at * slot_count, slot_count)
    wanted = lax.all_to_all(
        by_slot.reshape(tab_count, slot_count, row_count), "tab", split_axis=0, concat_axis=0, tiled=True
    )
    listed = jnp.transpose(wanted, (1, 0, 2)).reshape(-1)

    first_size = slot_count % LOOK_SLOTS
    starts = ([0] if first_size else []) + list(range(first_size, slot_count, LOOK_SLOTS))
    arrived = []
    for begin in starts:
        looked = lookup(
            tables, listed, own_rows, tab_count, begin, LOOK_SLOTS if begin or not first_size else first_size
        )
        arrived.append(lax.all_to_all(looked, "tab", split_axis=0, concat_axis=0, tiled=True))

    ready = 1.0 + arrived[0][0, 0, embed_dim, 0]

    def padded(weight):
        return jnp.pad(weight * ready, ((0, size - weight.shape[0]), (0, size - weight.shape[1])))

    weights = jnp.stack(
        [padded(cross_w[at]) for at in range(layer_count)] + [padded(tower1_w.T), padded(tower2_w)]
    )
    vectors = [cross_b[at] for at in range(layer_count)]
    vectors += [tower1_b, tower2_b, out_w[:width], out_w[width:], out_w[:0]]
    cols = jnp.stack(
        [jnp.pad((v * ready).astype(F32), (0, size - v.shape[0])) for v in vectors], axis=1
    )


    def near_parts(own):
        return [own, swap(own, "rep", 1)]

    def far_bases(own):
        bases = [own]
        for mask in masks_of("rep")[1:]:
            bases = bases + [swap(part, "rep", mask) for part in bases]
        return bases[1:]

    def far_parts(bases):
        return [part for far in bases for part in near_parts(far)]

    wanted = wanted + (ready - 1.0).astype(I32)
    near_ids = [part[:, :, None, :] for part in near_parts(wanted)]
    far_ids = [part[:, :, None, :] for part in far_parts(far_bases(wanted))]
    logits, dense_grad, slots, left, right, sums = dense_step(
        arrived, starts, table_place, dense_in, labels, weights, cols, out_b, layer_count, width,
        near_ids + far_ids,
    )
    returned = lax.all_to_all(
        slots.reshape(tab_count, slot_count, slots.shape[1], row_count),
        "tab",
        split_axis=0,
        concat_axis=0,
        tiled=True,
    )

    share = table_len // rep_count
    base = (rep_at * share).astype(I32).reshape(1)

    def gate(value, result):
        return value * (1.0 + 0.0 * result.astype(F32)).astype(value.dtype)

    bits = [rep_at & 1, (rep_at >> 1) & 1, tab_at & 1, (tab_at >> 2) & 1, (tab_at >> 1) & 1]
    own = sum(bit << (4 - at) for at, bit in enumerate(bits)).astype(I32).reshape(1)
    (send,) = weight_parts(left, right, own, 1)
    keep, strips = weight_parts(left, right, own, 0)
    matrix_count = layer_count + 2
    far_grads = None
    table_grad = None
    token = jnp.zeros((), F32)
    near_jobs = list(range(slot_count))[::-1]
    far_jobs = list(range(slot_count))[::-1]

    def add_next(near, times, after):
        nonlocal table_grad, token
        jobs = near_jobs if near else far_jobs
        for _ in range(min(times, len(jobs))):
            table_grad, token = add_rows(
                near_grads if near else far_grads,
                near_ids if near else far_ids,
                base,
                share,
                embed_dim,
                jobs.pop(),
                table_grad,
                not near,
                after,
            )

    def zero_of(value):
        return 0.0 * value.astype(F32)

    small = jnp.concatenate([strips.reshape(matrix_count * 8, size), sums], axis=0)
    total_rows = sums.shape[0]

    def small_step(value, masks):
        return small_sum(
            value, total_rows, [functools.partial(swap_both, rep_mask=r, tab_mask=t) for r, t in masks]
        )

    got = swap(send, "rep", 1)
    ahead = [added((keep[at, 1, 1], got[at, 1, 1])).astype(BF) for at in range(2)]
    first = [swap(ahead[at], *HALVES[at][0]) for at in range(2)]
    small = small_step(small + zero_of(ahead[0][0, 0, 0, 0, 0]) + zero_of(ahead[1][0, 0, 0, 0, 0]), [(1, 0)])
    small = small_step(small, [(2, 0), (0, 1), (2, 1)])
    keep, got, _ = lax.optimization_barrier((keep, got, ahead))
    behind = [added((keep[at, 1, 0], got[at, 1, 0])).astype(BF) for at in range(2)]
    later = [swap(behind[at], *HALVES[at][0]) for at in range(2)]
    keep, got, _ = lax.optimization_barrier((keep, got, behind))
    kept = [added((keep[at, 0], got[at, 0])) for at in range(2)]
    ready = zero_of(small[0, 0])
    sends = [added((kept[at][1], first[at]), ready).astype(BF) for at in range(2)]
    sent = [swap(sends[at], *HALVES[at][1]) for at in range(2)]
    returned = gate(returned, sends[0][0, 0, 0, 0, 0] + sends[1][0, 0, 0, 0, 0])
    near_grads = near_parts(returned)
    add_next(True, 1, behind + sends)
    bases = far_bases(gate(returned, token))
    add_next(True, NEAR_FIRST - 1, sends)
    sources = [[kept[at][0], later[at], sent[at]] for at in range(2)]

    def take_far(high, low):
        both = [added([part[high, low] for part in sources[at]], token) for at in range(2)]
        return jnp.stack(both)

    kept = take_far(0, 0)
    sends = [take_far(high, low).astype(BF) for high, low in FAR]
    far = [swap(value, "tab", 4 * high + 2 * low) for value, (high, low) in zip(sends, FAR)]
    add_next(True, slot_count, [kept] + sends)
    piece = added([kept, *far], token).astype(BF)
    for axis, known in (("rep", 2), ("tab", 3)):
        for mask in masks_of(axis)[known:]:
            piece = (piece.astype(F32) + swap(piece, axis, mask).astype(F32)).astype(BF)
    parts = [piece, swap(piece, "tab", 2), swap(piece, "tab", 4), swap(piece, "tab", 6)]
    far_grads = far_parts([gate(part, piece[0, 0, 0, 0]) for part in bases])
    add_next(False, FAR_FIRST, [piece])
    values = joined(parts, token)
    from_y = swap(values, "tab", 1)
    from_x = swap(values, "rep", 2)
    small = small + zero_of(values[0, 0, 0, 0, 0])
    small = small_step(small, [(0, 2), (0, 4), (0, 6)])
    for rep_mask in masks_of("rep")[2:]:
        small = small_step(small, [(rep_mask, 0)])
    for tab_mask in masks_of("tab")[3:]:
        small = small_step(small, [(0, tab_mask)])
    add_next(False, 1, [values])
    other = [swap(values, "rep", 1)]
    add_next(False, 1, other)
    token = token + zero_of(small[0, 0])
    last = [swap(from_y[0], "rep", 2), swap(from_x[1], "tab", 1)]
    other += [swap(from_y, "rep", 1), swap(from_x, "rep", 1)]
    add_next(False, slot_count, other)
    last = [gate(part, token) for part in last]
    blocks = [values, from_y, from_x] + last + other + [swap(part, "rep", 1) for part in last]

    strips = small[:-8].reshape(matrix_count, 8, size)
    sums = small[-8:]
    cross_w_grad, tower1_w_grad, tower2_w_grad = assemble(
        blocks, strips, own, layer_count, width, hidden
    )
    scalars = sums[layer_count + 4]
    return (
        scalars[0] / (row_count * tab_count * rep_count),
        logits.reshape(row_count),
        dense_grad[:dense_width].T,
        cross_w_grad,
        sums[:layer_count, :width],
        tower1_w_grad[0].T,
        sums[layer_count, :hidden],
        tower2_w_grad[0],
        sums[layer_count + 1, :hidden],
        jnp.concatenate([sums[layer_count + 2, :width], sums[layer_count + 3, :hidden]]),
        scalars[128],
        table_grad,
    )


def solution(mesh):
    placed = (
        P(("tab", "rep"), None),
        P(),
        P(),
        P(("tab", "rep"), None),
        P(("tab", "rep")),
        P("tab", None, None),
        P(),
        P(),
        P(),
        P(),
        P(),
        P(),
        P(),
        P(),
    )
    return jax.shard_map(
        on_device,
        mesh=mesh,
        in_specs=placed,
        out_specs=(
            P(),
            P(("tab", "rep")),
            P(("tab", "rep"), None),
            P(),
            P(),
            P(),
            P(),
            P(),
            P(),
            P(),
            P(),
            P("tab", None, "rep"),
        ),
        check_vma=False,
    )
```

```python
import functools

import jax
import jax.numpy as jnp
from jax import lax
from jax.experimental import pallas as pl
from jax.experimental.pallas import tpu as pltpu
from jax.sharding import PartitionSpec as P

BF = jnp.bfloat16
F32 = jnp.float32
I32 = jnp.int32
LOOK_SLOTS = 3
LOOK_LANES = 40
LOOK_BLOCKS = 8
LOOK_ROWS = 32
ADD_LOW = 512
ADD_TABS = 4
NEAR_FIRST = 2
FAR_FIRST = 2
MAIN = 1024
CHUNK = 384
PIECE = 32
MIB = 1024 * 1024
NT = (((1,), (1,)), ((), ()))
TN = (((0,), (0,)), ((), ()))


def round_up(size, unit):
    return -(-size // unit) * unit


def params(mib):
    return pltpu.CompilerParams(vmem_limit_bytes=mib * MIB)


def cost(flops, size):
    return pl.CostEstimate(flops=flops // 1000, bytes_accessed=size // 1000, transcendentals=0)


def swap(value, axis, mask):
    return lax.ppermute(value, axis, [(at, at ^ mask) for at in range(lax.axis_size(axis))])


def swap_both(value, rep_mask, tab_mask):
    rep_count = lax.axis_size("rep")
    perm = []
    for tab in range(lax.axis_size("tab")):
        for at in range(rep_count):
            perm.append((tab * rep_count + at, (tab ^ tab_mask) * rep_count + (at ^ rep_mask)))
    return lax.ppermute(value, ("tab", "rep"), perm)


def masks_of(axis):
    size = lax.axis_size(axis)
    return [1 << bit for bit in range(size.bit_length() - 1)]


def lookup_kernel(first_slot, ids_ref, rows_ref, table_hbm, out_ref, raw, stack, major, picked, sems):
    tab_count, slot_count, pad_dim, count = out_ref.shape
    embed_dim = raw.shape[1]
    total = tab_count * count
    copies = [
        pltpu.make_async_copy(table_hbm.at[first_slot + at], raw.at[at], sems.at[at])
        for at in range(slot_count)
    ]
    for copy in copies:
        copy.start()
    lane = lax.broadcasted_iota(I32, (1, 128), 1)
    stack[...] = jnp.zeros_like(stack)
    most = jnp.maximum(rows_ref[first_slot], 1)
    for at in range(1, slot_count):
        most = jnp.maximum(most, rows_ref[first_slot + at])
    for copy in copies:
        copy.wait()
    unit = 128 * LOOK_BLOCKS

    @pl.loop(0, (most + unit - 1) // unit)
    def _(step):
        for block in range(LOOK_BLOCKS):
            first = pl.multiple_of((step * LOOK_BLOCKS + block) * 128, 128)
            for at in range(slot_count):
                stack[block, at * LOOK_LANES : at * LOOK_LANES + embed_dim, :] = raw[
                    at, :, pl.ds(first, 128)
                ].astype(F32)
            major[pl.ds(first, 128), :] = stack[block].T

    @pl.loop(0, total // LOOK_ROWS)
    def _(step):
        base = step * LOOK_ROWS
        starts = [(first_slot + at) * total + base for at in range(slot_count)]
        for row in range(LOOK_ROWS):
            value = None
            for at in reversed(range(slot_count)):
                one = major[pl.ds(ids_ref[starts[at] + row], 1), :]
                value = one if value is None else jnp.where(lane < (at + 1) * LOOK_LANES, one, value)
            picked[pl.ds(base + row, 1), :] = value

    @pl.loop(0, tab_count)
    def _(tab):
        for block in range(0, count, 128):
            turned = picked[pl.ds(pl.multiple_of(tab * count + block, 128), 128), :].T
            for at in range(slot_count):
                rows = turned[at * LOOK_LANES : at * LOOK_LANES + pad_dim]
                out_ref[tab, at, :, block : block + 128] = rows.astype(BF)


def lookup(tables, wanted, own_rows, tab_count, first_slot, slot_count):
    all_count, embed_dim, table_len = tables.shape
    count = wanted.shape[0] // (all_count * tab_count)
    smem = pl.BlockSpec(memory_space=pltpu.SMEM)
    return pl.pallas_call(
        functools.partial(lookup_kernel, first_slot),
        in_specs=[smem, smem, pl.BlockSpec(memory_space=pl.ANY)],
        out_specs=pl.BlockSpec(memory_space=pltpu.VMEM),
        out_shape=jax.ShapeDtypeStruct((tab_count, slot_count, round_up(embed_dim, 8), count), BF),
        scratch_shapes=[
            pltpu.VMEM((slot_count, embed_dim, table_len), BF),
            pltpu.VMEM((LOOK_BLOCKS, 128, 128), F32),
            pltpu.VMEM((table_len, 128), F32),
            pltpu.VMEM((tab_count * count, 128), F32),
            pltpu.SemaphoreType.DMA((slot_count,)),
        ],
        compiler_params=params(56),
        cost_estimate=cost(
            600 * tab_count * count * table_len * slot_count // 8,
            2 * slot_count * embed_dim * (table_len + tab_count * count),
        ),
        name="lookup",
    )(wanted, own_rows, tables)


def add_kernel(part_count, has_before, base_ref, *refs):
    ids_refs = refs[:part_count]
    grad_refs = refs[part_count : 2 * part_count]
    before_ref = refs[2 * part_count] if has_before else None
    out_ref, token_ref, total = refs[-3:]
    step = pl.program_id(0)
    embed_dim = out_ref.shape[1]
    cols = grad_refs[0].shape[3]
    high_count = total.shape[1] // embed_dim

    @pl.when(step == 0)
    def _():
        total[...] = jnp.zeros_like(total)
        token_ref[...] = jnp.zeros_like(token_ref)

    high_iota = lax.broadcasted_iota(I32, (high_count, cols), 0)
    low_iota = lax.broadcasted_iota(I32, (ADD_LOW, cols), 0)
    product = None
    for ids_ref, grad_ref in zip(ids_refs, grad_refs):
        for tab in range(ids_ref.shape[0]):
            local = ids_ref[tab, 0] - base_ref[0]
            high = lax.shift_right_arithmetic(local, ADD_LOW.bit_length() - 1)
            low = local & (ADD_LOW - 1)
            high_hot = jnp.where(high_iota == high, 1.0, 0.0)
            low_hot = jnp.where(low_iota == low, 1.0, 0.0).astype(BF)
            grads = grad_ref[tab, 0, :embed_dim].astype(F32)
            left = (grads[:, None, :] * high_hot[None, :, :]).astype(BF)
            left = left.reshape(embed_dim * high_count, cols)
            term = lax.dot_general(left, low_hot, NT, preferred_element_type=F32)
            product = term if product is None else product + term
    for lane in range(ADD_LOW // 128):
        total[lane] += product[:, lane * 128 : (lane + 1) * 128]

    @pl.when(step == pl.num_programs(0) - 1)
    def _():
        for at in range(high_count):
            for part in range(0, embed_dim, 8):
                size = min(8, embed_dim - part)
                for lane in range(ADD_LOW // 128):
                    first = at * ADD_LOW + lane * 128
                    value = total[lane, pl.ds(part * high_count + at, size, stride=high_count), :]
                    if before_ref is not None:
                        value = value + before_ref[0, part : part + size, first : first + 128]
                    out_ref[0, part : part + size, first : first + 128] = value


def add_rows(grads, wanted, base, share, embed_dim, slot, so_far, accumulate, after):
    tab_count, slot_count, pad_dim, count = grads[0].shape
    part_count = len(grads)
    anywhere = pl.BlockSpec(memory_space=pl.ANY)
    block = pl.BlockSpec((1, embed_dim, share), lambda t: (slot, 0, 0))
    whole = [] if so_far is None else [so_far]
    table_grad, token = pl.pallas_call(
        functools.partial(add_kernel, part_count, accumulate),
        grid=(tab_count // ADD_TABS,),
        in_specs=[pl.BlockSpec(memory_space=pltpu.SMEM)]
        + [pl.BlockSpec((ADD_TABS, 1, 1, count), lambda t: (t, slot, 0, 0))] * part_count
        + [pl.BlockSpec((ADD_TABS, 1, pad_dim, count), lambda t: (t, slot, 0, 0))] * part_count
        + [block if accumulate else anywhere] * len(whole)
        + [anywhere] * len(after),
        out_specs=[block, pl.BlockSpec((8, 128), lambda t: (0, 0))],
        scratch_shapes=[pltpu.VMEM((ADD_LOW // 128, embed_dim * (share // ADD_LOW), 128), F32)],
        out_shape=[
            jax.ShapeDtypeStruct((slot_count, embed_dim, share), F32),
            jax.ShapeDtypeStruct((8, 128), F32),
        ],
        input_output_aliases={1 + 2 * part_count: 0} if whole else {},
        compiler_params=params(40),
        cost_estimate=cost(
            2 * part_count * tab_count * count * share * embed_dim,
            2 * embed_dim * (2 * share + part_count * tab_count * count),
        ),
        name="add_rows",
    )(base, *wanted, *grads, *whole, *after)
    return table_grad, token[0, 0]


def row_sums(value):
    part = value[:, :128]
    for first in range(128, value.shape[1], 128):
        part = part + value[:, first : first + 128]
    return jnp.sum(part.T, axis=0, keepdims=True)


def dense_kernel(
    dense_width,
    width,
    starts,
    after_count,
    place_ref,
    bias_ref,
    *refs,
):
    group_count = len(starts)
    arrived_refs = refs[:group_count]
    first = group_count + 4
    dense_refs = refs[group_count:first] + refs[first + after_count :]
    dense_body(dense_width, width, starts, place_ref, bias_ref, arrived_refs, *dense_refs)


def dense_body(
    dense_width,
    width,
    starts,
    place_ref,
    bias_ref,
    arrived_refs,
    dense_ref,
    label_ref,
    weight_hbm,
    cols_ref,
    logits_ref,
    dense_grad_ref,
    slots_ref,
    left_ref,
    right_ref,
    sums_ref,
    weight,
    anchor,
    current,
    update,
    first_pre,
    second_pre,
    grad_anchor,
    grad_current,
    sems,
):
    layer_count = update.shape[0]
    tower1, tower2 = layer_count, layer_count + 1
    pad_dim = arrived_refs[0].shape[2]
    field_count = place_ref.shape[0]
    embed_dim = (width - dense_width) // field_count
    slot_count = sum(ref.shape[1] for ref in arrived_refs)
    size, cols = anchor.shape
    spans = [pl.ds(first, CHUNK) for first in range(0, size, CHUNK)]
    copies = [
        pltpu.make_async_copy(weight_hbm.at[at], weight.at[at], sems.at[at])
        for at in range(layer_count + 2)
    ]
    for copy in copies:
        copy.start()

    def column(at, span):
        return cols_ref[span, at : at + 1]

    def times(at, span, operand):
        return jnp.dot(weight[at, span, :], operand[...], preferred_element_type=F32)

    def transposed_times(at, span, operand):
        return lax.dot_general(weight[at, :, span], operand[...], TN, preferred_element_type=F32)

    anchor[0:16] = dense_ref[...]
    tail = width // 8 * 8
    anchor[tail:] = jnp.zeros((size - tail, cols), F32)
    for field in range(field_count):
        first = dense_width + field * embed_dim
        tab = place_ref[field] // slot_count
        slot = place_ref[field] - tab * slot_count
        value = arrived_refs[0][tab, jnp.minimum(slot, arrived_refs[0].shape[1] - 1)]
        for begin, ref in zip(starts[1:], arrived_refs[1:]):
            other = ref[tab, jnp.clip(slot - begin, 0, ref.shape[1] - 1)]
            value = jnp.where(slot >= begin, other, value)
        anchor[first : first + embed_dim] = value.astype(F32)[:embed_dim]
    for span in spans:
        left_ref[0, span] = anchor[span].astype(BF)
        left_ref[tower1, span] = anchor[span].astype(BF)
    for layer in range(layer_count):
        copies[layer].wait()
        for span in spans:
            value = transposed_times(layer, span, left_ref.at[layer]) + column(layer, span)
            update[layer, span] = value
            before = anchor if layer == 0 else current
            after = anchor[span] * value + before[span]
            current[span] = after
            if layer + 1 < layer_count:
                left_ref[layer + 1, span] = after.astype(BF)
    copies[tower1].wait()
    for span in spans:
        value = transposed_times(tower1, span, left_ref.at[0]) + column(tower1, span)
        first_pre[span] = value
        left_ref[tower2, span] = (value * jax.nn.sigmoid(value)).astype(BF)
    copies[tower2].wait()
    logits = jnp.full((1, cols), bias_ref[0], F32)
    for span in spans:
        value = transposed_times(tower2, span, left_ref.at[tower2]) + column(tower2, span)
        second_pre[span] = value
        act = value * jax.nn.sigmoid(value)
        terms = current[span] * column(layer_count + 2, span) + act * column(layer_count + 3, span)
        logits = logits + jnp.sum(terms, axis=0, keepdims=True)
    logits_ref[...] = logits
    target = label_ref[...]
    residue = jax.nn.sigmoid(logits) - target
    softplus = jnp.maximum(logits, 0.0) + jnp.log1p(jnp.exp(-jnp.abs(logits)))
    sums_ref[layer_count + 4 :, :] = jnp.zeros((sums_ref.shape[0] - layer_count - 4, size), F32)
    loss_row = jnp.sum(softplus - target * logits, axis=1, keepdims=True)
    bias_row = jnp.sum(residue, axis=1, keepdims=True)
    sums_ref[layer_count + 4 : layer_count + 5, 0:128] = jnp.broadcast_to(loss_row, (1, 128))
    sums_ref[layer_count + 4 : layer_count + 5, 128:256] = jnp.broadcast_to(bias_row, (1, 128))
    for span in spans:
        value = second_pre[span]
        sig = jax.nn.sigmoid(value)
        act = value * sig
        grad = residue * column(layer_count + 3, span) * (sig * (1.0 + value * (1.0 - sig)))
        low = grad.astype(BF)
        right_ref[tower2, span] = low
        sums_ref[tower2 : tower2 + 1, span] = row_sums(low.astype(F32))
        sums_ref[layer_count + 3 : layer_count + 4, span] = row_sums(residue * act)
        sums_ref[layer_count + 2 : layer_count + 3, span] = row_sums(residue * current[span])
        grad_current[span] = residue * column(layer_count + 2, span)
    for span in spans:
        value = first_pre[span]
        sig = jax.nn.sigmoid(value)
        grad = times(tower2, span, right_ref.at[tower2]) * (sig * (1.0 + value * (1.0 - sig)))
        low = grad.astype(BF)
        right_ref[tower1, span] = low
        sums_ref[tower1 : tower1 + 1, span] = row_sums(low.astype(F32))
    for span in spans:
        grad_anchor[span] = times(tower1, span, right_ref.at[tower1])
    for layer in reversed(range(layer_count)):
        for span in spans:
            grad = grad_current[span]
            low = (anchor[span] * grad).astype(BF)
            right_ref[layer, span] = low
            sums_ref[layer : layer + 1, span] = row_sums(low.astype(F32))
            grad_anchor[span] += grad * update[layer, span]
        for span in spans:
            grad_current[span] += times(layer, span, right_ref.at[layer])
    for span in spans:
        grad_anchor[span] += grad_current[span]
    dense_grad_ref[...] = grad_anchor[0:16]
    slots_ref[...] = jnp.zeros_like(slots_ref)
    for field in range(field_count):
        first = dense_width + field * embed_dim
        slots_ref[place_ref[field], :embed_dim] = grad_anchor[first : first + embed_dim].astype(BF)


def dense_step(arrived, starts, place, dense_in, labels, weights, cols, out_b, layer_count, width, after):
    tab_count, _, pad_dim, count = arrived[0].shape
    slot_count = tab_count * sum(part.shape[1] for part in arrived)
    dense_width = dense_in.shape[1]
    size = weights.shape[1]
    matrix_count = layer_count + 2
    dense_rows = jnp.pad(dense_in.T.astype(F32), ((0, 16 - dense_width), (0, 0)))
    vmem = pl.BlockSpec(memory_space=pltpu.VMEM)
    smem = pl.BlockSpec(memory_space=pltpu.SMEM)
    flat = pltpu.VMEM((size, count), F32)
    return pl.pallas_call(
        functools.partial(dense_kernel, dense_width, width, starts, len(after)),
        in_specs=[smem, smem] + [vmem] * (len(arrived) + 2) + [ pl.BlockSpec(memory_space=pl.ANY), vmem]
        + [pl.BlockSpec(memory_space=pl.ANY)] * len(after),
        out_specs=[vmem] * 6,
        out_shape=[
            jax.ShapeDtypeStruct((1, count), F32),
            jax.ShapeDtypeStruct((16, count), F32),
            jax.ShapeDtypeStruct((slot_count, pad_dim, count), BF),
            jax.ShapeDtypeStruct((matrix_count, size, count), BF),
            jax.ShapeDtypeStruct((matrix_count, size, count), BF),
            jax.ShapeDtypeStruct((8, size), F32),
        ],
        scratch_shapes=[
            pltpu.VMEM(weights.shape, BF),
            flat,
            flat,
            pltpu.VMEM((layer_count, size, count), F32),
            flat,
            flat,
            flat,
            flat,
            pltpu.SemaphoreType.DMA((matrix_count,)),
        ],
        compiler_params=params(60),
        cost_estimate=cost(4 * matrix_count * size * size * count, 2 * weights.size + 30 * size * count),
        name="dense",
    )(
        place,
        out_b.astype(F32).reshape(1),
        *arrived,
        dense_rows,
        labels.astype(F32).reshape(1, count),
        weights,
        cols,
        *after,
    )


def chunk_place(piece, swapped):
    if not swapped:
        return piece
    return (piece & 3) | ((piece & 4) << 1) | ((piece & 8) >> 1)


def weight_kernel(core, own_ref, left_ref, right_ref, out_ref, *refs):
    pieces = MAIN // PIECE // 2
    half = MAIN // 2
    moved = refs[-1]
    for at in range(pieces):
        first = pl.multiple_of(((core * pieces + at) ^ own_ref[0]) * PIECE, PIECE)
        moved[at * PIECE : (at + 1) * PIECE] = left_ref[0, pl.ds(first, PIECE), :]
    product = lax.dot_general(
        moved[...], right_ref[0, :MAIN, :], NT, preferred_element_type=F32
    ).astype(out_ref.dtype)
    for chunk in range(2):
        for at in range(pieces):
            out_ref[chunk, chunk_place(at, chunk == 1), 0] = product[
                at * PIECE : (at + 1) * PIECE, chunk * half : (chunk + 1) * half
            ]
    if core == 0:
        strip_ref = refs[0]
        below = lax.dot_general(
            left_ref[0, MAIN : MAIN + 16, :], right_ref[0], NT, preferred_element_type=F32
        )
        beside = lax.dot_general(
            right_ref[0, MAIN : MAIN + 16, :], left_ref[0], NT, preferred_element_type=F32
        )
        strip_ref[0, 0:3] = below[0:3]
        strip_ref[0, 3:6] = beside[0:3]
        strip_ref[0, 6:8] = jnp.zeros((2, strip_ref.shape[2]), F32)


def weight_parts(left, right, own, core):
    matrix_count, size, count = left.shape
    half = MAIN // 2
    pieces = MAIN // PIECE // 2
    out_specs = [pl.BlockSpec((2, pieces, 1, PIECE, half), lambda m: (0, 0, m, 0, 0))]
    shapes = [jax.ShapeDtypeStruct((2, pieces, matrix_count, PIECE, half), BF if core else F32)]
    if core == 0:
        out_specs.append(pl.BlockSpec((1, 8, size), lambda m: (m, 0, 0)))
        shapes.append(jax.ShapeDtypeStruct((matrix_count, 8, size), F32))
    outs = pl.pallas_call(
        functools.partial(weight_kernel, core),
        grid=(matrix_count,),
        in_specs=[
            pl.BlockSpec(memory_space=pltpu.SMEM),
            pl.BlockSpec((1, size, count), lambda m: (m, 0, 0)),
            pl.BlockSpec((1, size, count), lambda m: (m, 0, 0)),
        ],
        out_specs=out_specs,
        out_shape=shapes,
        scratch_shapes=[pltpu.VMEM((half, count), BF)],
        compiler_params=params(60),
        cost_estimate=cost(matrix_count * size * size * count, 5 * matrix_count * size * size),
        name="weight_parts",
    )(own, left, right)
    return [outs[0].reshape((2, 2, 2, 2, 2, matrix_count, PIECE, half))] + list(outs[1:])


HALVES = [[("rep", 2), ("tab", 1)], [("tab", 1), ("rep", 2)]]
FAR = [(0, 1), (1, 0), (1, 1)]


def added(parts, *gates):
    value = parts[0].astype(F32)
    for other in parts[1:]:
        value = value + other.astype(F32)
    for gate in gates:
        value = value + gate
    return value


def joined(parts, token):
    one = (1.0 + token).astype(BF)
    return jnp.stack([part * one for part in parts], axis=1)


def pack(small, total_rows):
    rounded = lax.reduce_precision(small, 8, 7)
    rest = small[-total_rows:] - rounded[-total_rows:]
    return jnp.concatenate([rounded.astype(BF), rest.astype(BF)], axis=0)


def small_sum(small, total_rows, sends):
    packed = pack(small, total_rows)
    rounded = lax.reduce_precision(small, 8, 7)
    rest = lax.reduce_precision(small[-total_rows:] - rounded[-total_rows:], 8, 7)
    terms = [(rounded, rest)]
    for send in sends:
        got = send(packed).astype(F32)
        terms.append((got[:-total_rows], got[-total_rows:]))
    while len(terms) > 1:
        terms = [
            (left[0] + right[0], left[1] + right[1]) for left, right in zip(terms[::2], terms[1::2])
        ]
    total, rest = terms[0]
    return jnp.concatenate([total[:-total_rows], total[-total_rows:] + rest], axis=0)


def assemble_kernel(layer_count, own_ref, *refs):
    blocks = refs[:10]
    strip_ref, cross_ref, first_ref, second_ref = refs[10:]
    matrix = pl.program_id(0)

    def fill(out_ref):
        def put(core, chunk, upper, at, value):
            rows, lanes = value.shape
            piece = 16 * core + chunk_place(4 * upper + at, chunk == 1)
            first = pl.multiple_of((piece ^ own_ref[0]) * rows, rows)
            out_ref[0, pl.ds(first, rows), chunk * lanes : (chunk + 1) * lanes] = value.astype(F32)

        for core in range(2):
            refs_here = blocks[5 * core : 5 * core + 5]
            for at in range(4):
                for ref, uppers in zip(refs_here[:3], ((0, 0), (1, 2), (2, 1))):
                    for chunk in range(2):
                        put(core, chunk, uppers[chunk], at, ref[chunk, at, 0])
                for chunk in range(2):
                    put(core, chunk, 3, at, refs_here[3 + chunk][at, 0])
        height, width = out_ref.shape[1:]
        if width > MAIN:
            extra = width - MAIN
            for first in range(0, MAIN, 128):
                turned = strip_ref[0, :, first : first + 128].T
                out_ref[0, first : first + 128, MAIN:] = turned[:, 3 : 3 + extra]
        if height > MAIN:
            out_ref[0, MAIN:, :] = strip_ref[0, 0 : height - MAIN, :width]

    @pl.when(matrix < layer_count)
    def _():
        fill(cross_ref)

    @pl.when(matrix == layer_count)
    def _():
        fill(first_ref)

    @pl.when(matrix == layer_count + 1)
    def _():
        fill(second_ref)


def assemble(blocks, strips, own, layer_count, width, hidden):
    matrix_count = layer_count + 2
    size = strips.shape[2]
    both = pl.BlockSpec(blocks[0].shape[:2] + (1,) + blocks[0].shape[3:], lambda m: (0, 0, m, 0, 0))
    single = pl.BlockSpec(blocks[3].shape[:1] + (1,) + blocks[3].shape[2:], lambda m: (0, m, 0, 0))
    return pl.pallas_call(
        functools.partial(assemble_kernel, layer_count),
        grid=(matrix_count,),
        in_specs=[pl.BlockSpec(memory_space=pltpu.SMEM)]
        + ([both] * 3 + [single] * 2) * 2
        + [pl.BlockSpec((1, 8, size), lambda m: (m, 0, 0))],
        out_specs=[
            pl.BlockSpec((1, width, width), lambda m: (jnp.minimum(m, layer_count - 1), 0, 0)),
            pl.BlockSpec((1, width, hidden), lambda m: (0, 0, 0)),
            pl.BlockSpec((1, hidden, hidden), lambda m: (0, 0, 0)),
        ],
        out_shape=[
            jax.ShapeDtypeStruct((layer_count, width, width), F32),
            jax.ShapeDtypeStruct((1, width, hidden), F32),
            jax.ShapeDtypeStruct((1, hidden, hidden), F32),
        ],
        compiler_params=params(56),
        cost_estimate=cost(0, 6 * matrix_count * size * size),
        name="assemble",
    )(own, *blocks, strips)


def on_device(
    ids,
    table_rows,
    table_place,
    dense_in,
    labels,
    tables,
    cross_w,
    cross_b,
    tower1_w,
    tower1_b,
    tower2_w,
    tower2_b,
    out_w,
    out_b,
):
    tab_count = lax.axis_size("tab")
    rep_count = lax.axis_size("rep")
    slot_count, embed_dim, table_len = tables.shape
    row_count, dense_width = dense_in.shape
    field_count = ids.shape[1]
    layer_count, width = cross_w.shape[:2]
    hidden = tower1_w.shape[0]
    size = round_up(width, 128)
    all_slots = slot_count * tab_count
    tab_at = lax.axis_index("tab")
    rep_at = lax.axis_index("rep")

    matches = table_place[:, None] == jnp.arange(all_slots, dtype=I32)[None, :]
    effective = ids % table_rows[None, :]
    by_slot = jnp.sum(jnp.where(matches[:, :, None], effective.T[:, None, :], 0), axis=0)
    slot_rows = jnp.sum(jnp.where(matches, table_rows[:, None], 0), axis=0)
    own_rows = lax.dynamic_slice_in_dim(slot_rows, tab_at * slot_count, slot_count)
    wanted = lax.all_to_all(
        by_slot.reshape(tab_count, slot_count, row_count), "tab", split_axis=0, concat_axis=0, tiled=True
    )
    listed = jnp.transpose(wanted, (1, 0, 2)).reshape(-1)

    starts = list(range(0, slot_count, LOOK_SLOTS))
    arrived = []
    for begin in starts:
        looked = lookup(
            tables, listed, own_rows, tab_count, begin, min(LOOK_SLOTS, slot_count - begin)
        )
        arrived.append(lax.all_to_all(looked, "tab", split_axis=0, concat_axis=0, tiled=True))

    ready = 1.0 + arrived[0][0, 0, embed_dim, 0]

    def padded(weight):
        return jnp.pad(weight * ready, ((0, size - weight.shape[0]), (0, size - weight.shape[1])))

    weights = jnp.stack(
        [padded(cross_w[at]) for at in range(layer_count)] + [padded(tower1_w.T), padded(tower2_w)]
    )
    vectors = [cross_b[at] for at in range(layer_count)]
    vectors += [tower1_b, tower2_b, out_w[:width], out_w[width:], out_w[:0]]
    cols = jnp.stack(
        [jnp.pad((v * ready).astype(F32), (0, size - v.shape[0])) for v in vectors], axis=1
    )


    def near_parts(own):
        return [own, swap(own, "rep", 1)]

    def far_bases(own):
        bases = [own]
        for mask in masks_of("rep")[1:]:
            bases = bases + [swap(part, "rep", mask) for part in bases]
        return bases[1:]

    def far_parts(bases):
        return [part for far in bases for part in near_parts(far)]

    wanted = wanted + (ready - 1.0).astype(I32)
    near_ids = [part[:, :, None, :] for part in near_parts(wanted)]
    far_ids = [part[:, :, None, :] for part in far_parts(far_bases(wanted))]
    logits, dense_grad, slots, left, right, sums = dense_step(
        arrived, starts, table_place, dense_in, labels, weights, cols, out_b, layer_count, width,
        near_ids + far_ids,
    )
    returned = lax.all_to_all(
        slots.reshape(tab_count, slot_count, slots.shape[1], row_count),
        "tab",
        split_axis=0,
        concat_axis=0,
        tiled=True,
    )

    share = table_len // rep_count
    base = (rep_at * share).astype(I32).reshape(1)

    def gate(value, result):
        return value * (1.0 + 0.0 * result.astype(F32)).astype(value.dtype)

    bits = [rep_at & 1, (rep_at >> 1) & 1, tab_at & 1, (tab_at >> 2) & 1, (tab_at >> 1) & 1]
    own = sum(bit << (4 - at) for at, bit in enumerate(bits)).astype(I32).reshape(1)
    (send,) = weight_parts(left, right, own, 1)
    keep, strips = weight_parts(left, right, own, 0)
    matrix_count = layer_count + 2
    far_grads = None
    table_grad = None
    token = jnp.zeros((), F32)
    near_jobs = list(range(slot_count))[::-1]
    far_jobs = list(range(slot_count))[::-1]

    def add_next(near, times, after):
        nonlocal table_grad, token
        jobs = near_jobs if near else far_jobs
        for _ in range(min(times, len(jobs))):
            table_grad, token = add_rows(
                near_grads if near else far_grads,
                near_ids if near else far_ids,
                base,
                share,
                embed_dim,
                jobs.pop(),
                table_grad,
                not near,
                after,
            )

    def zero_of(value):
        return 0.0 * value.astype(F32)

    small = jnp.concatenate([strips.reshape(matrix_count * 8, size), sums], axis=0)
    total_rows = sums.shape[0]

    def small_step(value, masks):
        return small_sum(
            value, total_rows, [functools.partial(swap_both, rep_mask=r, tab_mask=t) for r, t in masks]
        )

    got = swap(send, "rep", 1)
    ahead = [added((keep[at, 1, 1], got[at, 1, 1])).astype(BF) for at in range(2)]
    first = [swap(ahead[at], *HALVES[at][0]) for at in range(2)]
    small = small_step(small + zero_of(ahead[0][0, 0, 0, 0, 0]) + zero_of(ahead[1][0, 0, 0, 0, 0]), [(1, 0)])
    small = small_step(small, [(2, 0), (0, 1), (2, 1)])
    keep, got, _ = lax.optimization_barrier((keep, got, ahead))
    behind = [added((keep[at, 1, 0], got[at, 1, 0])).astype(BF) for at in range(2)]
    later = [swap(behind[at], *HALVES[at][0]) for at in range(2)]
    keep, got, _ = lax.optimization_barrier((keep, got, behind))
    kept = [added((keep[at, 0], got[at, 0])) for at in range(2)]
    ready = zero_of(small[0, 0])
    sends = [added((kept[at][1], first[at]), ready).astype(BF) for at in range(2)]
    sent = [swap(sends[at], *HALVES[at][1]) for at in range(2)]
    returned = gate(returned, sends[0][0, 0, 0, 0, 0] + sends[1][0, 0, 0, 0, 0])
    near_grads = near_parts(returned)
    add_next(True, 1, behind + sends)
    bases = far_bases(gate(returned, token))
    add_next(True, NEAR_FIRST - 1, sends)
    sources = [[kept[at][0], later[at], sent[at]] for at in range(2)]

    def take_far(high, low):
        both = [added([part[high, low] for part in sources[at]], token) for at in range(2)]
        return jnp.stack(both)

    kept = take_far(0, 0)
    sends = [take_far(high, low).astype(BF) for high, low in FAR]
    far = [swap(value, "tab", 4 * high + 2 * low) for value, (high, low) in zip(sends, FAR)]
    add_next(True, slot_count, [kept] + sends)
    piece = added([kept, *far], token).astype(BF)
    for axis, known in (("rep", 2), ("tab", 3)):
        for mask in masks_of(axis)[known:]:
            piece = (piece.astype(F32) + swap(piece, axis, mask).astype(F32)).astype(BF)
    parts = [piece, swap(piece, "tab", 2), swap(piece, "tab", 4), swap(piece, "tab", 6)]
    far_grads = far_parts([gate(part, piece[0, 0, 0, 0]) for part in bases])
    add_next(False, FAR_FIRST, [piece])
    values = joined(parts, token)
    from_y = swap(values, "tab", 1)
    from_x = swap(values, "rep", 2)
    small = small + zero_of(values[0, 0, 0, 0, 0])
    small = small_step(small, [(0, 2), (0, 4), (0, 6)])
    for rep_mask in masks_of("rep")[2:]:
        small = small_step(small, [(rep_mask, 0)])
    for tab_mask in masks_of("tab")[3:]:
        small = small_step(small, [(0, tab_mask)])
    add_next(False, 1, [values])
    other = [swap(values, "rep", 1)]
    add_next(False, 1, other)
    token = token + zero_of(small[0, 0])
    last = [swap(gate(from_y[0], token), "rep", 2), swap(gate(from_x[1], token), "tab", 1)]
    other += [swap(from_y, "rep", 1), swap(from_x, "rep", 1)]
    add_next(False, slot_count, other)
    last = [gate(part, token) for part in last]
    blocks = [values, from_y, from_x] + last + other + [swap(part, "rep", 1) for part in last]

    strips = small[:-8].reshape(matrix_count, 8, size)
    sums = small[-8:]
    cross_w_grad, tower1_w_grad, tower2_w_grad = assemble(
        blocks, strips, own, layer_count, width, hidden
    )
    scalars = sums[layer_count + 4]
    return (
        scalars[0] / (row_count * tab_count * rep_count),
        logits.reshape(row_count),
        dense_grad[:dense_width].T,
        cross_w_grad,
        sums[:layer_count, :width],
        tower1_w_grad[0].T,
        sums[layer_count, :hidden],
        tower2_w_grad[0],
        sums[layer_count + 1, :hidden],
        jnp.concatenate([sums[layer_count + 2, :width], sums[layer_count + 3, :hidden]]),
        scalars[128],
        table_grad,
    )


def solution(mesh):
    placed = (
        P(("tab", "rep"), None),
        P(),
        P(),
        P(("tab", "rep"), None),
        P(("tab", "rep")),
        P("tab", None, None),
        P(),
        P(),
        P(),
        P(),
        P(),
        P(),
        P(),
        P(),
    )
    return jax.shard_map(
        on_device,
        mesh=mesh,
        in_specs=placed,
        out_specs=(
            P(),
            P(("tab", "rep")),
            P(("tab", "rep"), None),
            P(),
            P(),
            P(),
            P(),
            P(),
            P(),
            P(),
            P(),
            P("tab", None, "rep"),
        ),
        check_vma=False,
    )
```

```python
import functools

import jax
import jax.numpy as jnp
from jax import lax
from jax.experimental import pallas as pl
from jax.experimental.pallas import tpu as pltpu
from jax.sharding import PartitionSpec as P

BF = jnp.bfloat16
F32 = jnp.float32
I32 = jnp.int32
LOOK_SLOTS = 3
LOOK_LANES = 40
LOOK_BLOCKS = 8
LOOK_ROWS = 32
ADD_LOW = 512
ADD_TABS = 8
NEAR_FIRST = 2
FAR_FIRST = 2
MAIN = 1024
CHUNK = 384
PIECE = 32
MIB = 1024 * 1024
NT = (((1,), (1,)), ((), ()))
TN = (((0,), (0,)), ((), ()))


def round_up(size, unit):
    return -(-size // unit) * unit


def params(mib):
    return pltpu.CompilerParams(vmem_limit_bytes=mib * MIB)


def cost(flops, size):
    return pl.CostEstimate(flops=flops // 1000, bytes_accessed=size // 1000, transcendentals=0)


def swap(value, axis, mask):
    return lax.ppermute(value, axis, [(at, at ^ mask) for at in range(lax.axis_size(axis))])


def swap_both(value, rep_mask, tab_mask):
    rep_count = lax.axis_size("rep")
    perm = []
    for tab in range(lax.axis_size("tab")):
        for at in range(rep_count):
            perm.append((tab * rep_count + at, (tab ^ tab_mask) * rep_count + (at ^ rep_mask)))
    return lax.ppermute(value, ("tab", "rep"), perm)


def masks_of(axis):
    size = lax.axis_size(axis)
    return [1 << bit for bit in range(size.bit_length() - 1)]


def lookup_kernel(first_slot, ids_ref, rows_ref, table_hbm, out_ref, raw, stack, major, picked, sems):
    tab_count, slot_count, pad_dim, count = out_ref.shape
    embed_dim = raw.shape[1]
    total = tab_count * count
    copies = [
        pltpu.make_async_copy(table_hbm.at[first_slot + at], raw.at[at], sems.at[at])
        for at in range(slot_count)
    ]
    for copy in copies:
        copy.start()
    lane = lax.broadcasted_iota(I32, (1, 128), 1)
    stack[...] = jnp.zeros_like(stack)
    most = jnp.maximum(rows_ref[first_slot], 1)
    for at in range(1, slot_count):
        most = jnp.maximum(most, rows_ref[first_slot + at])
    for copy in copies:
        copy.wait()
    unit = 128 * LOOK_BLOCKS

    @pl.loop(0, (most + unit - 1) // unit)
    def _(step):
        for block in range(LOOK_BLOCKS):
            first = pl.multiple_of((step * LOOK_BLOCKS + block) * 128, 128)
            for at in range(slot_count):
                stack[block, at * LOOK_LANES : at * LOOK_LANES + embed_dim, :] = raw[
                    at, :, pl.ds(first, 128)
                ].astype(F32)
            major[pl.ds(first, 128), :] = stack[block].T

    @pl.loop(0, total // LOOK_ROWS)
    def _(step):
        base = step * LOOK_ROWS
        starts = [(first_slot + at) * total + base for at in range(slot_count)]
        for row in range(LOOK_ROWS):
            value = None
            for at in reversed(range(slot_count)):
                one = major[pl.ds(ids_ref[starts[at] + row], 1), :]
                value = one if value is None else jnp.where(lane < (at + 1) * LOOK_LANES, one, value)
            picked[pl.ds(base + row, 1), :] = value

    @pl.loop(0, tab_count)
    def _(tab):
        for block in range(0, count, 128):
            turned = picked[pl.ds(pl.multiple_of(tab * count + block, 128), 128), :].T
            for at in range(slot_count):
                rows = turned[at * LOOK_LANES : at * LOOK_LANES + pad_dim]
                out_ref[tab, at, :, block : block + 128] = rows.astype(BF)


def lookup(tables, wanted, own_rows, tab_count, first_slot, slot_count):
    all_count, embed_dim, table_len = tables.shape
    count = wanted.shape[0] // (all_count * tab_count)
    smem = pl.BlockSpec(memory_space=pltpu.SMEM)
    return pl.pallas_call(
        functools.partial(lookup_kernel, first_slot),
        in_specs=[smem, smem, pl.BlockSpec(memory_space=pl.ANY)],
        out_specs=pl.BlockSpec(memory_space=pltpu.VMEM),
        out_shape=jax.ShapeDtypeStruct((tab_count, slot_count, round_up(embed_dim, 8), count), BF),
        scratch_shapes=[
            pltpu.VMEM((slot_count, embed_dim, table_len), BF),
            pltpu.VMEM((LOOK_BLOCKS, 128, 128), F32),
            pltpu.VMEM((table_len, 128), F32),
            pltpu.VMEM((tab_count * count, 128), F32),
            pltpu.SemaphoreType.DMA((slot_count,)),
        ],
        compiler_params=params(56),
        cost_estimate=cost(
            600 * tab_count * count * table_len * slot_count // 8,
            2 * slot_count * embed_dim * (table_len + tab_count * count),
        ),
        name="lookup",
    )(wanted, own_rows, tables)


def add_kernel(part_count, has_before, steps, base_ref, *refs):
    ids_refs = refs[:part_count]
    grad_refs = refs[part_count : 2 * part_count]
    before_ref = refs[2 * part_count] if has_before else None
    out_ref, token_ref, total = refs[-3:]
    step = pl.program_id(0)
    embed_dim = out_ref.shape[1]
    cols = grad_refs[0].shape[3]
    high_count = total.shape[1] // embed_dim

    @pl.when(step == 0)
    def _():
        if steps > 1:
            total[...] = jnp.zeros_like(total)
        token_ref[...] = jnp.zeros_like(token_ref)

    high_iota = lax.broadcasted_iota(I32, (high_count, cols), 0)
    low_iota = lax.broadcasted_iota(I32, (ADD_LOW, cols), 0)
    product = None
    for ids_ref, grad_ref in zip(ids_refs, grad_refs):
        for tab in range(ids_ref.shape[0]):
            local = ids_ref[tab, 0] - base_ref[0]
            high = lax.shift_right_arithmetic(local, ADD_LOW.bit_length() - 1)
            low = local & (ADD_LOW - 1)
            high_hot = jnp.where(high_iota == high, 1.0, 0.0)
            low_hot = jnp.where(low_iota == low, 1.0, 0.0).astype(BF)
            grads = grad_ref[tab, 0, :embed_dim].astype(F32)
            left = (grads[:, None, :] * high_hot[None, :, :]).astype(BF)
            left = left.reshape(embed_dim * high_count, cols)
            term = lax.dot_general(left, low_hot, NT, preferred_element_type=F32)
            product = term if product is None else product + term
    for lane in range(ADD_LOW // 128):
        part = product[:, lane * 128 : (lane + 1) * 128]
        total[lane] = part if steps == 1 else total[lane] + part

    @pl.when(step == pl.num_programs(0) - 1)
    def _():
        for at in range(high_count):
            for part in range(0, embed_dim, 8):
                size = min(8, embed_dim - part)
                for lane in range(ADD_LOW // 128):
                    first = at * ADD_LOW + lane * 128
                    value = total[lane, pl.ds(part * high_count + at, size, stride=high_count), :]
                    if before_ref is not None:
                        value = value + before_ref[0, part : part + size, first : first + 128]
                    out_ref[0, part : part + size, first : first + 128] = value


def add_rows(grads, wanted, base, share, embed_dim, slot, so_far, accumulate, after):
    tab_count, slot_count, pad_dim, count = grads[0].shape
    part_count = len(grads)
    anywhere = pl.BlockSpec(memory_space=pl.ANY)
    block = pl.BlockSpec((1, embed_dim, share), lambda t: (slot, 0, 0))
    whole = [] if so_far is None else [so_far]
    table_grad, token = pl.pallas_call(
        functools.partial(add_kernel, part_count, accumulate, tab_count // ADD_TABS),
        grid=(tab_count // ADD_TABS,),
        in_specs=[pl.BlockSpec(memory_space=pltpu.SMEM)]
        + [pl.BlockSpec((ADD_TABS, 1, 1, count), lambda t: (t, slot, 0, 0))] * part_count
        + [pl.BlockSpec((ADD_TABS, 1, pad_dim, count), lambda t: (t, slot, 0, 0))] * part_count
        + [block if accumulate else anywhere] * len(whole)
        + [anywhere] * len(after),
        out_specs=[block, pl.BlockSpec((8, 128), lambda t: (0, 0))],
        scratch_shapes=[pltpu.VMEM((ADD_LOW // 128, embed_dim * (share // ADD_LOW), 128), F32)],
        out_shape=[
            jax.ShapeDtypeStruct((slot_count, embed_dim, share), F32),
            jax.ShapeDtypeStruct((8, 128), F32),
        ],
        input_output_aliases={1 + 2 * part_count: 0} if whole else {},
        compiler_params=params(40),
        cost_estimate=cost(
            2 * part_count * tab_count * count * share * embed_dim,
            2 * embed_dim * (2 * share + part_count * tab_count * count),
        ),
        name="add_rows",
    )(base, *wanted, *grads, *whole, *after)
    return table_grad, token[0, 0]


def row_sums(value):
    part = value[:, :128]
    for first in range(128, value.shape[1], 128):
        part = part + value[:, first : first + 128]
    return jnp.sum(part.T, axis=0, keepdims=True)


def dense_kernel(
    dense_width,
    width,
    starts,
    after_count,
    place_ref,
    bias_ref,
    *refs,
):
    group_count = len(starts)
    arrived_refs = refs[:group_count]
    first = group_count + 4
    dense_refs = refs[group_count:first] + refs[first + after_count :]
    dense_body(dense_width, width, starts, place_ref, bias_ref, arrived_refs, *dense_refs)


def dense_body(
    dense_width,
    width,
    starts,
    place_ref,
    bias_ref,
    arrived_refs,
    dense_ref,
    label_ref,
    weight_hbm,
    cols_ref,
    logits_ref,
    dense_grad_ref,
    slots_ref,
    left_ref,
    right_ref,
    sums_ref,
    weight,
    anchor,
    current,
    update,
    first_pre,
    second_pre,
    grad_anchor,
    grad_current,
    sems,
):
    layer_count = update.shape[0]
    tower1, tower2 = layer_count, layer_count + 1
    pad_dim = arrived_refs[0].shape[2]
    field_count = place_ref.shape[0]
    embed_dim = (width - dense_width) // field_count
    slot_count = sum(ref.shape[1] for ref in arrived_refs)
    size, cols = anchor.shape
    spans = [pl.ds(first, CHUNK) for first in range(0, size, CHUNK)]
    copies = [
        pltpu.make_async_copy(weight_hbm.at[at], weight.at[at], sems.at[at])
        for at in range(layer_count + 2)
    ]
    for copy in copies:
        copy.start()

    def column(at, span):
        return cols_ref[span, at : at + 1]

    def times(at, span, operand):
        return jnp.dot(weight[at, span, :], operand[...], preferred_element_type=F32)

    def transposed_times(at, span, operand):
        return lax.dot_general(weight[at, :, span], operand[...], TN, preferred_element_type=F32)

    anchor[0:16] = dense_ref[...]
    tail = width // 8 * 8
    anchor[tail:] = jnp.zeros((size - tail, cols), F32)
    for field in range(field_count):
        first = dense_width + field * embed_dim
        tab = place_ref[field] // slot_count
        slot = place_ref[field] - tab * slot_count
        value = arrived_refs[0][tab, jnp.minimum(slot, arrived_refs[0].shape[1] - 1)]
        for begin, ref in zip(starts[1:], arrived_refs[1:]):
            other = ref[tab, jnp.clip(slot - begin, 0, ref.shape[1] - 1)]
            value = jnp.where(slot >= begin, other, value)
        anchor[first : first + embed_dim] = value.astype(F32)[:embed_dim]
    for span in spans:
        left_ref[0, span] = anchor[span].astype(BF)
        left_ref[tower1, span] = anchor[span].astype(BF)
    for layer in range(layer_count):
        copies[layer].wait()
        for span in spans:
            value = transposed_times(layer, span, left_ref.at[layer]) + column(layer, span)
            update[layer, span] = value
            before = anchor if layer == 0 else current
            after = anchor[span] * value + before[span]
            current[span] = after
            if layer + 1 < layer_count:
                left_ref[layer + 1, span] = after.astype(BF)
    copies[tower1].wait()
    for span in spans:
        value = transposed_times(tower1, span, left_ref.at[0]) + column(tower1, span)
        first_pre[span] = value
        left_ref[tower2, span] = (value * jax.nn.sigmoid(value)).astype(BF)
    copies[tower2].wait()
    logits = jnp.full((1, cols), bias_ref[0], F32)
    for span in spans:
        value = transposed_times(tower2, span, left_ref.at[tower2]) + column(tower2, span)
        second_pre[span] = value
        act = value * jax.nn.sigmoid(value)
        terms = current[span] * column(layer_count + 2, span) + act * column(layer_count + 3, span)
        logits = logits + jnp.sum(terms, axis=0, keepdims=True)
    logits_ref[...] = logits
    target = label_ref[...]
    residue = jax.nn.sigmoid(logits) - target
    softplus = jnp.maximum(logits, 0.0) + jnp.log1p(jnp.exp(-jnp.abs(logits)))
    sums_ref[layer_count + 4 :, :] = jnp.zeros((sums_ref.shape[0] - layer_count - 4, size), F32)
    loss_row = jnp.sum(softplus - target * logits, axis=1, keepdims=True)
    bias_row = jnp.sum(residue, axis=1, keepdims=True)
    sums_ref[layer_count + 4 : layer_count + 5, 0:128] = jnp.broadcast_to(loss_row, (1, 128))
    sums_ref[layer_count + 4 : layer_count + 5, 128:256] = jnp.broadcast_to(bias_row, (1, 128))
    for span in spans:
        value = second_pre[span]
        sig = jax.nn.sigmoid(value)
        act = value * sig
        grad = residue * column(layer_count + 3, span) * (sig * (1.0 + value * (1.0 - sig)))
        low = grad.astype(BF)
        right_ref[tower2, span] = low
        sums_ref[tower2 : tower2 + 1, span] = row_sums(low.astype(F32))
        sums_ref[layer_count + 3 : layer_count + 4, span] = row_sums(residue * act)
        sums_ref[layer_count + 2 : layer_count + 3, span] = row_sums(residue * current[span])
        grad_current[span] = residue * column(layer_count + 2, span)
    for span in spans:
        value = first_pre[span]
        sig = jax.nn.sigmoid(value)
        grad = times(tower2, span, right_ref.at[tower2]) * (sig * (1.0 + value * (1.0 - sig)))
        low = grad.astype(BF)
        right_ref[tower1, span] = low
        sums_ref[tower1 : tower1 + 1, span] = row_sums(low.astype(F32))
    for span in spans:
        grad_anchor[span] = times(tower1, span, right_ref.at[tower1])
    for layer in reversed(range(layer_count)):
        for span in spans:
            grad = grad_current[span]
            low = (anchor[span] * grad).astype(BF)
            right_ref[layer, span] = low
            sums_ref[layer : layer + 1, span] = row_sums(low.astype(F32))
            grad_anchor[span] += grad * update[layer, span]
        for span in spans:
            grad_current[span] += times(layer, span, right_ref.at[layer])
    for span in spans:
        grad_anchor[span] += grad_current[span]
    dense_grad_ref[...] = grad_anchor[0:16]
    slots_ref[...] = jnp.zeros_like(slots_ref)
    for field in range(field_count):
        first = dense_width + field * embed_dim
        slots_ref[place_ref[field], :embed_dim] = grad_anchor[first : first + embed_dim].astype(BF)


def dense_step(arrived, starts, place, dense_in, labels, weights, cols, out_b, layer_count, width, after):
    tab_count, _, pad_dim, count = arrived[0].shape
    slot_count = tab_count * sum(part.shape[1] for part in arrived)
    dense_width = dense_in.shape[1]
    size = weights.shape[1]
    matrix_count = layer_count + 2
    dense_rows = jnp.pad(dense_in.T.astype(F32), ((0, 16 - dense_width), (0, 0)))
    vmem = pl.BlockSpec(memory_space=pltpu.VMEM)
    smem = pl.BlockSpec(memory_space=pltpu.SMEM)
    flat = pltpu.VMEM((size, count), F32)
    return pl.pallas_call(
        functools.partial(dense_kernel, dense_width, width, starts, len(after)),
        in_specs=[smem, smem] + [vmem] * (len(arrived) + 2) + [ pl.BlockSpec(memory_space=pl.ANY), vmem]
        + [pl.BlockSpec(memory_space=pl.ANY)] * len(after),
        out_specs=[vmem] * 6,
        out_shape=[
            jax.ShapeDtypeStruct((1, count), F32),
            jax.ShapeDtypeStruct((16, count), F32),
            jax.ShapeDtypeStruct((slot_count, pad_dim, count), BF),
            jax.ShapeDtypeStruct((matrix_count, size, count), BF),
            jax.ShapeDtypeStruct((matrix_count, size, count), BF),
            jax.ShapeDtypeStruct((8, size), F32),
        ],
        scratch_shapes=[
            pltpu.VMEM(weights.shape, BF),
            flat,
            flat,
            pltpu.VMEM((layer_count, size, count), F32),
            flat,
            flat,
            flat,
            flat,
            pltpu.SemaphoreType.DMA((matrix_count,)),
        ],
        compiler_params=params(60),
        cost_estimate=cost(4 * matrix_count * size * size * count, 2 * weights.size + 30 * size * count),
        name="dense",
    )(
        place,
        out_b.astype(F32).reshape(1),
        *arrived,
        dense_rows,
        labels.astype(F32).reshape(1, count),
        weights,
        cols,
        *after,
    )


def chunk_place(piece, swapped):
    if not swapped:
        return piece
    return (piece & 3) | ((piece & 4) << 1) | ((piece & 8) >> 1)


def weight_kernel(core, own_ref, left_ref, right_ref, out_ref, *refs):
    pieces = MAIN // PIECE // 2
    half = MAIN // 2
    moved = refs[-1]
    for at in range(pieces):
        first = pl.multiple_of(((core * pieces + at) ^ own_ref[0]) * PIECE, PIECE)
        moved[at * PIECE : (at + 1) * PIECE] = left_ref[0, pl.ds(first, PIECE), :]
    product = lax.dot_general(
        moved[...], right_ref[0, :MAIN, :], NT, preferred_element_type=F32
    ).astype(out_ref.dtype)
    for chunk in range(2):
        for at in range(pieces):
            out_ref[chunk, chunk_place(at, chunk == 1), 0] = product[
                at * PIECE : (at + 1) * PIECE, chunk * half : (chunk + 1) * half
            ]
    if core == 0:
        strip_ref = refs[0]
        below = lax.dot_general(
            left_ref[0, MAIN : MAIN + 16, :], right_ref[0], NT, preferred_element_type=F32
        )
        beside = lax.dot_general(
            right_ref[0, MAIN : MAIN + 16, :], left_ref[0], NT, preferred_element_type=F32
        )
        strip_ref[0, 0:3] = below[0:3]
        strip_ref[0, 3:6] = beside[0:3]
        strip_ref[0, 6:8] = jnp.zeros((2, strip_ref.shape[2]), F32)


def weight_parts(left, right, own, core):
    matrix_count, size, count = left.shape
    half = MAIN // 2
    pieces = MAIN // PIECE // 2
    out_specs = [pl.BlockSpec((2, pieces, 1, PIECE, half), lambda m: (0, 0, m, 0, 0))]
    shapes = [jax.ShapeDtypeStruct((2, pieces, matrix_count, PIECE, half), BF if core else F32)]
    if core == 0:
        out_specs.append(pl.BlockSpec((1, 8, size), lambda m: (m, 0, 0)))
        shapes.append(jax.ShapeDtypeStruct((matrix_count, 8, size), F32))
    outs = pl.pallas_call(
        functools.partial(weight_kernel, core),
        grid=(matrix_count,),
        in_specs=[
            pl.BlockSpec(memory_space=pltpu.SMEM),
            pl.BlockSpec((1, size, count), lambda m: (m, 0, 0)),
            pl.BlockSpec((1, size, count), lambda m: (m, 0, 0)),
        ],
        out_specs=out_specs,
        out_shape=shapes,
        scratch_shapes=[pltpu.VMEM((half, count), BF)],
        compiler_params=params(60),
        cost_estimate=cost(matrix_count * size * size * count, 5 * matrix_count * size * size),
        name="weight_parts",
    )(own, left, right)
    return [outs[0].reshape((2, 2, 2, 2, 2, matrix_count, PIECE, half))] + list(outs[1:])


HALVES = [[("rep", 2), ("tab", 1)], [("tab", 1), ("rep", 2)]]
FAR = [(0, 1), (1, 0), (1, 1)]


def added(parts, *gates):
    value = parts[0].astype(F32)
    for other in parts[1:]:
        value = value + other.astype(F32)
    for gate in gates:
        value = value + gate
    return value


def joined(parts, token):
    one = (1.0 + token).astype(BF)
    return jnp.stack([part * one for part in parts], axis=1)


def pack(small, total_rows):
    rounded = lax.reduce_precision(small, 8, 7)
    rest = small[-total_rows:] - rounded[-total_rows:]
    return jnp.concatenate([rounded.astype(BF), rest.astype(BF)], axis=0)


def small_sum(small, total_rows, sends):
    packed = pack(small, total_rows)
    rounded = lax.reduce_precision(small, 8, 7)
    rest = lax.reduce_precision(small[-total_rows:] - rounded[-total_rows:], 8, 7)
    terms = [(rounded, rest)]
    for send in sends:
        got = send(packed).astype(F32)
        terms.append((got[:-total_rows], got[-total_rows:]))
    while len(terms) > 1:
        terms = [
            (left[0] + right[0], left[1] + right[1]) for left, right in zip(terms[::2], terms[1::2])
        ]
    total, rest = terms[0]
    return jnp.concatenate([total[:-total_rows], total[-total_rows:] + rest], axis=0)


def assemble_kernel(layer_count, own_ref, *refs):
    blocks = refs[:10]
    strip_ref, cross_ref, first_ref, second_ref = refs[10:]
    matrix = pl.program_id(0)

    def fill(out_ref):
        def put(core, chunk, upper, at, value):
            rows, lanes = value.shape
            piece = 16 * core + chunk_place(4 * upper + at, chunk == 1)
            first = pl.multiple_of((piece ^ own_ref[0]) * rows, rows)
            out_ref[0, pl.ds(first, rows), chunk * lanes : (chunk + 1) * lanes] = value.astype(F32)

        for core in range(2):
            refs_here = blocks[5 * core : 5 * core + 5]
            for at in range(4):
                for ref, uppers in zip(refs_here[:3], ((0, 0), (1, 2), (2, 1))):
                    for chunk in range(2):
                        put(core, chunk, uppers[chunk], at, ref[chunk, at, 0])
                for chunk in range(2):
                    put(core, chunk, 3, at, refs_here[3 + chunk][at, 0])
        height, width = out_ref.shape[1:]
        if width > MAIN:
            extra = width - MAIN
            for first in range(0, MAIN, 128):
                turned = strip_ref[0, :, first : first + 128].T
                out_ref[0, first : first + 128, MAIN:] = turned[:, 3 : 3 + extra]
        if height > MAIN:
            out_ref[0, MAIN:, :] = strip_ref[0, 0 : height - MAIN, :width]

    @pl.when(matrix < layer_count)
    def _():
        fill(cross_ref)

    @pl.when(matrix == layer_count)
    def _():
        fill(first_ref)

    @pl.when(matrix == layer_count + 1)
    def _():
        fill(second_ref)


def assemble(blocks, strips, own, layer_count, width, hidden):
    matrix_count = layer_count + 2
    size = strips.shape[2]
    both = pl.BlockSpec(blocks[0].shape[:2] + (1,) + blocks[0].shape[3:], lambda m: (0, 0, m, 0, 0))
    single = pl.BlockSpec(blocks[3].shape[:1] + (1,) + blocks[3].shape[2:], lambda m: (0, m, 0, 0))
    return pl.pallas_call(
        functools.partial(assemble_kernel, layer_count),
        grid=(matrix_count,),
        in_specs=[pl.BlockSpec(memory_space=pltpu.SMEM)]
        + ([both] * 3 + [single] * 2) * 2
        + [pl.BlockSpec((1, 8, size), lambda m: (m, 0, 0))],
        out_specs=[
            pl.BlockSpec((1, width, width), lambda m: (jnp.minimum(m, layer_count - 1), 0, 0)),
            pl.BlockSpec((1, width, hidden), lambda m: (0, 0, 0)),
            pl.BlockSpec((1, hidden, hidden), lambda m: (0, 0, 0)),
        ],
        out_shape=[
            jax.ShapeDtypeStruct((layer_count, width, width), F32),
            jax.ShapeDtypeStruct((1, width, hidden), F32),
            jax.ShapeDtypeStruct((1, hidden, hidden), F32),
        ],
        compiler_params=params(56),
        cost_estimate=cost(0, 6 * matrix_count * size * size),
        name="assemble",
    )(own, *blocks, strips)


def on_device(
    ids,
    table_rows,
    table_place,
    dense_in,
    labels,
    tables,
    cross_w,
    cross_b,
    tower1_w,
    tower1_b,
    tower2_w,
    tower2_b,
    out_w,
    out_b,
):
    tab_count = lax.axis_size("tab")
    rep_count = lax.axis_size("rep")
    slot_count, embed_dim, table_len = tables.shape
    row_count, dense_width = dense_in.shape
    field_count = ids.shape[1]
    layer_count, width = cross_w.shape[:2]
    hidden = tower1_w.shape[0]
    size = round_up(width, 128)
    all_slots = slot_count * tab_count
    tab_at = lax.axis_index("tab")
    rep_at = lax.axis_index("rep")

    matches = table_place[:, None] == jnp.arange(all_slots, dtype=I32)[None, :]
    effective = ids % table_rows[None, :]
    by_slot = jnp.sum(jnp.where(matches[:, :, None], effective.T[:, None, :], 0), axis=0)
    slot_rows = jnp.sum(jnp.where(matches, table_rows[:, None], 0), axis=0)
    own_rows = lax.dynamic_slice_in_dim(slot_rows, tab_at * slot_count, slot_count)
    wanted = lax.all_to_all(
        by_slot.reshape(tab_count, slot_count, row_count), "tab", split_axis=0, concat_axis=0, tiled=True
    )
    listed = jnp.transpose(wanted, (1, 0, 2)).reshape(-1)

    starts = list(range(0, slot_count, LOOK_SLOTS))
    arrived = []
    for begin in starts:
        looked = lookup(
            tables, listed, own_rows, tab_count, begin, min(LOOK_SLOTS, slot_count - begin)
        )
        arrived.append(lax.all_to_all(looked, "tab", split_axis=0, concat_axis=0, tiled=True))

    ready = 1.0 + arrived[0][0, 0, embed_dim, 0]

    def padded(weight):
        return jnp.pad(weight * ready, ((0, size - weight.shape[0]), (0, size - weight.shape[1])))

    weights = jnp.stack(
        [padded(cross_w[at]) for at in range(layer_count)] + [padded(tower1_w.T), padded(tower2_w)]
    )
    vectors = [cross_b[at] for at in range(layer_count)]
    vectors += [tower1_b, tower2_b, out_w[:width], out_w[width:], out_w[:0]]
    cols = jnp.stack(
        [jnp.pad((v * ready).astype(F32), (0, size - v.shape[0])) for v in vectors], axis=1
    )


    def near_parts(own):
        return [own, swap(own, "rep", 1)]

    def far_bases(own):
        bases = [own]
        for mask in masks_of("rep")[1:]:
            bases = bases + [swap(part, "rep", mask) for part in bases]
        return bases[1:]

    def far_parts(bases):
        return [part for far in bases for part in near_parts(far)]

    wanted = wanted + (ready - 1.0).astype(I32)
    near_ids = [part[:, :, None, :] for part in near_parts(wanted)]
    far_ids = [part[:, :, None, :] for part in far_parts(far_bases(wanted))]
    logits, dense_grad, slots, left, right, sums = dense_step(
        arrived, starts, table_place, dense_in, labels, weights, cols, out_b, layer_count, width,
        near_ids + far_ids,
    )
    returned = lax.all_to_all(
        slots.reshape(tab_count, slot_count, slots.shape[1], row_count),
        "tab",
        split_axis=0,
        concat_axis=0,
        tiled=True,
    )

    share = table_len // rep_count
    base = (rep_at * share).astype(I32).reshape(1)

    def gate(value, result):
        return value * (1.0 + 0.0 * result.astype(F32)).astype(value.dtype)

    bits = [rep_at & 1, (rep_at >> 1) & 1, tab_at & 1, (tab_at >> 2) & 1, (tab_at >> 1) & 1]
    own = sum(bit << (4 - at) for at, bit in enumerate(bits)).astype(I32).reshape(1)
    (send,) = weight_parts(left, right, own, 1)
    keep, strips = weight_parts(left, right, own, 0)
    matrix_count = layer_count + 2
    far_grads = None
    table_grad = None
    token = jnp.zeros((), F32)
    near_jobs = list(range(slot_count))[::-1]
    far_jobs = list(range(slot_count))[::-1]

    def add_next(near, times, after):
        nonlocal table_grad, token
        jobs = near_jobs if near else far_jobs
        for _ in range(min(times, len(jobs))):
            table_grad, token = add_rows(
                near_grads if near else far_grads,
                near_ids if near else far_ids,
                base,
                share,
                embed_dim,
                jobs.pop(),
                table_grad,
                not near,
                after,
            )

    def zero_of(value):
        return 0.0 * value.astype(F32)

    small = jnp.concatenate([strips.reshape(matrix_count * 8, size), sums], axis=0)
    total_rows = sums.shape[0]

    def small_step(value, masks):
        return small_sum(
            value, total_rows, [functools.partial(swap_both, rep_mask=r, tab_mask=t) for r, t in masks]
        )

    got = swap(send, "rep", 1)
    ahead = [added((keep[at, 1, 1], got[at, 1, 1])).astype(BF) for at in range(2)]
    first = [swap(ahead[at], *HALVES[at][0]) for at in range(2)]
    small = small_step(small + zero_of(ahead[0][0, 0, 0, 0, 0]) + zero_of(ahead[1][0, 0, 0, 0, 0]), [(1, 0)])
    small = small_step(small, [(2, 0), (0, 1), (2, 1)])
    keep, got, _ = lax.optimization_barrier((keep, got, ahead))
    behind = [added((keep[at, 1, 0], got[at, 1, 0])).astype(BF) for at in range(2)]
    later = [swap(behind[at], *HALVES[at][0]) for at in range(2)]
    keep, got, _ = lax.optimization_barrier((keep, got, behind))
    kept = [added((keep[at, 0], got[at, 0])) for at in range(2)]
    ready = zero_of(small[0, 0])
    sends = [added((kept[at][1], first[at]), ready).astype(BF) for at in range(2)]
    sent = [swap(sends[at], *HALVES[at][1]) for at in range(2)]
    returned = gate(returned, sends[0][0, 0, 0, 0, 0] + sends[1][0, 0, 0, 0, 0])
    near_grads = near_parts(returned)
    add_next(True, 1, behind + sends)
    bases = far_bases(gate(returned, token))
    add_next(True, NEAR_FIRST - 1, sends)
    sources = [[kept[at][0], later[at], sent[at]] for at in range(2)]

    def take_far(high, low):
        both = [added([part[high, low] for part in sources[at]], token) for at in range(2)]
        return jnp.stack(both)

    kept = take_far(0, 0)
    sends = [take_far(high, low).astype(BF) for high, low in FAR]
    far = [swap(value, "tab", 4 * high + 2 * low) for value, (high, low) in zip(sends, FAR)]
    add_next(True, slot_count, [kept] + sends)
    piece = added([kept, *far], token).astype(BF)
    for axis, known in (("rep", 2), ("tab", 3)):
        for mask in masks_of(axis)[known:]:
            piece = (piece.astype(F32) + swap(piece, axis, mask).astype(F32)).astype(BF)
    parts = [piece, swap(piece, "tab", 2), swap(piece, "tab", 4), swap(piece, "tab", 6)]
    far_grads = far_parts([gate(part, piece[0, 0, 0, 0]) for part in bases])
    add_next(False, FAR_FIRST, [piece])
    values = joined(parts, token)
    from_y = swap(values, "tab", 1)
    from_x = swap(values, "rep", 2)
    add_next(False, 1, [values])
    other = [swap(values, "rep", 1)]
    add_next(False, 1, other)
    last = [swap(gate(from_y[0], token), "rep", 2), swap(gate(from_x[1], token), "tab", 1)]
    small = small + zero_of(token)
    small = small_step(small, [(0, 2), (0, 4), (0, 6)])
    for rep_mask in masks_of("rep")[2:]:
        small = small_step(small, [(rep_mask, 0)])
    for tab_mask in masks_of("tab")[3:]:
        small = small_step(small, [(0, tab_mask)])
    other += [swap(from_y, "rep", 1), swap(from_x, "rep", 1)]
    add_next(False, slot_count, other)
    token = token + zero_of(small[0, 0])
    last = [gate(part, token) for part in last]
    blocks = [values, from_y, from_x] + last + other + [swap(part, "rep", 1) for part in last]

    strips = small[:-8].reshape(matrix_count, 8, size)
    sums = small[-8:]
    cross_w_grad, tower1_w_grad, tower2_w_grad = assemble(
        blocks, strips, own, layer_count, width, hidden
    )
    scalars = sums[layer_count + 4]
    return (
        scalars[0] / (row_count * tab_count * rep_count),
        logits.reshape(row_count),
        dense_grad[:dense_width].T,
        cross_w_grad,
        sums[:layer_count, :width],
        tower1_w_grad[0].T,
        sums[layer_count, :hidden],
        tower2_w_grad[0],
        sums[layer_count + 1, :hidden],
        jnp.concatenate([sums[layer_count + 2, :width], sums[layer_count + 3, :hidden]]),
        scalars[128],
        table_grad,
    )


def solution(mesh):
    placed = (
        P(("tab", "rep"), None),
        P(),
        P(),
        P(("tab", "rep"), None),
        P(("tab", "rep")),
        P("tab", None, None),
        P(),
        P(),
        P(),
        P(),
        P(),
        P(),
        P(),
        P(),
    )
    return jax.shard_map(
        on_device,
        mesh=mesh,
        in_specs=placed,
        out_specs=(
            P(),
            P(("tab", "rep")),
            P(("tab", "rep"), None),
            P(),
            P(),
            P(),
            P(),
            P(),
            P(),
            P(),
            P(),
            P("tab", None, "rep"),
        ),
        check_vma=False,
    )
```

```python
import functools

import jax
import jax.numpy as jnp
from jax import lax
from jax.experimental import pallas as pl
from jax.experimental.pallas import tpu as pltpu
from jax.sharding import PartitionSpec as P

BF = jnp.bfloat16
F32 = jnp.float32
I32 = jnp.int32
LOOK_SLOTS = 3
LOOK_LANES = 40
LOOK_BLOCKS = 8
LOOK_ROWS = 32
ADD_LOW = 512
ADD_TABS = 8
NEAR_FIRST = 2
FAR_FIRST = 2
MAIN = 1024
CHUNK = 384
PIECE = 32
MIB = 1024 * 1024
NT = (((1,), (1,)), ((), ()))
TN = (((0,), (0,)), ((), ()))


def round_up(size, unit):
    return -(-size // unit) * unit


def params(mib):
    return pltpu.CompilerParams(vmem_limit_bytes=mib * MIB)


def cost(flops, size):
    return pl.CostEstimate(flops=flops // 1000, bytes_accessed=size // 1000, transcendentals=0)


def swap(value, axis, mask):
    return lax.ppermute(value, axis, [(at, at ^ mask) for at in range(lax.axis_size(axis))])


def swap_both(value, rep_mask, tab_mask):
    rep_count = lax.axis_size("rep")
    perm = []
    for tab in range(lax.axis_size("tab")):
        for at in range(rep_count):
            perm.append((tab * rep_count + at, (tab ^ tab_mask) * rep_count + (at ^ rep_mask)))
    return lax.ppermute(value, ("tab", "rep"), perm)


def masks_of(axis):
    size = lax.axis_size(axis)
    return [1 << bit for bit in range(size.bit_length() - 1)]


def lookup_kernel(first_slot, ids_ref, rows_ref, table_hbm, out_ref, raw, stack, major, picked, sems):
    tab_count, slot_count, pad_dim, count = out_ref.shape
    embed_dim = raw.shape[1]
    total = tab_count * count
    copies = [
        pltpu.make_async_copy(table_hbm.at[first_slot + at], raw.at[at], sems.at[at])
        for at in range(slot_count)
    ]
    for copy in copies:
        copy.start()
    lane = lax.broadcasted_iota(I32, (1, 128), 1)
    stack[...] = jnp.zeros_like(stack)
    most = jnp.maximum(rows_ref[first_slot], 1)
    for at in range(1, slot_count):
        most = jnp.maximum(most, rows_ref[first_slot + at])
    for copy in copies:
        copy.wait()
    unit = 128 * LOOK_BLOCKS

    @pl.loop(0, (most + unit - 1) // unit)
    def _(step):
        for block in range(LOOK_BLOCKS):
            first = pl.multiple_of((step * LOOK_BLOCKS + block) * 128, 128)
            for at in range(slot_count):
                stack[block, at * LOOK_LANES : at * LOOK_LANES + embed_dim, :] = raw[
                    at, :, pl.ds(first, 128)
                ].astype(F32)
            major[pl.ds(first, 128), :] = stack[block].T

    @pl.loop(0, total // LOOK_ROWS)
    def _(step):
        base = step * LOOK_ROWS
        starts = [(first_slot + at) * total + base for at in range(slot_count)]
        for row in range(LOOK_ROWS):
            value = None
            for at in reversed(range(slot_count)):
                one = major[pl.ds(ids_ref[starts[at] + row], 1), :]
                value = one if value is None else jnp.where(lane < (at + 1) * LOOK_LANES, one, value)
            picked[pl.ds(base + row, 1), :] = value

    @pl.loop(0, tab_count)
    def _(tab):
        for block in range(0, count, 128):
            turned = picked[pl.ds(pl.multiple_of(tab * count + block, 128), 128), :].T
            for at in range(slot_count):
                rows = turned[at * LOOK_LANES : at * LOOK_LANES + pad_dim]
                out_ref[tab, at, :, block : block + 128] = rows.astype(BF)


def lookup(tables, wanted, own_rows, tab_count, first_slot, slot_count):
    all_count, embed_dim, table_len = tables.shape
    count = wanted.shape[0] // (all_count * tab_count)
    smem = pl.BlockSpec(memory_space=pltpu.SMEM)
    return pl.pallas_call(
        functools.partial(lookup_kernel, first_slot),
        in_specs=[smem, smem, pl.BlockSpec(memory_space=pl.ANY)],
        out_specs=pl.BlockSpec(memory_space=pltpu.VMEM),
        out_shape=jax.ShapeDtypeStruct((tab_count, slot_count, round_up(embed_dim, 8), count), BF),
        scratch_shapes=[
            pltpu.VMEM((slot_count, embed_dim, table_len), BF),
            pltpu.VMEM((LOOK_BLOCKS, 128, 128), F32),
            pltpu.VMEM((table_len, 128), F32),
            pltpu.VMEM((tab_count * count, 128), F32),
            pltpu.SemaphoreType.DMA((slot_count,)),
        ],
        compiler_params=params(56),
        cost_estimate=cost(
            600 * tab_count * count * table_len * slot_count // 8,
            2 * slot_count * embed_dim * (table_len + tab_count * count),
        ),
        name="lookup",
    )(wanted, own_rows, tables)


def add_kernel(part_count, has_before, steps, base_ref, *refs):
    ids_refs = refs[:part_count]
    grad_refs = refs[part_count : 2 * part_count]
    before_ref = refs[2 * part_count] if has_before else None
    out_ref, token_ref, total = refs[-3:]
    step = pl.program_id(0)
    embed_dim = out_ref.shape[1]
    cols = grad_refs[0].shape[3]
    high_count = total.shape[1] // embed_dim

    @pl.when(step == 0)
    def _():
        if steps > 1:
            total[...] = jnp.zeros_like(total)
        token_ref[...] = jnp.zeros_like(token_ref)

    high_iota = lax.broadcasted_iota(I32, (high_count, cols), 0)
    low_iota = lax.broadcasted_iota(I32, (ADD_LOW, cols), 0)
    product = None
    for ids_ref, grad_ref in zip(ids_refs, grad_refs):
        for tab in range(ids_ref.shape[0]):
            local = ids_ref[tab, 0] - base_ref[0]
            high = lax.shift_right_arithmetic(local, ADD_LOW.bit_length() - 1)
            low = local & (ADD_LOW - 1)
            high_hot = jnp.where(high_iota == high, 1.0, 0.0)
            low_hot = jnp.where(low_iota == low, 1.0, 0.0).astype(BF)
            grads = grad_ref[tab, 0, :embed_dim].astype(F32)
            left = (grads[:, None, :] * high_hot[None, :, :]).astype(BF)
            left = left.reshape(embed_dim * high_count, cols)
            term = lax.dot_general(left, low_hot, NT, preferred_element_type=F32)
            product = term if product is None else product + term
    for lane in range(ADD_LOW // 128):
        part = product[:, lane * 128 : (lane + 1) * 128]
        total[lane] = part if steps == 1 else total[lane] + part

    @pl.when(step == pl.num_programs(0) - 1)
    def _():
        for at in range(high_count):
            for part in range(0, embed_dim, 8):
                size = min(8, embed_dim - part)
                for lane in range(ADD_LOW // 128):
                    first = at * ADD_LOW + lane * 128
                    value = total[lane, pl.ds(part * high_count + at, size, stride=high_count), :]
                    if before_ref is not None:
                        value = value + before_ref[0, part : part + size, first : first + 128]
                    out_ref[0, part : part + size, first : first + 128] = value


def add_rows(grads, wanted, base, share, embed_dim, slot, so_far, accumulate, after):
    tab_count, slot_count, pad_dim, count = grads[0].shape
    part_count = len(grads)
    anywhere = pl.BlockSpec(memory_space=pl.ANY)
    block = pl.BlockSpec((1, embed_dim, share), lambda t: (slot, 0, 0))
    whole = [] if so_far is None else [so_far]
    table_grad, token = pl.pallas_call(
        functools.partial(add_kernel, part_count, accumulate, tab_count // ADD_TABS),
        grid=(tab_count // ADD_TABS,),
        in_specs=[pl.BlockSpec(memory_space=pltpu.SMEM)]
        + [pl.BlockSpec((ADD_TABS, 1, 1, count), lambda t: (t, slot, 0, 0))] * part_count
        + [pl.BlockSpec((ADD_TABS, 1, pad_dim, count), lambda t: (t, slot, 0, 0))] * part_count
        + [block if accumulate else anywhere] * len(whole)
        + [anywhere] * len(after),
        out_specs=[block, pl.BlockSpec((8, 128), lambda t: (0, 0))],
        scratch_shapes=[pltpu.VMEM((ADD_LOW // 128, embed_dim * (share // ADD_LOW), 128), F32)],
        out_shape=[
            jax.ShapeDtypeStruct((slot_count, embed_dim, share), F32),
            jax.ShapeDtypeStruct((8, 128), F32),
        ],
        input_output_aliases={1 + 2 * part_count: 0} if whole else {},
        compiler_params=params(40),
        cost_estimate=cost(
            2 * part_count * tab_count * count * share * embed_dim,
            2 * embed_dim * (2 * share + part_count * tab_count * count),
        ),
        name="add_rows",
    )(base, *wanted, *grads, *whole, *after)
    return table_grad, token[0, 0]


def row_sums(value):
    part = value[:, :128]
    for first in range(128, value.shape[1], 128):
        part = part + value[:, first : first + 128]
    return jnp.sum(part.T, axis=0, keepdims=True)


def dense_kernel(
    dense_width,
    width,
    starts,
    after_count,
    place_ref,
    bias_ref,
    *refs,
):
    group_count = len(starts)
    arrived_refs = refs[:group_count]
    first = group_count + 4
    dense_refs = refs[group_count:first] + refs[first + after_count :]
    dense_body(dense_width, width, starts, place_ref, bias_ref, arrived_refs, *dense_refs)


def dense_body(
    dense_width,
    width,
    starts,
    place_ref,
    bias_ref,
    arrived_refs,
    dense_ref,
    label_ref,
    weight_hbm,
    cols_ref,
    logits_ref,
    dense_grad_ref,
    slots_ref,
    left_ref,
    right_ref,
    sums_ref,
    weight,
    anchor,
    current,
    update,
    first_pre,
    second_pre,
    grad_anchor,
    grad_current,
    sems,
):
    layer_count = update.shape[0]
    tower1, tower2 = layer_count, layer_count + 1
    pad_dim = arrived_refs[0].shape[2]
    field_count = place_ref.shape[0]
    embed_dim = (width - dense_width) // field_count
    slot_count = sum(ref.shape[1] for ref in arrived_refs)
    size, cols = anchor.shape
    spans = [pl.ds(first, CHUNK) for first in range(0, size, CHUNK)]
    copies = [
        pltpu.make_async_copy(weight_hbm.at[at], weight.at[at], sems.at[at])
        for at in range(layer_count + 2)
    ]
    for copy in copies:
        copy.start()

    def column(at, span):
        return cols_ref[span, at : at + 1]

    def times(at, span, operand):
        return jnp.dot(weight[at, span, :], operand[...], preferred_element_type=F32)

    def transposed_times(at, span, operand):
        return lax.dot_general(weight[at, :, span], operand[...], TN, preferred_element_type=F32)

    anchor[0:16] = dense_ref[...]
    tail = width // 8 * 8
    anchor[tail:] = jnp.zeros((size - tail, cols), F32)
    for field in range(field_count):
        first = dense_width + field * embed_dim
        tab = place_ref[field] // slot_count
        slot = place_ref[field] - tab * slot_count
        value = arrived_refs[0][tab, jnp.minimum(slot, arrived_refs[0].shape[1] - 1)]
        for begin, ref in zip(starts[1:], arrived_refs[1:]):
            other = ref[tab, jnp.clip(slot - begin, 0, ref.shape[1] - 1)]
            value = jnp.where(slot >= begin, other, value)
        anchor[first : first + embed_dim] = value.astype(F32)[:embed_dim]
    for span in spans:
        left_ref[0, span] = anchor[span].astype(BF)
        left_ref[tower1, span] = anchor[span].astype(BF)
    for layer in range(layer_count):
        copies[layer].wait()
        for span in spans:
            value = transposed_times(layer, span, left_ref.at[layer]) + column(layer, span)
            update[layer, span] = value
            before = anchor if layer == 0 else current
            after = anchor[span] * value + before[span]
            current[span] = after
            if layer + 1 < layer_count:
                left_ref[layer + 1, span] = after.astype(BF)
    copies[tower1].wait()
    for span in spans:
        value = transposed_times(tower1, span, left_ref.at[0]) + column(tower1, span)
        first_pre[span] = value
        left_ref[tower2, span] = (value * jax.nn.sigmoid(value)).astype(BF)
    copies[tower2].wait()
    logits = jnp.full((1, cols), bias_ref[0], F32)
    for span in spans:
        value = transposed_times(tower2, span, left_ref.at[tower2]) + column(tower2, span)
        second_pre[span] = value
        act = value * jax.nn.sigmoid(value)
        terms = current[span] * column(layer_count + 2, span) + act * column(layer_count + 3, span)
        logits = logits + jnp.sum(terms, axis=0, keepdims=True)
    logits_ref[...] = logits
    target = label_ref[...]
    residue = jax.nn.sigmoid(logits) - target
    softplus = jnp.maximum(logits, 0.0) + jnp.log1p(jnp.exp(-jnp.abs(logits)))
    sums_ref[layer_count + 4 :, :] = jnp.zeros((sums_ref.shape[0] - layer_count - 4, size), F32)
    loss_row = jnp.sum(softplus - target * logits, axis=1, keepdims=True)
    bias_row = jnp.sum(residue, axis=1, keepdims=True)
    sums_ref[layer_count + 4 : layer_count + 5, 0:128] = jnp.broadcast_to(loss_row, (1, 128))
    sums_ref[layer_count + 4 : layer_count + 5, 128:256] = jnp.broadcast_to(bias_row, (1, 128))
    for span in spans:
        value = second_pre[span]
        sig = jax.nn.sigmoid(value)
        act = value * sig
        grad = residue * column(layer_count + 3, span) * (sig * (1.0 + value * (1.0 - sig)))
        low = grad.astype(BF)
        right_ref[tower2, span] = low
        sums_ref[tower2 : tower2 + 1, span] = row_sums(low.astype(F32))
        sums_ref[layer_count + 3 : layer_count + 4, span] = row_sums(residue * act)
        sums_ref[layer_count + 2 : layer_count + 3, span] = row_sums(residue * current[span])
        grad_current[span] = residue * column(layer_count + 2, span)
    for span in spans:
        value = first_pre[span]
        sig = jax.nn.sigmoid(value)
        grad = times(tower2, span, right_ref.at[tower2]) * (sig * (1.0 + value * (1.0 - sig)))
        low = grad.astype(BF)
        right_ref[tower1, span] = low
        sums_ref[tower1 : tower1 + 1, span] = row_sums(low.astype(F32))
    for span in spans:
        grad_anchor[span] = times(tower1, span, right_ref.at[tower1])
    for layer in reversed(range(layer_count)):
        for span in spans:
            grad = grad_current[span]
            low = (anchor[span] * grad).astype(BF)
            right_ref[layer, span] = low
            sums_ref[layer : layer + 1, span] = row_sums(low.astype(F32))
            grad_anchor[span] += grad * update[layer, span]
        for span in spans:
            grad_current[span] += times(layer, span, right_ref.at[layer])
    for span in spans:
        grad_anchor[span] += grad_current[span]
    dense_grad_ref[...] = grad_anchor[0:16]
    slots_ref[...] = jnp.zeros_like(slots_ref)
    for field in range(field_count):
        first = dense_width + field * embed_dim
        slots_ref[place_ref[field], :embed_dim] = grad_anchor[first : first + embed_dim].astype(BF)


def dense_step(arrived, starts, place, dense_in, labels, weights, cols, out_b, layer_count, width, after):
    tab_count, _, pad_dim, count = arrived[0].shape
    slot_count = tab_count * sum(part.shape[1] for part in arrived)
    dense_width = dense_in.shape[1]
    size = weights.shape[1]
    matrix_count = layer_count + 2
    dense_rows = jnp.pad(dense_in.T.astype(F32), ((0, 16 - dense_width), (0, 0)))
    vmem = pl.BlockSpec(memory_space=pltpu.VMEM)
    smem = pl.BlockSpec(memory_space=pltpu.SMEM)
    flat = pltpu.VMEM((size, count), F32)
    return pl.pallas_call(
        functools.partial(dense_kernel, dense_width, width, starts, len(after)),
        in_specs=[smem, smem] + [vmem] * (len(arrived) + 2) + [ pl.BlockSpec(memory_space=pl.ANY), vmem]
        + [pl.BlockSpec(memory_space=pl.ANY)] * len(after),
        out_specs=[vmem] * 6,
        out_shape=[
            jax.ShapeDtypeStruct((1, count), F32),
            jax.ShapeDtypeStruct((16, count), F32),
            jax.ShapeDtypeStruct((slot_count, pad_dim, count), BF),
            jax.ShapeDtypeStruct((matrix_count, size, count), BF),
            jax.ShapeDtypeStruct((matrix_count, size, count), BF),
            jax.ShapeDtypeStruct((8, size), F32),
        ],
        scratch_shapes=[
            pltpu.VMEM(weights.shape, BF),
            flat,
            flat,
            pltpu.VMEM((layer_count, size, count), F32),
            flat,
            flat,
            flat,
            flat,
            pltpu.SemaphoreType.DMA((matrix_count,)),
        ],
        compiler_params=params(60),
        cost_estimate=cost(4 * matrix_count * size * size * count, 2 * weights.size + 30 * size * count),
        name="dense",
    )(
        place,
        out_b.astype(F32).reshape(1),
        *arrived,
        dense_rows,
        labels.astype(F32).reshape(1, count),
        weights,
        cols,
        *after,
    )


def chunk_place(piece, swapped):
    if not swapped:
        return piece
    return (piece & 3) | ((piece & 4) << 1) | ((piece & 8) >> 1)


def weight_kernel(core, own_ref, left_ref, right_ref, out_ref, *refs):
    pieces = MAIN // PIECE // 2
    half = MAIN // 2
    moved = refs[-1]
    for at in range(pieces):
        first = pl.multiple_of(((core * pieces + at) ^ own_ref[0]) * PIECE, PIECE)
        moved[at * PIECE : (at + 1) * PIECE] = left_ref[0, pl.ds(first, PIECE), :]
    product = lax.dot_general(
        moved[...], right_ref[0, :MAIN, :], NT, preferred_element_type=F32
    ).astype(out_ref.dtype)
    for chunk in range(2):
        for at in range(pieces):
            out_ref[chunk, chunk_place(at, chunk == 1), 0] = product[
                at * PIECE : (at + 1) * PIECE, chunk * half : (chunk + 1) * half
            ]
    if core == 0:
        strip_ref = refs[0]
        below = lax.dot_general(
            left_ref[0, MAIN : MAIN + 16, :], right_ref[0], NT, preferred_element_type=F32
        )
        beside = lax.dot_general(
            right_ref[0, MAIN : MAIN + 16, :], left_ref[0], NT, preferred_element_type=F32
        )
        strip_ref[0, 0:3] = below[0:3]
        strip_ref[0, 3:6] = beside[0:3]
        strip_ref[0, 6:8] = jnp.zeros((2, strip_ref.shape[2]), F32)


def weight_parts(left, right, own, core):
    matrix_count, size, count = left.shape
    half = MAIN // 2
    pieces = MAIN // PIECE // 2
    out_specs = [pl.BlockSpec((2, pieces, 1, PIECE, half), lambda m: (0, 0, m, 0, 0))]
    shapes = [jax.ShapeDtypeStruct((2, pieces, matrix_count, PIECE, half), BF if core else F32)]
    if core == 0:
        out_specs.append(pl.BlockSpec((1, 8, size), lambda m: (m, 0, 0)))
        shapes.append(jax.ShapeDtypeStruct((matrix_count, 8, size), F32))
    outs = pl.pallas_call(
        functools.partial(weight_kernel, core),
        grid=(matrix_count,),
        in_specs=[
            pl.BlockSpec(memory_space=pltpu.SMEM),
            pl.BlockSpec((1, size, count), lambda m: (m, 0, 0)),
            pl.BlockSpec((1, size, count), lambda m: (m, 0, 0)),
        ],
        out_specs=out_specs,
        out_shape=shapes,
        scratch_shapes=[pltpu.VMEM((half, count), BF)],
        compiler_params=params(60),
        cost_estimate=cost(matrix_count * size * size * count, 5 * matrix_count * size * size),
        name="weight_parts",
    )(own, left, right)
    return [outs[0].reshape((2, 2, 2, 2, 2, matrix_count, PIECE, half))] + list(outs[1:])


HALVES = [[("rep", 2), ("tab", 1)], [("tab", 1), ("rep", 2)]]
FAR = [(0, 1), (1, 0), (1, 1)]


def added(parts, *gates):
    value = parts[0].astype(F32)
    for other in parts[1:]:
        value = value + other.astype(F32)
    for gate in gates:
        value = value + gate
    return value


def joined(parts, token):
    one = (1.0 + token).astype(BF)
    return jnp.stack([part * one for part in parts], axis=1)


def pack(small, total_rows):
    rounded = lax.reduce_precision(small, 8, 7)
    rest = small[-total_rows:] - rounded[-total_rows:]
    return jnp.concatenate([rounded.astype(BF), rest.astype(BF)], axis=0)


def small_sum(small, total_rows, sends):
    packed = pack(small, total_rows)
    rounded = lax.reduce_precision(small, 8, 7)
    rest = lax.reduce_precision(small[-total_rows:] - rounded[-total_rows:], 8, 7)
    terms = [(rounded, rest)]
    for send in sends:
        got = send(packed).astype(F32)
        terms.append((got[:-total_rows], got[-total_rows:]))
    while len(terms) > 1:
        terms = [
            (left[0] + right[0], left[1] + right[1]) for left, right in zip(terms[::2], terms[1::2])
        ]
    total, rest = terms[0]
    return jnp.concatenate([total[:-total_rows], total[-total_rows:] + rest], axis=0)


def assemble_kernel(layer_count, own_ref, *refs):
    blocks = refs[:10]
    strip_ref, cross_ref, first_ref, second_ref = refs[10:]
    matrix = pl.program_id(0)

    def fill(out_ref):
        def put(core, chunk, upper, at, value):
            rows, lanes = value.shape
            piece = 16 * core + chunk_place(4 * upper + at, chunk == 1)
            first = pl.multiple_of((piece ^ own_ref[0]) * rows, rows)
            out_ref[0, pl.ds(first, rows), chunk * lanes : (chunk + 1) * lanes] = value.astype(F32)

        for core in range(2):
            refs_here = blocks[5 * core : 5 * core + 5]
            for at in range(4):
                for ref, uppers in zip(refs_here[:3], ((0, 0), (1, 2), (2, 1))):
                    for chunk in range(2):
                        put(core, chunk, uppers[chunk], at, ref[chunk, at, 0])
                for chunk in range(2):
                    put(core, chunk, 3, at, refs_here[3 + chunk][at, 0])
        height, width = out_ref.shape[1:]
        if width > MAIN:
            extra = width - MAIN
            for first in range(0, MAIN, 128):
                turned = strip_ref[0, :, first : first + 128].T
                out_ref[0, first : first + 128, MAIN:] = turned[:, 3 : 3 + extra]
        if height > MAIN:
            out_ref[0, MAIN:, :] = strip_ref[0, 0 : height - MAIN, :width]

    @pl.when(matrix < layer_count)
    def _():
        fill(cross_ref)

    @pl.when(matrix == layer_count)
    def _():
        fill(first_ref)

    @pl.when(matrix == layer_count + 1)
    def _():
        fill(second_ref)


def assemble(blocks, strips, own, layer_count, width, hidden):
    matrix_count = layer_count + 2
    size = strips.shape[2]
    both = pl.BlockSpec(blocks[0].shape[:2] + (1,) + blocks[0].shape[3:], lambda m: (0, 0, m, 0, 0))
    single = pl.BlockSpec(blocks[3].shape[:1] + (1,) + blocks[3].shape[2:], lambda m: (0, m, 0, 0))
    return pl.pallas_call(
        functools.partial(assemble_kernel, layer_count),
        grid=(matrix_count,),
        in_specs=[pl.BlockSpec(memory_space=pltpu.SMEM)]
        + ([both] * 3 + [single] * 2) * 2
        + [pl.BlockSpec((1, 8, size), lambda m: (m, 0, 0))],
        out_specs=[
            pl.BlockSpec((1, width, width), lambda m: (jnp.minimum(m, layer_count - 1), 0, 0)),
            pl.BlockSpec((1, width, hidden), lambda m: (0, 0, 0)),
            pl.BlockSpec((1, hidden, hidden), lambda m: (0, 0, 0)),
        ],
        out_shape=[
            jax.ShapeDtypeStruct((layer_count, width, width), F32),
            jax.ShapeDtypeStruct((1, width, hidden), F32),
            jax.ShapeDtypeStruct((1, hidden, hidden), F32),
        ],
        compiler_params=params(56),
        cost_estimate=cost(0, 6 * matrix_count * size * size),
        name="assemble",
    )(own, *blocks, strips)


def on_device(
    ids,
    table_rows,
    table_place,
    dense_in,
    labels,
    tables,
    cross_w,
    cross_b,
    tower1_w,
    tower1_b,
    tower2_w,
    tower2_b,
    out_w,
    out_b,
):
    tab_count = lax.axis_size("tab")
    rep_count = lax.axis_size("rep")
    slot_count, embed_dim, table_len = tables.shape
    row_count, dense_width = dense_in.shape
    field_count = ids.shape[1]
    layer_count, width = cross_w.shape[:2]
    hidden = tower1_w.shape[0]
    size = round_up(width, 128)
    all_slots = slot_count * tab_count
    tab_at = lax.axis_index("tab")
    rep_at = lax.axis_index("rep")

    matches = table_place[:, None] == jnp.arange(all_slots, dtype=I32)[None, :]
    effective = ids % table_rows[None, :]
    by_slot = jnp.sum(jnp.where(matches[:, :, None], effective.T[:, None, :], 0), axis=0)
    slot_rows = jnp.sum(jnp.where(matches, table_rows[:, None], 0), axis=0)
    own_rows = lax.dynamic_slice_in_dim(slot_rows, tab_at * slot_count, slot_count)
    wanted = lax.all_to_all(
        by_slot.reshape(tab_count, slot_count, row_count), "tab", split_axis=0, concat_axis=0, tiled=True
    )
    listed = jnp.transpose(wanted, (1, 0, 2)).reshape(-1)

    starts = list(range(0, slot_count, LOOK_SLOTS))
    arrived = []
    for begin in starts:
        looked = lookup(
            tables, listed, own_rows, tab_count, begin, min(LOOK_SLOTS, slot_count - begin)
        )
        arrived.append(lax.all_to_all(looked, "tab", split_axis=0, concat_axis=0, tiled=True))

    ready = 1.0 + arrived[0][0, 0, embed_dim, 0]

    def padded(weight):
        return jnp.pad(weight * ready, ((0, size - weight.shape[0]), (0, size - weight.shape[1])))

    weights = jnp.stack(
        [padded(cross_w[at]) for at in range(layer_count)] + [padded(tower1_w.T), padded(tower2_w)]
    )
    vectors = [cross_b[at] for at in range(layer_count)]
    vectors += [tower1_b, tower2_b, out_w[:width], out_w[width:], out_w[:0]]
    cols = jnp.stack(
        [jnp.pad((v * ready).astype(F32), (0, size - v.shape[0])) for v in vectors], axis=1
    )


    def near_parts(own):
        return [own, swap(own, "rep", 1)]

    def far_bases(own):
        bases = [own]
        for mask in masks_of("rep")[1:]:
            bases = bases + [swap(part, "rep", mask) for part in bases]
        return bases[1:]

    def far_parts(bases):
        return [part for far in bases for part in near_parts(far)]

    wanted = wanted + (ready - 1.0).astype(I32)
    near_ids = [part[:, :, None, :] for part in near_parts(wanted)]
    far_ids = [part[:, :, None, :] for part in far_parts(far_bases(wanted))]
    logits, dense_grad, slots, left, right, sums = dense_step(
        arrived, starts, table_place, dense_in, labels, weights, cols, out_b, layer_count, width,
        near_ids + far_ids,
    )
    returned = lax.all_to_all(
        slots.reshape(tab_count, slot_count, slots.shape[1], row_count),
        "tab",
        split_axis=0,
        concat_axis=0,
        tiled=True,
    )

    share = table_len // rep_count
    base = (rep_at * share).astype(I32).reshape(1)

    def gate(value, result):
        return value * (1.0 + 0.0 * result.astype(F32)).astype(value.dtype)

    bits = [rep_at & 1, (rep_at >> 1) & 1, tab_at & 1, (tab_at >> 2) & 1, (tab_at >> 1) & 1]
    own = sum(bit << (4 - at) for at, bit in enumerate(bits)).astype(I32).reshape(1)
    (send,) = weight_parts(left, right, own, 1)
    keep, strips = weight_parts(left, right, own, 0)
    matrix_count = layer_count + 2
    far_grads = None
    table_grad = None
    token = jnp.zeros((), F32)
    near_jobs = list(range(slot_count))[::-1]
    far_jobs = list(range(slot_count))[::-1]

    def add_next(near, times, after):
        nonlocal table_grad, token
        jobs = near_jobs if near else far_jobs
        for _ in range(min(times, len(jobs))):
            table_grad, token = add_rows(
                near_grads if near else far_grads,
                near_ids if near else far_ids,
                base,
                share,
                embed_dim,
                jobs.pop(),
                table_grad,
                not near,
                after,
            )

    def zero_of(value):
        return 0.0 * value.astype(F32)

    small = jnp.concatenate([strips.reshape(matrix_count * 8, size), sums], axis=0)
    total_rows = sums.shape[0]

    def small_step(value, masks):
        return small_sum(
            value, total_rows, [functools.partial(swap_both, rep_mask=r, tab_mask=t) for r, t in masks]
        )

    got = swap(send, "rep", 1)
    ahead = [added((keep[at, 1, 1], got[at, 1, 1])).astype(BF) for at in range(2)]
    first = [swap(ahead[at], *HALVES[at][0]) for at in range(2)]
    small = small_step(small + zero_of(ahead[0][0, 0, 0, 0, 0]) + zero_of(ahead[1][0, 0, 0, 0, 0]), [(1, 0)])
    small = small_step(small, [(2, 0), (0, 1), (2, 1)])
    keep, got, _ = lax.optimization_barrier((keep, got, ahead))
    behind = [added((keep[at, 1, 0], got[at, 1, 0])).astype(BF) for at in range(2)]
    later = [swap(behind[at], *HALVES[at][0]) for at in range(2)]
    keep, got, _ = lax.optimization_barrier((keep, got, behind))
    kept = [added((keep[at, 0], got[at, 0])) for at in range(2)]
    ready = zero_of(small[0, 0])
    sends = [added((kept[at][1], first[at]), ready).astype(BF) for at in range(2)]
    sent = [swap(sends[at], *HALVES[at][1]) for at in range(2)]
    returned = gate(returned, sends[0][0, 0, 0, 0, 0] + sends[1][0, 0, 0, 0, 0])
    near_grads = near_parts(returned)
    add_next(True, 1, behind + sends)
    bases = far_bases(gate(returned, token))
    add_next(True, NEAR_FIRST - 1, sends)
    sources = [[kept[at][0], later[at], sent[at]] for at in range(2)]

    def take_far(high, low):
        both = [added([part[high, low] for part in sources[at]], token) for at in range(2)]
        return jnp.stack(both)

    kept = take_far(0, 0)
    sends = [take_far(high, low).astype(BF) for high, low in FAR]
    far = [swap(value, "tab", 4 * high + 2 * low) for value, (high, low) in zip(sends, FAR)]
    add_next(True, slot_count, [kept] + sends)
    piece = added([kept, *far], token).astype(BF)
    for axis, known in (("rep", 2), ("tab", 3)):
        for mask in masks_of(axis)[known:]:
            piece = (piece.astype(F32) + swap(piece, axis, mask).astype(F32)).astype(BF)
    parts = [piece, swap(piece, "tab", 2), swap(piece, "tab", 4), swap(piece, "tab", 6)]
    far_grads = far_parts([gate(part, piece[0, 0, 0, 0]) for part in bases])
    add_next(False, FAR_FIRST, [piece])
    values = joined(parts, token)
    from_y = swap(values, "tab", 1)
    from_x = swap(values, "rep", 2)
    small = small + zero_of(values[0, 0, 0, 0, 0])
    small = small_step(small, [(0, 2), (0, 4), (0, 6)])
    for rep_mask in masks_of("rep")[2:]:
        small = small_step(small, [(rep_mask, 0)])
    for tab_mask in masks_of("tab")[3:]:
        small = small_step(small, [(0, tab_mask)])
    add_next(False, 1, [values])
    other = [swap(values, "rep", 1)]
    add_next(False, 1, other)
    token = token + zero_of(small[0, 0])
    last = [swap(gate(from_y[0], token), "rep", 2), swap(gate(from_x[1], token), "tab", 1)]
    other += [swap(from_y, "rep", 1), swap(from_x, "rep", 1)]
    add_next(False, slot_count, other)
    last = [gate(part, token) for part in last]
    blocks = [values, from_y, from_x] + last + other + [swap(part, "rep", 1) for part in last]

    strips = small[:-8].reshape(matrix_count, 8, size)
    sums = small[-8:]
    cross_w_grad, tower1_w_grad, tower2_w_grad = assemble(
        blocks, strips, own, layer_count, width, hidden
    )
    scalars = sums[layer_count + 4]
    return (
        scalars[0] / (row_count * tab_count * rep_count),
        logits.reshape(row_count),
        dense_grad[:dense_width].T,
        cross_w_grad,
        sums[:layer_count, :width],
        tower1_w_grad[0].T,
        sums[layer_count, :hidden],
        tower2_w_grad[0],
        sums[layer_count + 1, :hidden],
        jnp.concatenate([sums[layer_count + 2, :width], sums[layer_count + 3, :hidden]]),
        scalars[128],
        table_grad,
    )


def solution(mesh):
    placed = (
        P(("tab", "rep"), None),
        P(),
        P(),
        P(("tab", "rep"), None),
        P(("tab", "rep")),
        P("tab", None, None),
        P(),
        P(),
        P(),
        P(),
        P(),
        P(),
        P(),
        P(),
    )
    return jax.shard_map(
        on_device,
        mesh=mesh,
        in_specs=placed,
        out_specs=(
            P(),
            P(("tab", "rep")),
            P(("tab", "rep"), None),
            P(),
            P(),
            P(),
            P(),
            P(),
            P(),
            P(),
            P(),
            P("tab", None, "rep"),
        ),
        check_vma=False,
    )
```
